256 devices in a mesh: strip: 16 (over z, x_lo), period: 16 (over y, x_hi, core).
Axes of the slice: x: 4 (x_hi: 2, x_lo: 2; x = x_hi * 2 + x_lo), y: 4, z: 8, core: 2. Of those that a mesh axis runs over, the one named last changes fastest.
Arguments:
- u_start: float32 [16, 64, 64, 128], P('strip', 'period'), may hold values from 0 to 0.02
- dual_prec: float32 [5, 16, 64, 64, 128], P(None, 'strip', 'period'), may hold values from 0 to 0.5
- dual_bound: float32 [16, 64, 64, 128], P('strip', 'period'), may hold values from 0 to 0.5
- dual_cap: float32 [64], P('period'), may hold values from 0 to 2
- capacity: float32 [64], P('period'), may hold values from 0.005 to 0.03
- block_value: float32 [16, 64, 128], P('strip'), may hold values from -6 to 6
- ton_class: int32 [16, 64, 128], P('strip'), may hold values from 0 to 7
- density: float32 [8], replicated, may hold values from 1 to 3
- slope_code: int32 [16, 128], P('strip'), may hold values from 0 to 15
- omega_start: float32 [1], replicated, may hold values from 0.5 to 2
Outputs:
- mined_share: float32 [16, 64, 64, 128], P('strip', 'period')
- arc_prices: float32 [5, 16, 64, 64, 128], P(None, 'strip', 'period')
- bound_prices: float32 [16, 64, 64, 128], P('strip', 'period')
- capacity_prices: float32 [64], P('period')
- primal_weight: float32 [1], replicated
The draws below stay inside these ranges and needn't reach their ends.
All inputs are finite; a program needn't handle non-finite values.
Results may differ from the reference program's by a relative error of at most 0.0001.
Values sent between devices are 32-bit elements; how exact they have to be, the bound alone decides.
No kernel may reach another device: no remote copies, remote signals or barrier semaphores. Data moves between devices by JAX's collectives and lax.ppermute only.
A program may use at most 64 MiB of HBM per device.

```python
import math
import jax
import jax.numpy as jnp
from jax import lax

NY = 128
NZ = 64
NARCS = 5
NCLASS = 8
OUTER = 2
INNER = 3
NX = 16
NP = 64


def draw_ton_class(key, part):
    base_class = jax.random.randint(key, (NX, NZ, NY), 0, NCLASS // 2)
    rising = jnp.arange(NX) * (NCLASS // 2 + 1) // NX
    return (base_class + rising[:, None, None]).astype(jnp.int32)


def touch_ends(array, key, smallest, top_value):
    shape = array.shape
    spot = [jax.random.randint(jax.random.fold_in(key, axis), (), 0, shape[axis]) for axis in range(len(shape))]
    array = array.at[tuple(spot)].set(smallest)
    longest = shape.index(max(shape))
    spot[longest] = (spot[longest] + 1) % shape[longest]
    return array.at[tuple(spot)].set(top_value)


def block_scale(key, extent, shards, least, high):
    level = 1.0
    for dim, parts in shards:
        draws = jax.random.uniform(jax.random.fold_in(jax.random.fold_in(key, 6), dim), (parts,), jnp.float32, least / len(shards), high / len(shards))
        level = level * jnp.repeat(jnp.exp(draws), extent[dim] // parts).reshape((-1,) + (1,) * (len(extent) - 1 - dim))
    return level


def bell_draw(key, extent, scale, most, split=(), held_as=jnp.bfloat16):
    values = jax.random.normal(key, extent, jnp.float32) * scale
    if len(split) > 0:
        values = block_scale(key, extent, split, -0.22, 0.18) * values
    return jnp.clip(values, min=-most, max=most).astype(held_as)


def setup_inputs(seed: int = 0) -> dict:
    splits = jax.random.split(jax.random.key(seed), 11)
    return {
        "u_start": jnp.clip(0.02 * jax.random.uniform(splits[0], (NX, NP, NZ, NY), jnp.float32) ** block_scale(splits[0], (NX, NP, NZ, NY), ((0, 16), (1, 16)), -0.2, 0.2), 0.0, 0.02),
        "dual_prec": jnp.clip(0.5 * jax.random.uniform(splits[1], (NARCS, NX, NP, NZ, NY), jnp.float32) ** block_scale(splits[1], (NARCS, NX, NP, NZ, NY), ((1, 16), (2, 16)), -0.2, 0.2), 0.0, 0.5),
        "dual_bound": jnp.clip(0.5 * jax.random.uniform(splits[2], (NX, NP, NZ, NY), jnp.float32) ** block_scale(splits[2], (NX, NP, NZ, NY), ((0, 16), (1, 16)), -0.2, 0.2), 0.0, 0.5),
        "dual_cap": jnp.clip(2.0 * jax.random.uniform(splits[3], (NP,), jnp.float32) ** block_scale(splits[3], (NP,), ((0, 16),), -0.2, 0.2), 0.0, 2.0),
        "capacity": jnp.clip(0.005 + 0.024999999 * jax.random.uniform(splits[4], (NP,), jnp.float32) ** block_scale(splits[4], (NP,), ((0, 16),), -0.2, 0.2), 0.005, 0.03),
        "block_value": bell_draw(splits[5], (NX, NZ, NY), 1.0, 6.0, ((0, 16),), jnp.float32),
        "ton_class": draw_ton_class(jax.random.fold_in(splits[10], 71), 0),
        "density": jnp.clip(jnp.exp(jax.random.uniform(splits[7], (NCLASS,), jnp.float32, math.log(1.0), math.log(3.0))), 1.0, 3.0),
        "slope_code": touch_ends(jax.random.randint(splits[8], (NX, NY), 0, 16), jax.random.fold_in(splits[8], 1), 0, 15).astype(jnp.int32),
        "omega_start": jnp.clip(jnp.exp(jax.random.uniform(splits[9], (1,), jnp.float32, math.log(0.5), math.log(2.0))), 0.5, 2.0),
    }


ARC_OFFSETS = ((0, 0), (1, 0), (-1, 0), (0, 1), (0, -1))
RATE = math.log(1.1) / 12.0
EPS = 1e-06
SLOPE = 11.0

def arc_masks(code_rows, first_row, total_rows, depth_cells, across):
    row_ids = (first_row + jnp.arange(code_rows.shape[0]))[:, None, None]
    depth_ids = jnp.arange(depth_cells)[None, :, None]
    col_ids = jnp.arange(across)[None, None, :]
    pattern = code_rows[:, None, :]
    mask_list = []
    for arc_index, (step_x, step_y) in enumerate(ARC_OFFSETS):
        inside = (row_ids >= 0) & (row_ids < total_rows) & (row_ids + step_x >= 0) & (row_ids + step_x < total_rows)
        inside = inside & (col_ids + step_y >= 0) & (col_ids + step_y < across) & (depth_ids >= 1)
        if arc_index > 0:
            inside = inside & (pattern // 2 ** (arc_index - 1) % 2 == 1)
        mask_list.append(inside.astype(jnp.float32))
    return jnp.stack(mask_list)

def tonnage(ton_class, density):
    class_ids = jnp.arange(density.shape[0])
    class_table = (1.0 + class_ids.astype(jnp.float32)) * density
    onehot = (class_ids[:, None, None, None] == ton_class[None]).astype(jnp.float32)
    return jnp.einsum('k,kxzy->xzy', class_table, onehot, precision=lax.Precision.HIGHEST)

def upper_cell(values_in, step_y):
    depth_cells = values_in.shape[2]
    across = values_in.shape[3]
    padded = jnp.pad(values_in, ((0, 0), (0, 0), (1, 0), (1, 1)))
    return padded[:, :, 0:depth_cells, 1 + step_y:1 + step_y + across]

def lower_cell(values_in, step_y):
    depth_cells = values_in.shape[2]
    across = values_in.shape[3]
    padded = jnp.pad(values_in, ((0, 0), (0, 0), (0, 1), (1, 1)))
    return padded[:, :, 1:depth_cells + 1, 1 - step_y:1 - step_y + across]

def adjoint(arc_duals, from_left, from_right, bound_duals):
    result = lax.optimization_barrier(jnp.sum(arc_duals, axis=0)) + bound_duals
    for arc_index, (step_x, step_y) in enumerate(ARC_OFFSETS):
        source = arc_duals[arc_index]
        if step_x == 1:
            source = jnp.concatenate([from_left, source[:-1]], axis=0)
        elif step_x == -1:
            source = jnp.concatenate([source[1:], from_right], axis=0)
        result = result - lower_cell(source, step_y)
    return result

def reference(u_start, dual_prec, dual_bound, dual_cap, capacity, block_value, ton_class, density, slope_code, omega_start):
    arc_active = arc_masks(slope_code, 0, NX, NZ, NY)[:, :, None]
    tonnage_grid = tonnage(ton_class, density)
    tons_col = tonnage_grid[:, None]
    tons_all = jnp.sum(tonnage_grid)
    blocks_all = float(NX * NY * NZ)
    root_blocks = math.sqrt(blocks_all)
    period_ids = jnp.arange(NP).astype(jnp.float32)[None, :, None, None]
    profit = block_value[:, None] * jnp.exp(-RATE * period_ids)
    zero_rim = jnp.zeros((1, NP, NZ, NY), jnp.float32)
    primal = u_start
    arc_duals = dual_prec * arc_active
    bound_duals = dual_bound
    cap_duals = dual_cap
    weight = omega_start[0]
    for restart in range(OUTER):
        primal_first, duals_first, bound_first, cap_first = (primal, arc_duals, bound_duals, cap_duals)
        primal_sum = jnp.zeros_like(primal)
        duals_sum = jnp.zeros_like(arc_duals)
        bound_sum = jnp.zeros_like(bound_duals)
        cap_sum = jnp.zeros_like(cap_duals)
        for sweep_index in range(INNER):
            gradient_x = adjoint(arc_duals, zero_rim, zero_rim, bound_duals)
            gradient_u = jnp.flip(jnp.cumsum(jnp.flip(gradient_x, 1), axis=1), 1) + tons_col * cap_duals[None, :, None, None] / root_blocks
            step_primal = 1.0 / (weight * (SLOPE * (NP - period_ids) + tons_col / root_blocks))
            primal_new = jnp.maximum(primal - step_primal * (gradient_u - profit), 0.0)
            extrapolated = 2.0 * primal_new - primal
            cumulative = jnp.cumsum(extrapolated, axis=1)
            padded = jnp.pad(cumulative, ((1, 1), (0, 0), (0, 0), (0, 0)))
            step_prec = weight / (2.0 * (period_ids + 1.0))
            step_bound = weight / (period_ids + 1.0)
            new_list = []
            for arc_index, (step_x, step_y) in enumerate(ARC_OFFSETS):
                ahead_cells = upper_cell(padded[1 + step_x:1 + step_x + NX], step_y)
                new_list.append(jnp.maximum(arc_duals[arc_index] + step_prec * (cumulative - ahead_cells), 0.0) * arc_active[arc_index])
            duals_new = jnp.stack(new_list)
            bound_new = jnp.maximum(bound_duals + step_bound * (cumulative - 1.0), 0.0)
            row_total = jnp.einsum('xzy,xtzy->t', tonnage_grid, extrapolated, precision=lax.Precision.HIGHEST)
            cap_new = jnp.maximum(cap_duals + weight * (row_total - blocks_all * capacity) / tons_all, 0.0)
            primal_sum = primal_sum + primal_new
            duals_sum = duals_sum + duals_new
            bound_sum = bound_sum + bound_new
            cap_sum = cap_sum + cap_new
            primal, arc_duals, bound_duals, cap_duals = (primal_new, duals_new, bound_new, cap_new)
        primal = primal_sum / INNER
        arc_duals = duals_sum / INNER
        bound_duals = bound_sum / INNER
        cap_duals = cap_sum / INNER
        primal_move = jnp.sum((primal - primal_first) ** 2)
        dual_move = jnp.sum((arc_duals - duals_first) ** 2) + jnp.sum((bound_duals - bound_first) ** 2) + jnp.sum((cap_duals - cap_first) ** 2)
        weight = jnp.sqrt(weight * jnp.sqrt((dual_move + EPS) / (primal_move + EPS)))
    return (primal, arc_duals, bound_duals, cap_duals, jnp.reshape(weight, (1,)))
```

```python
import math

import jax
import jax.numpy as jnp
from jax import lax
from jax.experimental import pallas as pl
from jax.experimental.pallas import tpu as pltpu
from jax.sharding import PartitionSpec as P

OUTER = 2
INNER = 3
NX = 16
NY = 128
NZ = 64
NP = 64
RATE = math.log(1.1) / 12.0
EPS = 1e-06
SLOPE = 11.0
BLOCKS = float(NX * NY * NZ)
ROOT = math.sqrt(BLOCKS)
F32 = jnp.float32

TILES = 16
ROWS = NP // 2
DEVICES = 256
ARCS = 5
BOUND, SHARE, LEFT, RIGHT, EXTRA = 5, 6, 7, 8, 18
SLOTS = 19
LANE_PRIMAL, LANE_DUAL, LANE_TONS = 40, 41, 42
HALO1, HALO2, HALO3, HALO4, TONS, VALUE = 5, 6, 7, 8, 9, 10
PLANES = 11


def lanes(shape):
    return lax.broadcasted_iota(jnp.int32, shape, len(shape) - 1)


def subs(shape):
    return lax.broadcasted_iota(jnp.int32, shape, len(shape) - 2)


def later_half(shape):
    return lanes(shape) >= 64


def half_matrix():
    a = subs((128, 128)) >= 64
    b = lanes((128, 128)) >= 64
    return (a == b).astype(F32)


def half_sums(rows):
    return jnp.dot(
        rows, half_matrix(), precision=lax.Precision.HIGHEST, preferred_element_type=F32
    )


def period_table():
    shape = (ROWS, 128)
    return (2 * subs(shape) + later_half(shape).astype(jnp.int32)).astype(F32)


def down(v):
    return pltpu.roll(v, 1, v.ndim - 1)


def up(v):
    return pltpu.roll(v, 127, v.ndim - 1)


def swap(v):
    return pltpu.roll(v, 64, v.ndim - 1)


def pack_kernel(caps, limits, share, prec, bound, left, right, out):
    def put(field, source):
        for a in range(2):
            both = jnp.concatenate([source(2 * a), source(2 * a + 1)], axis=0)
            turned = both.T
            out[:, 2 * field + a] = turned.reshape(TILES, 8, 128)

    for k in range(ARCS):
        put(k, lambda t, k=k: prec[k, t])
    put(BOUND, lambda t: bound[t])
    put(SHARE, lambda t: share[t])
    put(LEFT, lambda t: left[t])
    put(RIGHT, lambda t: right[t])
    half = later_half((1, 128))
    for a in range(2):
        cap_row = jnp.where(half, caps[2 * a + 1], caps[2 * a])
        limit_row = jnp.where(half, limits[2 * a + 1], limits[2 * a])
        for j in range(TILES):
            if j > 0:
                out[j, EXTRA, a : a + 1] = out[j - 1, 2 * 3 + a, 7:8]
            else:
                out[j, EXTRA, a : a + 1] = jnp.zeros((1, 128), F32)
            if j < TILES - 1:
                out[j, EXTRA, 2 + a : 3 + a] = out[j + 1, 2 * 4 + a, 0:1]
            else:
                out[j, EXTRA, 2 + a : 3 + a] = jnp.zeros((1, 128), F32)
            out[j, EXTRA, 4 + a : 5 + a] = cap_row
            out[j, EXTRA, 6 + a : 7 + a] = limit_row


def planes_kernel(place, density, slope, ton_class, value, out, turned):
    x, tile = place[0], place[1]
    classes = ton_class[...]
    tons = jnp.zeros(classes.shape, F32)
    for c in range(8):
        tons = jnp.where(classes == c, (1.0 + c) * density[c], tons)
    turned[...] = jnp.concatenate([tons, value[...]], axis=0).T
    both = turned[pl.ds(pl.multiple_of(8 * tile, 8), 8), :]
    other = swap(both)
    shape = (8, 128)
    half = later_half(shape)
    out[TONS] = jnp.where(half, other, both)
    out[VALUE] = jnp.where(half, both, other)
    codes = jnp.broadcast_to(slope[...].astype(F32), shape)
    column = 8 * tile + subs(shape)

    def code_at(column):
        picked = jnp.sum(jnp.where(lanes(shape) == column, codes, 0.0), axis=1, keepdims=True)
        return jnp.broadcast_to(picked, shape).astype(jnp.int32)

    deep = (lanes(shape) & 63) >= 1
    code = code_at(column)

    def mask(code, bit, inside):
        return (deep & (((code >> bit) & 1) == 1) & inside).astype(F32)

    out[0] = deep.astype(F32)
    out[1] = mask(code, 0, jnp.full(shape, x) + 1 < NX)
    out[2] = mask(code, 1, jnp.full(shape, x) >= 1)
    out[3] = mask(code, 2, column + 1 < NY)
    out[4] = mask(code, 3, column >= 1)
    zero = jnp.zeros(shape, jnp.int32)
    out[HALO1] = jnp.zeros(shape, F32)
    out[HALO2] = jnp.zeros(shape, F32)
    out[HALO3] = mask(code_at(zero + 8 * tile - 1), 2, zero == 0)
    out[HALO4] = mask(code_at(zero + 8 * tile + 8), 3, zero == 0)


def adjoint_row(prices, bound, halo1, halo2, halo3, halo4, carry):
    shape = (8, 128)
    total = prices[0] + prices[1] + prices[2] + prices[3] + prices[4] + bound
    from_front = jnp.where(subs(shape) == 0, halo3, pltpu.roll(prices[3], 1, 0))
    from_back = jnp.where(subs(shape) == 7, halo4, pltpu.roll(prices[4], 7, 0))
    lower = prices[0] + halo1 + halo2 + from_front + from_back
    g = total - up(lower)
    pair = g + swap(g)
    return carry + jnp.where(later_half(shape), g, pair), carry + pair


def unpack_kernel(got, planes, prices, halos, edges, bound, share, caps, limits, tail, masks):
    masks[...] = planes[...]
    deep = planes[0]
    for n, field in ((HALO1, LEFT), (HALO2, RIGHT)):
        tile = got[0, 2 * field]
        masks[n] = jnp.broadcast_to(tile[:, 0:1], (8, 128)) * deep
    for s in range(TILES):
        edges[0, 2 * s : 2 * s + 2] = got[s, EXTRA, 0:2] * masks[HALO3][0:2]
        edges[1, 2 * s : 2 * s + 2] = got[s, EXTRA, 2:4] * masks[HALO4][0:2]
        caps[2 * s : 2 * s + 2] = got[s, EXTRA, 4:6]
        limits[2 * s : 2 * s + 2] = got[s, EXTRA, 6:8]
    carry = jnp.zeros((8, 128), F32)
    for r in reversed(range(ROWS)):
        s, a = divmod(r, 2)
        p = [got[s, 2 * k + a] * masks[k] for k in range(ARCS)]
        for k in range(ARCS):
            prices[k, r] = p[k]
        b = got[s, 2 * BOUND + a]
        bound[r] = b
        share[r] = got[s, 2 * SHARE + a]
        h1 = got[s, 2 * LEFT + a] * masks[HALO1]
        h2 = got[s, 2 * RIGHT + a] * masks[HALO2]
        halos[0, r] = h1
        halos[1, r] = h2
        tail[r], carry = adjoint_row(
            p, b, h1, h2, edges[0, r : r + 1], edges[1, r : r + 1], carry
        )


def summed_row(got):
    total = got[0:8]
    for n in range(1, DEVICES // 8):
        total = total + got[8 * n : 8 * n + 8]
    return jnp.sum(total, axis=0, keepdims=True)


def lane_value(row, lane):
    return jnp.sum(jnp.where(lanes((1, 128)) == lane, row, 0.0), axis=1, keepdims=True)


def caps_after(row, caps, limits, weight):
    shape = (ROWS, 128)
    spread = jnp.where((lanes(shape) & 63) == subs(shape), jnp.broadcast_to(row, shape), 0.0)
    totals = half_sums(spread)
    tons_all = lane_value(row, LANE_TONS)
    return jnp.maximum(caps + weight * (totals - BLOCKS * limits) / tons_all, 0.0)


def weight_after(row, weight, mean, first):
    move_cap = jnp.sum(
        jnp.sum((mean - first) ** 2, axis=0, keepdims=True), axis=1, keepdims=True
    ) * (1.0 / 64.0)
    primal_move = lane_value(row, LANE_PRIMAL)
    dual_move = lane_value(row, LANE_DUAL) + move_cap
    return jnp.sqrt(weight * jnp.sqrt((dual_move + EPS) / (primal_move + EPS)))


def primal_step(caps, tail, share, planes, weight, new, head, first, last, row, cap_rows, rate_rows):
    shape = (8, 128)
    tons = planes[TONS]
    value = planes[VALUE]
    lean = tons / ROOT
    cap_rows[...] = caps
    periods = period_table()
    rate_rows[0] = jnp.exp(-RATE * periods)
    rate_rows[1] = SLOPE * (NP - periods)
    half = later_half(shape)
    carry = jnp.zeros(shape, F32)
    mined = []
    for r in range(ROWS):
        one = slice(r, r + 1)
        gradient = tail[r] + tons * cap_rows[one] / ROOT
        tau = 1.0 / (weight * (rate_rows[1, one] + lean))
        old = share[r]
        now = jnp.maximum(old - tau * (gradient - value * rate_rows[0, one]), 0.0)
        new[r] = now
        ahead = 2.0 * now - old
        pair = ahead + swap(ahead)
        cumulative = carry + jnp.where(half, pair, ahead)
        carry = carry + pair
        head[r] = cumulative
        first[one] = cumulative[0:1]
        last[one] = cumulative[7:8]
        mined.append(tons * ahead)
    mined.append(tons)
    sums = half_sums(jnp.concatenate(mined, axis=0))
    lane = lanes(shape)
    total = jnp.where(lane == LANE_TONS, sums[8 * ROWS :], 0.0)
    for r in range(ROWS):
        total = total + jnp.where((lane & 63) == r, sums[8 * r : 8 * r + 8], 0.0)
    row[...] = jnp.broadcast_to(jnp.sum(total, axis=0, keepdims=True), row.shape)


def primal_first_kernel(caps, tail, share, planes, weight, *rest):
    primal_step(caps[...], tail, share, planes, weight[...], *rest)


def primal_kernel(got, caps, limits, tail, share, planes, weight, caps_new, *rest):
    row = summed_row(got)
    caps_now = caps_after(row, caps[...], limits[...], weight[...])
    caps_new[...] = caps_now
    primal_step(caps_now, tail, share, planes, weight[...], *rest)


def restart(got, caps0, caps1, caps2, limits, weight):
    row = summed_row(got)
    caps3 = caps_after(row, caps2[...], limits[...], weight[...])
    mean = (caps1[...] + caps2[...] + caps3) / INNER
    return mean, weight_after(row, weight[...], mean, caps0[...])


def primal_restart_kernel(
    got, caps0, caps1, caps2, limits, tail, share, planes, weight, caps_new, weight_new, *rest
):
    mean, new = restart(got, caps0, caps1, caps2, limits, weight)
    caps_new[...] = mean
    weight_new[...] = new
    primal_step(mean, tail, share, planes, new, *rest)


def finish_kernel(got, caps0, caps1, caps2, limits, weight, caps_new, weight_new):
    mean, new = restart(got, caps0, caps1, caps2, limits, weight)
    caps_new[...] = mean
    weight_new[...] = new


def dual_rows(
    weight, planes, head, right, left, front, back, first, last, prices, halos, edges, bound, steps
):
    periods = period_table()
    steps[0] = weight[...] / (2.0 * (periods + 1.0))
    steps[1] = weight[...] / (periods + 1.0)
    fronts, backs = front[...], back[...]
    steps[2] = down(fronts)
    steps[3] = down(backs)
    wide = (ROWS, 128)
    edge0 = jnp.broadcast_to(planes[HALO3][0:1], wide) * jnp.maximum(
        edges[0] + steps[0] * (fronts - down(first[...])), 0.0
    )
    edge1 = jnp.broadcast_to(planes[HALO4][0:1], wide) * jnp.maximum(
        edges[1] + steps[0] * (backs - down(last[...])), 0.0
    )
    return edge0, edge1


def dual_row(r, planes, head, right, left, prices, halos, bound, steps):
    shape = (8, 128)
    one = slice(r, r + 1)
    step = steps[0, one]
    here = head[r]
    under = down(here)
    sub = subs(shape)
    ahead = [
        under,
        down(right[r]),
        down(left[r]),
        jnp.where(sub == 7, steps[3, one], pltpu.roll(under, 7, 0)),
        jnp.where(sub == 0, steps[2, one], pltpu.roll(under, 1, 0)),
    ]
    p = [
        jnp.maximum(prices[k, r] + step * (here - ahead[k]), 0.0) * planes[k] for k in range(ARCS)
    ]
    b = jnp.maximum(bound[r] + steps[1, one] * (here - 1.0), 0.0)
    h1 = jnp.maximum(halos[0, r] + step * (left[r] - under), 0.0) * planes[HALO1]
    h2 = jnp.maximum(halos[1, r] + step * (right[r] - under), 0.0) * planes[HALO2]
    return p, b, h1, h2


def dual_kernel(
    weight, planes, head, right, left, front, back, first, last, prices, halos, edges, bound,
    prices_new, halos_new, edges_new, bound_new, tail, steps,
):
    edge0, edge1 = dual_rows(
        weight, planes, head, right, left, front, back, first, last, prices, halos, edges, bound, steps
    )
    edges_new[0] = edge0
    edges_new[1] = edge1
    carry = jnp.zeros((8, 128), F32)
    for r in reversed(range(ROWS)):
        p, b, h1, h2 = dual_row(r, planes, head, right, left, prices, halos, bound, steps)
        for k in range(ARCS):
            prices_new[k, r] = p[k]
        bound_new[r] = b
        halos_new[0, r] = h1
        halos_new[1, r] = h2
        tail[r], carry = adjoint_row(
            p, b, h1, h2, edges_new[0, r : r + 1], edges_new[1, r : r + 1], carry
        )


def mean_of(one, two, three):
    return (one + two + three) / INNER


def put_moves(row, primal_move, dual_move, row_new):
    lane = lanes((1, 128))

    def whole(v):
        return jnp.sum(jnp.sum(v, axis=0, keepdims=True), axis=1, keepdims=True)

    old = row[0:1]
    new = old + jnp.where(lane == LANE_PRIMAL, whole(primal_move), 0.0)
    new = new + jnp.where(lane == LANE_DUAL, whole(dual_move), 0.0)
    row_new[...] = jnp.broadcast_to(new, row_new.shape)


def dual_restart_kernel(
    weight, planes, head, right, left, front, back, first, last, prices, halos, edges, bound,
    prices0, prices1, halos1, edges1, bound0, bound1, share0, share1, share2, share3, row,
    prices_new, halos_new, edges_new, bound_new, tail, share_new, row_new, steps,
):
    edge0, edge1 = dual_rows(
        weight, planes, head, right, left, front, back, first, last, prices, halos, edges, bound, steps
    )
    edges_new[0] = mean_of(edges1[0], edges[0], edge0)
    edges_new[1] = mean_of(edges1[1], edges[1], edge1)
    shape = (8, 128)
    carry = jnp.zeros(shape, F32)
    primal_move = jnp.zeros(shape, F32)
    dual_move = jnp.zeros(shape, F32)
    for r in reversed(range(ROWS)):
        p, b, h1, h2 = dual_row(r, planes, head, right, left, prices, halos, bound, steps)
        p = [mean_of(prices1[k, r], prices[k, r], p[k]) for k in range(ARCS)]
        b = mean_of(bound1[r], bound[r], b)
        h1 = mean_of(halos1[0, r], halos[0, r], h1)
        h2 = mean_of(halos1[1, r], halos[1, r], h2)
        u = mean_of(share1[r], share2[r], share3[r])
        primal_move = primal_move + (u - share0[r]) ** 2
        dual_move = dual_move + (b - bound0[r]) ** 2
        for k in range(ARCS):
            dual_move = dual_move + (p[k] - prices0[k, r]) ** 2
            prices_new[k, r] = p[k]
        bound_new[r] = b
        halos_new[0, r] = h1
        halos_new[1, r] = h2
        share_new[r] = u
        tail[r], carry = adjoint_row(
            p, b, h1, h2, edges_new[0, r : r + 1], edges_new[1, r : r + 1], carry
        )
    put_moves(row, primal_move, dual_move, row_new)


def dual_final_kernel(
    weight, planes, head, right, left, front, back, first, last, prices, halos, edges, bound,
    prices0, prices1, bound0, bound1, share0, share1, share2, share3, row,
    send, row_new, steps,
):
    dual_rows(
        weight, planes, head, right, left, front, back, first, last, prices, halos, edges, bound, steps
    )
    shape = (8, 128)
    primal_move = jnp.zeros(shape, F32)
    dual_move = jnp.zeros(shape, F32)
    for r in reversed(range(ROWS)):
        s, a = divmod(r, 2)
        p, b, _, _ = dual_row(r, planes, head, right, left, prices, halos, bound, steps)
        p = [mean_of(prices1[k, r], prices[k, r], p[k]) for k in range(ARCS)]
        b = mean_of(bound1[r], bound[r], b)
        u = mean_of(share1[r], share2[r], share3[r])
        primal_move = primal_move + (u - share0[r]) ** 2
        dual_move = dual_move + (b - bound0[r]) ** 2
        for k in range(ARCS):
            dual_move = dual_move + (p[k] - prices0[k, r]) ** 2
            send[s, 2 * k + a] = p[k]
        send[s, 2 * BOUND + a] = b
        send[s, 2 * SHARE + a] = u
    put_moves(row, primal_move, dual_move, row_new)


def turn_back_kernel(got, share, prec, bound):
    def take(field, target):
        for a in range(2):
            turned = got[:, 2 * field + a].reshape(128, 128).T
            target(2 * a, turned[0:64])
            target(2 * a + 1, turned[64:128])

    for k in range(ARCS):

        def store(t, v, k=k):
            prec[k, t] = v

        take(k, store)

    def store_bound(t, v):
        bound[t] = v

    def store_share(t, v):
        share[t] = v

    take(BOUND, store_bound)
    take(SHARE, store_share)


def f32(*shape):
    return jax.ShapeDtypeStruct(shape, F32)


VMEM = pl.BlockSpec(memory_space=pltpu.VMEM)
SMEM = pl.BlockSpec(memory_space=pltpu.SMEM)
FIELD = (ROWS, 8, 128)


def call(kernel, outs, scratch=(), scalars=0):
    def run(*args):
        specs = [SMEM] * scalars + [VMEM] * (len(args) - scalars)
        return pl.pallas_call(
            kernel,
            out_shape=[f32(*shape) for shape in outs],
            in_specs=specs,
            out_specs=[VMEM] * len(outs),
            scratch_shapes=[pltpu.VMEM(shape, F32) for shape in scratch],
            compiler_params=pltpu.CompilerParams(vmem_limit_bytes=32 * 1024 * 1024),
        )(*args)

    return run


STEP_OUTS = [FIELD, FIELD, (ROWS, 128), (ROWS, 128), (DEVICES, 128)]
STEP_SCRATCH = [(ROWS, 128), (2, ROWS, 128)]
DUAL_OUTS = [(ARCS,) + FIELD, (2,) + FIELD, (2, ROWS, 128), FIELD, FIELD]


def chain(by):
    return [(i, i + by) for i in range(16) if 0 <= i + by < 16]


def share_row(row):
    return lax.all_to_all(row, ("strip", "period"), 0, 0, tiled=True)


def halo(head, first, last):
    right = lax.ppermute(head, "strip", chain(-1))
    left = lax.ppermute(head, "strip", chain(1))
    back = lax.ppermute(first, "period", chain(-1))
    front = lax.ppermute(last, "period", chain(1))
    return right, left, front, back


def per_device(
    u_start,
    dual_prec,
    dual_bound,
    dual_cap,
    capacity,
    block_value,
    ton_class,
    density,
    slope_code,
    omega_start,
):
    x, tile = lax.axis_index("strip"), lax.axis_index("period")
    prec = dual_prec[:, 0]
    top = (jnp.arange(NZ) == 0)[None, :, None]
    toward = ((slope_code & 1) * (x + 1 < NX)).astype(F32)[None]
    away = ((slope_code // 2 & 1) * (x >= 1)).astype(F32)[None]
    left0 = lax.ppermute(jnp.where(top, toward, prec[1]), "strip", chain(1))
    right0 = lax.ppermute(jnp.where(top, away, prec[2]), "strip", chain(-1))
    place = jnp.stack([x, tile]).astype(jnp.int32)
    (planes,) = call(planes_kernel, [(PLANES, 8, 128)], [(128, 128)], 2)(
        place, density, slope_code, ton_class[0], block_value[0]
    )
    (send,) = call(pack_kernel, [(TILES, SLOTS, 8, 128)], (), 2)(
        dual_cap, capacity, u_start[0], prec, dual_bound[0], left0, right0
    )
    got = lax.all_to_all(send, "period", 0, 0)
    prices, halos, edges, bound, share, caps, limits, tail, planes = call(
        unpack_kernel,
        [
            (ARCS,) + FIELD,
            (2,) + FIELD,
            (2, ROWS, 128),
            FIELD,
            FIELD,
            (ROWS, 128),
            (ROWS, 128),
            FIELD,
            (PLANES, 8, 128),
        ],
    )(got, planes)
    weight = jnp.reshape(omega_start, (1, 1))
    row_sums = None
    old_caps = None
    for outer in range(OUTER):
        shares, caps_list = [share], []
        price_list, halo_list, edge_list, bound_list = [prices], [halos], [edges], [bound]
        for inner in range(INNER):
            if inner == 0 and outer == 0:
                new, head, first, last, row = call(primal_first_kernel, STEP_OUTS, STEP_SCRATCH)(
                    caps, tail, share, planes, weight
                )
            elif inner == 0:
                caps, weight, new, head, first, last, row = call(
                    primal_restart_kernel, [(ROWS, 128), (1, 1)] + STEP_OUTS, STEP_SCRATCH
                )(row_sums, *old_caps, limits, tail, share, planes, weight)
            else:
                caps, new, head, first, last, row = call(
                    primal_kernel, [(ROWS, 128)] + STEP_OUTS, STEP_SCRATCH
                )(row_sums, caps, limits, tail, share, planes, weight)
            caps_list.append(caps)
            shares.append(new)
            share = new
            right, left, front, back = halo(head, first, last)
            common = (
                weight, planes, head, right, left, front, back, first, last,
                prices, halos, edges, bound,
            )
            steps = [(4, ROWS, 128)]
            if inner < INNER - 1:
                row_sums = share_row(row)
                prices, halos, edges, bound, tail = call(dual_kernel, DUAL_OUTS, steps)(*common)
                price_list.append(prices)
                halo_list.append(halos)
                edge_list.append(edges)
                bound_list.append(bound)
            elif outer < OUTER - 1:
                prices, halos, edges, bound, tail, share, row = call(
                    dual_restart_kernel, DUAL_OUTS + [FIELD, (DEVICES, 128)], steps
                )(
                    *common, price_list[0], price_list[1], halo_list[1], edge_list[1],
                    bound_list[0], bound_list[1], *shares, row,
                )
                row_sums = share_row(row)
                old_caps = caps_list
            else:
                send, row = call(
                    dual_final_kernel, [(TILES, 14, 8, 128), (DEVICES, 128)], steps
                )(
                    *common, price_list[0], price_list[1], bound_list[0], bound_list[1],
                    *shares, row,
                )
                got = lax.all_to_all(send, "period", 0, 0)
                row_sums = share_row(row)
                old_caps = caps_list
    mined, arcs, bounds = call(
        turn_back_kernel, [(4, NZ, NY), (ARCS, 4, NZ, NY), (4, NZ, NY)]
    )(got)
    caps, weight = call(finish_kernel, [(ROWS, 128), (1, 1)])(
        row_sums, *old_caps, limits, weight
    )
    own = lax.dynamic_slice(caps, (2 * tile, 0), (2, 128))[:, ::64]
    return (
        mined[None],
        arcs[:, None],
        bounds[None],
        jnp.reshape(own, (4,)),
        jnp.reshape(weight, (1,)),
    )


def solution(mesh):
    in_specs = (
        P("strip", "period", None, None),
        P(None, "strip", "period", None, None),
        P("strip", "period", None, None),
        P("period"),
        P("period"),
        P("strip", None, None),
        P("strip", None, None),
        P(),
        P("strip", None),
        P(),
    )
    out_specs = (
        P("strip", "period", None, None),
        P(None, "strip", "period", None, None),
        P("strip", "period", None, None),
        P("period"),
        P(),
    )
    return jax.shard_map(
        per_device, mesh=mesh, in_specs=in_specs, out_specs=out_specs, check_vma=False
    )
```

```python
import math

import jax
import jax.numpy as jnp
from jax import lax
from jax.experimental import pallas as pl
from jax.experimental.pallas import tpu as pltpu
from jax.sharding import PartitionSpec as P

OUTER = 2
INNER = 3
NX = 16
NY = 128
NZ = 64
NP = 64
RATE = math.log(1.1) / 12.0
EPS = 1e-06
SLOPE = 11.0
BLOCKS = float(NX * NY * NZ)
ROOT = math.sqrt(BLOCKS)
F32 = jnp.float32

PLANE = 32
TILES = 32
ROWS = NP // 2
DEVICES = 256
ARCS = 5
BOUND, SHARE, RIM, EXTRA, BLOCK = 5, 6, 7, 8, 9
SLOTS = 10
LANE_PRIMAL, LANE_DUAL, LANE_TONS = 40, 41, 42
HALO, EDGES, TONS, VALUE = 5, 6, 7, 8
PLANES = 9


def member(tile):
    chip, core = divmod(tile, 2)
    row, at = divmod(chip, 4)
    at = at if row % 2 == 0 else 3 - at
    return row % 2 * 16 + at * 4 + row // 2 * 2 + core


def lanes(shape):
    return lax.broadcasted_iota(jnp.int32, shape, len(shape) - 1)


def subs(shape):
    return lax.broadcasted_iota(jnp.int32, shape, len(shape) - 2)


def later_half(shape):
    return lanes(shape) >= 64


def half_matrix():
    a = subs((128, 128)) >= 64
    b = lanes((128, 128)) >= 64
    return (a == b).astype(F32)


def half_sums(rows):
    return jnp.dot(
        rows, half_matrix(), precision=lax.Precision.HIGHEST, preferred_element_type=F32
    )


def period_table():
    shape = (ROWS, 128)
    return (2 * subs(shape) + later_half(shape).astype(jnp.int32)).astype(F32)


def down(v):
    return pltpu.roll(v, 1, v.ndim - 1)


def up(v):
    return pltpu.roll(v, 127, v.ndim - 1)


def swap(v):
    return pltpu.roll(v, 64, v.ndim - 1)


def low(shape=(8, 128)):
    return subs(shape) < 4


def turn(v):
    return pltpu.roll(v, 4, v.ndim - 2)


def mix(one, two):
    return jnp.where(low(), one, turn(two)), jnp.where(low(), turn(one), two)


def pack_kernel(place, caps, limits, density, slope, ton_class, value, share, prec, bound, rim, out):
    x = place[0]
    row = (1, 128)
    code = slope[...]
    column = lanes(row)
    mask = [
        jnp.ones(row, F32),
        ((code & 1 == 1) & (jnp.full(row, x) + 1 < NX)).astype(F32),
        ((code >> 1 & 1 == 1) & (jnp.full(row, x) >= 1)).astype(F32),
        ((code >> 2 & 1 == 1) & (column + 1 < NY)).astype(F32),
        ((code >> 3 & 1 == 1) & (column >= 1)).astype(F32),
    ]
    top = subs((NZ, NY)) == 0

    def put(field, source):
        one = jnp.concatenate([source(0), source(1)], axis=0).T
        two = jnp.concatenate([source(2), source(3)], axis=0).T
        for m in range(TILES // 2):
            here = slice(8 * m, 8 * m + 8)
            even, odd = mix(one[here], two[here])
            out[member(2 * m), field] = even
            out[member(2 * m + 1), field] = odd

    for k in range(ARCS):
        put(k, lambda t, k=k: jnp.where(top, mask[k], prec[k, t]))
    put(BOUND, lambda t: bound[t])
    put(SHARE, lambda t: share[t])
    put(RIM, lambda t: rim[t])
    classes = ton_class[...]
    tons = jnp.zeros(classes.shape, F32)
    for c in range(8):
        tons = jnp.where(classes == c, (1.0 + c) * density[c], tons)
    blocks = jnp.concatenate([tons, value[...]], axis=0).T
    half = later_half(row)
    zero = jnp.zeros(row, F32)
    cap_rows = [jnp.where(half, caps[2 * a + 1], caps[2 * a]) for a in range(2)]
    limit_rows = [jnp.where(half, limits[2 * a + 1], limits[2 * a]) for a in range(2)]
    for j in range(TILES):
        i = member(j)
        two = blocks[8 * (j // 2) : 8 * (j // 2) + 8]
        out[i, BLOCK] = two if j % 2 == 0 else turn(two)
        for a in range(2):
            if j > 0:
                out[i, EXTRA, a : a + 1] = out[member(j - 1), 3, 4 * a + 3 : 4 * a + 4]
            else:
                out[i, EXTRA, a : a + 1] = zero
            if j < TILES - 1:
                out[i, EXTRA, 2 + a : 3 + a] = out[member(j + 1), 4, 4 * a : 4 * a + 1]
            else:
                out[i, EXTRA, 2 + a : 3 + a] = zero
            out[i, EXTRA, 4 + a : 5 + a] = cap_rows[a]
            out[i, EXTRA, 6 + a : 7 + a] = limit_rows[a]


def adjoint_row(prices, bound, halo, edges, r, carry):
    shape = (8, 128)
    sub = subs(shape)
    one = slice(r, r + 1)
    total = prices[0] + prices[1] + prices[2] + prices[3] + prices[4] + bound
    across = turn(jnp.where(low(), prices[1], prices[2]))
    before = pltpu.roll(prices[3], 1, 0)
    before = jnp.where(sub == 0, edges[0, 0, one], jnp.where(sub == 4, edges[0, 1, one], before))
    after = pltpu.roll(prices[4], 7, 0)
    after = jnp.where(sub == 3, edges[1, 0, one], jnp.where(sub == 7, edges[1, 1, one], after))
    lower = prices[0] + halo + across + before + after
    g = total - up(lower)
    pair = g + swap(g)
    return carry + jnp.where(later_half(shape), g, pair), carry + pair


def unpack_kernel(got, prices, halos, edges, bound, share, caps, limits, tail, masks):
    shape = (8, 128)
    lane = lanes(shape)
    deep = ((lane & 63) >= 1).astype(F32)
    half = later_half(shape)

    def pair(s, field):
        return mix(got[s, field], got[16 + s, field])

    for k in range(ARCS):
        masks[k] = jnp.broadcast_to(pair(0, k)[0][:, 0:1], shape) * deep
    masks[HALO] = jnp.broadcast_to(pair(0, RIM)[0][:, 0:1], shape) * deep
    for n in range(2):
        for x in range(2):
            at = 2 * n + x
            edge = got[16 * x, EXTRA, 2 * n : 2 * n + 1]
            masks[EDGES, at : at + 1] = jnp.broadcast_to(edge[:, 0:1], (1, 128)) * deep[0:1]
            masks[EDGES, 4 + at : 5 + at] = jnp.zeros((1, 128), F32)
    blocks = pair(0, BLOCK)[0]
    other = swap(blocks)
    masks[TONS] = jnp.where(half, other, blocks)
    masks[VALUE] = jnp.where(half, blocks, other)
    for s in range(ROWS // 2):
        two = slice(2 * s, 2 * s + 2)
        for n in range(2):
            for x in range(2):
                at = 2 * n + x
                edges[n, x, two] = got[16 * x + s, EXTRA, 2 * n : 2 * n + 2] * masks[EDGES, at : at + 1]
        caps[two] = got[s, EXTRA, 4:6]
        limits[two] = got[s, EXTRA, 6:8]
    carry = jnp.zeros(shape, F32)
    for s in reversed(range(ROWS // 2)):
        p = [pair(s, k) for k in range(ARCS)]
        b, u, h = pair(s, BOUND), pair(s, SHARE), pair(s, RIM)
        for a in (1, 0):
            r = 2 * s + a
            here = [p[k][a] * masks[k] for k in range(ARCS)]
            for k in range(ARCS):
                prices[k, r] = here[k]
            bound[r] = b[a]
            share[r] = u[a]
            halo = h[a] * masks[HALO]
            halos[r] = halo
            tail[r], carry = adjoint_row(here, b[a], halo, edges, r, carry)


def summed_row(got):
    total = got[0:8]
    for n in range(1, DEVICES // 8):
        total = total + got[8 * n : 8 * n + 8]
    return jnp.sum(total, axis=0, keepdims=True)


def lane_value(row, lane):
    return jnp.sum(jnp.where(lanes((1, 128)) == lane, row, 0.0), axis=1, keepdims=True)


def caps_after(row, caps, limits, weight):
    shape = (ROWS, 128)
    spread = jnp.where((lanes(shape) & 63) == subs(shape), jnp.broadcast_to(row, shape), 0.0)
    totals = half_sums(spread)
    tons_all = lane_value(row, LANE_TONS)
    return jnp.maximum(caps + weight * (totals - BLOCKS * limits) / tons_all, 0.0)


def weight_after(row, weight, mean, first):
    move_cap = jnp.sum(
        jnp.sum((mean - first) ** 2, axis=0, keepdims=True), axis=1, keepdims=True
    ) * (1.0 / 64.0)
    primal_move = lane_value(row, LANE_PRIMAL)
    dual_move = lane_value(row, LANE_DUAL) + move_cap
    return jnp.sqrt(weight * jnp.sqrt((dual_move + EPS) / (primal_move + EPS)))


def primal_step(
    caps, tail, share, planes, weight, new, head, low_rows, high_rows,
    first, last, row, cap_rows, rate_rows,
):
    shape = (8, 128)
    tons = planes[TONS]
    value = planes[VALUE]
    lean = tons / ROOT
    cap_rows[...] = caps
    periods = period_table()
    rate_rows[0] = jnp.exp(-RATE * periods)
    rate_rows[1] = SLOPE * (NP - periods)
    half = later_half(shape)
    carry = jnp.zeros(shape, F32)
    mined = []
    for r in range(ROWS):
        one = slice(r, r + 1)
        gradient = tail[r] + tons * cap_rows[one] / ROOT
        tau = 1.0 / (weight * (rate_rows[1, one] + lean))
        old = share[r]
        now = jnp.maximum(old - tau * (gradient - value * rate_rows[0, one]), 0.0)
        new[r] = now
        ahead = 2.0 * now - old
        pair = ahead + swap(ahead)
        cumulative = carry + jnp.where(half, pair, ahead)
        carry = carry + pair
        head[r] = cumulative
        for x in range(2):
            first[x, one] = cumulative[4 * x : 4 * x + 1]
            last[x, one] = cumulative[4 * x + 3 : 4 * x + 4]
        if r % 2 == 0:
            even = cumulative
        else:
            low_rows[r // 2], high_rows[r // 2] = mix(even, cumulative)
        mined.append(tons * ahead)
    mined.append(tons)
    sums = half_sums(jnp.concatenate(mined, axis=0))
    lane = lanes(shape)
    total = jnp.where(lane == LANE_TONS, sums[8 * ROWS :], 0.0)
    for r in range(ROWS):
        total = total + jnp.where((lane & 63) == r, sums[8 * r : 8 * r + 8], 0.0)
    row[...] = jnp.broadcast_to(jnp.sum(total, axis=0, keepdims=True), row.shape)


def primal_first_kernel(caps, tail, share, planes, weight, *rest):
    primal_step(caps[...], tail, share, planes, weight[...], *rest)


def primal_kernel(got, caps, limits, tail, share, planes, weight, caps_new, *rest):
    row = summed_row(got)
    caps_now = caps_after(row, caps[...], limits[...], weight[...])
    caps_new[...] = caps_now
    primal_step(caps_now, tail, share, planes, weight[...], *rest)


def restart(got, caps0, caps1, caps2, limits, weight):
    row = summed_row(got)
    caps3 = caps_after(row, caps2[...], limits[...], weight[...])
    mean = (caps1[...] + caps2[...] + caps3) / INNER
    return mean, weight_after(row, weight[...], mean, caps0[...])


def primal_restart_kernel(
    got, caps0, caps1, caps2, limits, tail, share, planes, weight, caps_new, weight_new, *rest
):
    mean, new = restart(got, caps0, caps1, caps2, limits, weight)
    caps_new[...] = mean
    weight_new[...] = new
    primal_step(mean, tail, share, planes, new, *rest)


def finish_kernel(got, caps0, caps1, caps2, limits, weight, caps_new, weight_new):
    mean, new = restart(got, caps0, caps1, caps2, limits, weight)
    caps_new[...] = mean
    weight_new[...] = new


def dual_rows(weight, planes, front, back, first, last, edges, steps, ahead):
    periods = period_table()
    steps[0] = weight[...] / (2.0 * (periods + 1.0))
    steps[1] = weight[...] / (periods + 1.0)
    new = []
    for n, outside, inside in ((0, front, first), (1, back, last)):
        new.append([])
        for x in range(2):
            at = 2 * n + x
            there = outside[x]
            ahead[n, x] = down(there)
            price = edges[n, x] + steps[0] * (there - down(inside[x]))
            new[n].append(jnp.maximum(price, 0.0) * planes[EDGES, at : at + 1])
    return new


def dual_pair(s, planes, head, lower, upper, prices, halos, bound, steps, ahead_rows):
    outside = mix(lower[s], upper[s])
    return [
        dual_row(2 * s + a, outside[a], planes, head, prices, halos, bound, steps, ahead_rows)
        for a in range(2)
    ]


def dual_row(r, outside, planes, head, prices, halos, bound, steps, ahead_rows):
    one = slice(r, r + 1)
    step = steps[0, one]
    here = head[r]
    under = down(here)
    away = down(outside)
    other = turn(under)
    sub = subs((8, 128))
    after = pltpu.roll(under, 7, 0)
    before = pltpu.roll(under, 1, 0)
    ahead = [
        under,
        jnp.where(low(), other, away),
        jnp.where(low(), away, other),
        jnp.where(
            sub == 3, ahead_rows[1, 0, one], jnp.where(sub == 7, ahead_rows[1, 1, one], after)
        ),
        jnp.where(
            sub == 0, ahead_rows[0, 0, one], jnp.where(sub == 4, ahead_rows[0, 1, one], before)
        ),
    ]
    p = [
        jnp.maximum(prices[k, r] + step * (here - ahead[k]), 0.0) * planes[k] for k in range(ARCS)
    ]
    b = jnp.maximum(bound[r] + steps[1, one] * (here - 1.0), 0.0)
    h = jnp.maximum(halos[r] + step * (outside - under), 0.0) * planes[HALO]
    return p, b, h


def dual_kernel(
    weight, planes, head, lower, upper, front, back, first, last, prices, halos, edges, bound,
    prices_new, halos_new, edges_new, bound_new, tail, steps, ahead,
):
    new = dual_rows(weight, planes, front, back, first, last, edges, steps, ahead)
    for n in range(2):
        for x in range(2):
            edges_new[n, x] = new[n][x]
    carry = jnp.zeros((8, 128), F32)
    for s in reversed(range(ROWS // 2)):
        both = dual_pair(s, planes, head, lower, upper, prices, halos, bound, steps, ahead)
        for a in (1, 0):
            r = 2 * s + a
            p, b, h = both[a]
            for k in range(ARCS):
                prices_new[k, r] = p[k]
            bound_new[r] = b
            halos_new[r] = h
            tail[r], carry = adjoint_row(p, b, h, edges_new, r, carry)


def mean_of(one, two, three):
    return (one + two + three) / INNER


def moves_kernel(moves, row, row_new):
    lane = lanes((1, 128))

    def whole(v):
        return jnp.sum(jnp.sum(v, axis=0, keepdims=True), axis=1, keepdims=True)

    new = row[0:1] + jnp.where(lane == LANE_PRIMAL, whole(moves[0]), 0.0)
    new = new + jnp.where(lane == LANE_DUAL, whole(moves[1]), 0.0)
    row_new[...] = jnp.broadcast_to(new, row_new.shape)


def dual_restart_kernel(
    weight, planes, head, lower, upper, front, back, first, last, prices, halos, edges, bound,
    prices0, prices1, halos1, edges1, bound0, bound1, share0, share1, share2, share3, row,
    prices_new, halos_new, edges_new, bound_new, tail, share_new, row_new, steps, ahead, moves,
):
    new = dual_rows(weight, planes, front, back, first, last, edges, steps, ahead)
    for n in range(2):
        for x in range(2):
            edges_new[n, x] = mean_of(edges1[n, x], edges[n, x], new[n][x])
    shape = (8, 128)
    carry = jnp.zeros(shape, F32)
    primal_move = jnp.zeros(shape, F32)
    dual_move = jnp.zeros(shape, F32)
    for s in reversed(range(ROWS // 2)):
        both = dual_pair(s, planes, head, lower, upper, prices, halos, bound, steps, ahead)
        for a in (1, 0):
            r = 2 * s + a
            p, b, h = both[a]
            p = [mean_of(prices1[k, r], prices[k, r], p[k]) for k in range(ARCS)]
            b = mean_of(bound1[r], bound[r], b)
            h = mean_of(halos1[r], halos[r], h)
            u = mean_of(share1[r], share2[r], share3[r])
            primal_move = primal_move + (u - share0[r]) ** 2
            dual_move = dual_move + (b - bound0[r]) ** 2
            for k in range(ARCS):
                dual_move = dual_move + (p[k] - prices0[k, r]) ** 2
                prices_new[k, r] = p[k]
            bound_new[r] = b
            halos_new[r] = h
            share_new[r] = u
            tail[r], carry = adjoint_row(p, b, h, edges_new, r, carry)
    moves[0] = primal_move
    moves[1] = dual_move
    moves_kernel(moves, row, row_new)


def dual_final_kernel(
    weight, planes, head, lower, upper, front, back, first, last, prices, halos, edges, bound,
    prices0, prices1, bound0, bound1, share0, share1, share2, share3, send, moves, steps, ahead,
):
    dual_rows(weight, planes, front, back, first, last, edges, steps, ahead)
    shape = (8, 128)
    primal_move = jnp.zeros(shape, F32)
    dual_move = jnp.zeros(shape, F32)
    for s in range(ROWS // 2):
        both = dual_pair(s, planes, head, lower, upper, prices, halos, bound, steps, ahead)
        means = []
        for a in range(2):
            r = 2 * s + a
            p, b, _ = both[a]
            p = [mean_of(prices1[k, r], prices[k, r], p[k]) for k in range(ARCS)]
            b = mean_of(bound1[r], bound[r], b)
            u = mean_of(share1[r], share2[r], share3[r])
            primal_move = primal_move + (u - share0[r]) ** 2
            dual_move = dual_move + (b - bound0[r]) ** 2
            for k in range(ARCS):
                dual_move = dual_move + (p[k] - prices0[k, r]) ** 2
            means.append(p + [b, u])
        for field in range(7):
            send[s, field], send[16 + s, field] = mix(means[0][field], means[1][field])
    moves[0] = primal_move
    moves[1] = dual_move


def turn_back_kernel(got, share, prec, bound):
    def take(field, target):
        rows = [
            mix(got[member(2 * m), field], got[member(2 * m + 1), field]) for m in range(TILES // 2)
        ]
        for a in range(2):
            turned = jnp.concatenate([pair[a] for pair in rows], axis=0).T
            target(2 * a, turned[0:64])
            target(2 * a + 1, turned[64:128])

    for k in range(ARCS):

        def store(t, v, k=k):
            prec[k, t] = v

        take(k, store)

    def store_bound(t, v):
        bound[t] = v

    def store_share(t, v):
        share[t] = v

    take(BOUND, store_bound)
    take(SHARE, store_share)


def f32(*shape):
    return jax.ShapeDtypeStruct(shape, F32)


VMEM = pl.BlockSpec(memory_space=pltpu.VMEM)
SMEM = pl.BlockSpec(memory_space=pltpu.SMEM)
FIELD = (ROWS, 8, 128)


def call(kernel, outs, scratch=(), scalars=0):
    def run(*args):
        specs = [SMEM] * scalars + [VMEM] * (len(args) - scalars)
        return pl.pallas_call(
            kernel,
            out_shape=[f32(*shape) for shape in outs],
            in_specs=specs,
            out_specs=[VMEM] * len(outs),
            scratch_shapes=[pltpu.VMEM(shape, F32) for shape in scratch],
            compiler_params=pltpu.CompilerParams(vmem_limit_bytes=12 * 1024 * 1024),
        )(*args)

    return run


STEP_OUTS = [
    FIELD, FIELD, (ROWS // 2, 8, 128), (ROWS // 2, 8, 128), (2, ROWS, 128), (2, ROWS, 128),
    (DEVICES, 128),
]
STEP_SCRATCH = [(ROWS, 128), (2, ROWS, 128)]
DUAL_OUTS = [(ARCS,) + FIELD, FIELD, (2, 2, ROWS, 128), FIELD, FIELD]
DUAL_SCRATCH = [(2, ROWS, 128), (2, 2, ROWS, 128)]
EVERY = ("strip", "period")


def share_row(row):
    return lax.all_to_all(row, EVERY, 0, 0, tiled=True)


def exchange(slots):
    groups = [[PLANE * z + i for i in range(PLANE)] for z in range(DEVICES // PLANE)]
    return lax.all_to_all(slots, EVERY, 0, 0, axis_index_groups=groups)


def along_x(value, by):
    planes = DEVICES // PLANE
    pairs = [
        (PLANE * z + i, PLANE * (z + by) + i)
        for z in range(planes)
        if 0 <= z + by < planes
        for i in range(PLANE)
    ]
    return lax.ppermute(value, EVERY, pairs)


def along_y(value, by):
    pairs = [
        (PLANE * z + member(j), PLANE * z + member(j + by))
        for z in range(DEVICES // PLANE)
        for j in range(TILES)
        if 0 <= j + by < TILES
    ]
    return lax.ppermute(value, EVERY, pairs)


def halo(low_rows, high_rows, first, last):
    back = along_y(first, -1)
    front = along_y(last, 1)
    lower = along_x(high_rows, 1)
    upper = along_x(low_rows, -1)
    return lower, upper, front, back


def per_device(
    u_start,
    dual_prec,
    dual_bound,
    dual_cap,
    capacity,
    block_value,
    ton_class,
    density,
    slope_code,
    omega_start,
):
    x, tile = lax.axis_index("strip"), lax.axis_index("period")
    prec = dual_prec[:, 0]
    top = (jnp.arange(NZ) == 0)[None, :, None]
    toward = ((slope_code & 1) * (x + 1 < NX)).astype(F32)[None]
    away = ((slope_code // 2 & 1) * (x >= 1)).astype(F32)[None]
    odd = x % 2 == 1
    rim = jnp.where(top, jnp.where(odd, toward, away), jnp.where(odd, prec[1], prec[2]))
    swaps = [(i, i + 1 if i % 2 else i - 1) for i in range(1, NX - 1)]
    rim = lax.ppermute(rim, "strip", swaps)
    place = jnp.reshape(x, (1,)).astype(jnp.int32)
    (send,) = call(pack_kernel, [(TILES, SLOTS, 8, 128)], (), 4)(
        place, dual_cap, capacity, density, slope_code, ton_class[0], block_value[0],
        u_start[0], prec, dual_bound[0], rim,
    )
    got = exchange(send)
    prices, halos, edges, bound, share, caps, limits, tail, planes = call(
        unpack_kernel,
        [
            (ARCS,) + FIELD, FIELD, (2, 2, ROWS, 128), FIELD, FIELD, (ROWS, 128), (ROWS, 128),
            FIELD, (PLANES, 8, 128),
        ],
    )(got)
    weight = jnp.reshape(omega_start, (1, 1))
    row_sums = None
    old_caps = None
    for outer in range(OUTER):
        shares, caps_list = [share], []
        price_list, halo_list, edge_list, bound_list = [prices], [halos], [edges], [bound]
        for inner in range(INNER):
            if inner == 0 and outer == 0:
                new, head, low_rows, high_rows, first, last, row = call(
                    primal_first_kernel, STEP_OUTS, STEP_SCRATCH
                )(caps, tail, share, planes, weight)
            elif inner == 0:
                caps, weight, new, head, low_rows, high_rows, first, last, row = call(
                    primal_restart_kernel, [(ROWS, 128), (1, 1)] + STEP_OUTS, STEP_SCRATCH
                )(row_sums, *old_caps, limits, tail, share, planes, weight)
            else:
                caps, new, head, low_rows, high_rows, first, last, row = call(
                    primal_kernel, [(ROWS, 128)] + STEP_OUTS, STEP_SCRATCH
                )(row_sums, caps, limits, tail, share, planes, weight)
            caps_list.append(caps)
            shares.append(new)
            share = new
            lower, upper, front, back = halo(low_rows, high_rows, first, last)
            common = (
                weight, planes, head, lower, upper, front, back, first, last,
                prices, halos, edges, bound,
            )
            if inner < INNER - 1:
                row_sums = share_row(row)
                prices, halos, edges, bound, tail = call(
                    dual_kernel, DUAL_OUTS, DUAL_SCRATCH
                )(*common)
                price_list.append(prices)
                halo_list.append(halos)
                edge_list.append(edges)
                bound_list.append(bound)
            elif outer < OUTER - 1:
                prices, halos, edges, bound, tail, share, row = call(
                    dual_restart_kernel, DUAL_OUTS + [FIELD, (DEVICES, 128)],
                    DUAL_SCRATCH + [(2, 8, 128)],
                )(
                    *common, price_list[0], price_list[1], halo_list[1], edge_list[1],
                    bound_list[0], bound_list[1], *shares, row,
                )
                row_sums = share_row(row)
                old_caps = caps_list
            else:
                send, moves = call(
                    dual_final_kernel, [(TILES, 7, 8, 128), (2, 8, 128)], DUAL_SCRATCH
                )(
                    *common, price_list[0], price_list[1], bound_list[0], bound_list[1], *shares,
                )
                got = exchange(send)
                (row,) = call(moves_kernel, [(DEVICES, 128)])(moves, row)
                row_sums = share_row(row)
                old_caps = caps_list
    mined, arcs, bounds = call(
        turn_back_kernel, [(4, NZ, NY), (ARCS, 4, NZ, NY), (4, NZ, NY)]
    )(got)
    caps, weight = call(finish_kernel, [(ROWS, 128), (1, 1)])(
        row_sums, *old_caps, limits, weight
    )
    own = lax.dynamic_slice(caps, (2 * tile, 0), (2, 128))[:, ::64]
    return (
        mined[None],
        arcs[:, None],
        bounds[None],
        jnp.reshape(own, (4,)),
        jnp.reshape(weight, (1,)),
    )


def solution(mesh):
    in_specs = (
        P("strip", "period", None, None),
        P(None, "strip", "period", None, None),
        P("strip", "period", None, None),
        P("period"),
        P("period"),
        P("strip", None, None),
        P("strip", None, None),
        P(),
        P("strip", None),
        P(),
    )
    out_specs = (
        P("strip", "period", None, None),
        P(None, "strip", "period", None, None),
        P("strip", "period", None, None),
        P("period"),
        P(),
    )
    return jax.shard_map(
        per_device, mesh=mesh, in_specs=in_specs, out_specs=out_specs, check_vma=False
    )
```

```python
import math

import jax
import jax.numpy as jnp
from jax import lax
from jax.experimental import pallas as pl
from jax.experimental.pallas import tpu as pltpu
from jax.sharding import PartitionSpec as P

OUTER = 2
INNER = 3
NX = 16
NY = 128
NZ = 64
NP = 64
RATE = math.log(1.1) / 12.0
EPS = 1e-06
SLOPE = 11.0
BLOCKS = float(NX * NY * NZ)
ROOT = math.sqrt(BLOCKS)
F32 = jnp.float32

PLANE = 32
TILES = 32
ROWS = NP // 2
DEVICES = 256
ARCS = 5
BOUND, SHARE, RIM, EXTRA, BLOCK = 5, 6, 7, 8, 9
SLOTS = 10
LANE_PRIMAL, LANE_DUAL, LANE_TONS = 40, 41, 42
HALO, EDGES, TONS, VALUE, ODD_X, ODD_Y = 5, 6, 7, 8, 9, 10
PLANES = 11
ROW = 7


def member(tile):
    chip, core = divmod(tile, 2)
    row, at = divmod(chip, 4)
    at = at if row % 2 == 0 else 3 - at
    return row % 2 * 16 + at * 4 + row // 2 * 2 + core


def lanes(shape):
    return lax.broadcasted_iota(jnp.int32, shape, len(shape) - 1)


def subs(shape):
    return lax.broadcasted_iota(jnp.int32, shape, len(shape) - 2)


def later_half(shape):
    return lanes(shape) >= 64


def half_matrix():
    a = subs((128, 128)) >= 64
    b = lanes((128, 128)) >= 64
    return (a == b).astype(F32)


def half_sums(rows):
    return jnp.dot(
        rows, half_matrix(), precision=lax.Precision.HIGHEST, preferred_element_type=F32
    )


def period_table():
    shape = (ROWS, 128)
    return (2 * subs(shape) + later_half(shape).astype(jnp.int32)).astype(F32)


def down(v):
    return pltpu.roll(v, 1, v.ndim - 1)


def up(v):
    return pltpu.roll(v, 127, v.ndim - 1)


def swap(v):
    return pltpu.roll(v, 64, v.ndim - 1)


def low(shape=(8, 128)):
    return subs(shape) < 4


def turn(v):
    return pltpu.roll(v, 4, v.ndim - 2)


def mix(one, two):
    return jnp.where(low(), one, turn(two)), jnp.where(low(), turn(one), two)


def fetch(pairs, sems):
    copies = [
        pltpu.make_async_copy(source, target, sems.at[n]) for n, (source, target) in enumerate(pairs)
    ]
    for copy in copies:
        copy.start()
    return copies


def put_tiles(source, target):
    one = jnp.concatenate([source(0), source(1)], axis=0).T
    two = jnp.concatenate([source(2), source(3)], axis=0).T
    for m in range(TILES // 2):
        here = slice(8 * m, 8 * m + 8)
        even, odd = mix(one[here], two[here])
        target(member(2 * m), even)
        target(member(2 * m + 1), odd)


def pack_kernel(
    small, place, slope_at, ton_class_at, value_at, share_at, prec_at, bound_at,
    out, slope, ton_class, value, share, prec, bound, sems,
):
    copies = fetch(
        [
            (slope_at, slope), (ton_class_at, ton_class), (value_at, value), (prec_at, prec),
            (bound_at, bound), (share_at, share),
        ],
        sems,
    )
    caps = [small[t] for t in range(4)]
    limits = [small[4 + t] for t in range(4)]
    density = [small[8 + c] for c in range(8)]
    for copy in copies:
        copy.wait()
    x = place[0]
    row = (1, 128)
    code = slope[...]
    column = lanes(row)
    mask = [
        jnp.ones(row, F32),
        ((code & 1 == 1) & (jnp.full(row, x) + 1 < NX)).astype(F32),
        ((code >> 1 & 1 == 1) & (jnp.full(row, x) >= 1)).astype(F32),
        ((code >> 2 & 1 == 1) & (column + 1 < NY)).astype(F32),
        ((code >> 3 & 1 == 1) & (column >= 1)).astype(F32),
    ]
    top = subs((NZ, NY)) == 0

    def put(field, source):
        def target(slot, tile):
            out[slot, field] = tile

        put_tiles(source, target)

    for k in range(ARCS):
        put(k, lambda t, k=k: jnp.where(top, mask[k], prec[k, t]))
    put(BOUND, lambda t: bound[t])
    put(SHARE, lambda t: share[t])
    classes = ton_class[...]
    tons = jnp.zeros(classes.shape, F32)
    for c in range(8):
        tons = jnp.where(classes == c, (1.0 + c) * density[c], tons)
    blocks = jnp.concatenate([tons, value[...]], axis=0).T
    half = later_half(row)
    zero = jnp.zeros(row, F32)
    cap_rows = [jnp.where(half, caps[2 * a + 1], caps[2 * a]) for a in range(2)]
    limit_rows = [jnp.where(half, limits[2 * a + 1], limits[2 * a]) for a in range(2)]
    for j in range(TILES):
        i = member(j)
        two = blocks[8 * (j // 2) : 8 * (j // 2) + 8]
        out[i, BLOCK] = two if j % 2 == 0 else turn(two)
        for a in range(2):
            if j > 0:
                out[i, EXTRA, a : a + 1] = out[member(j - 1), 3, 4 * a + 3 : 4 * a + 4]
            else:
                out[i, EXTRA, a : a + 1] = zero
            if j < TILES - 1:
                out[i, EXTRA, 2 + a : 3 + a] = out[member(j + 1), 4, 4 * a : 4 * a + 1]
            else:
                out[i, EXTRA, 2 + a : 3 + a] = zero
            out[i, EXTRA, 4 + a : 5 + a] = cap_rows[a]
            out[i, EXTRA, 6 + a : 7 + a] = limit_rows[a]


def rim_kernel(rim, send, out, tiles, sem):
    def target(slot, tile):
        tiles[slot] = tile

    put_tiles(lambda t: rim[t], target)
    copy = pltpu.make_async_copy(tiles, out.at[:, RIM], sem)
    copy.start()
    copy.wait()


def adjoint_row(prices, bound, halo, edges, r, carry):
    shape = (8, 128)
    sub = subs(shape)
    one = slice(r, r + 1)
    total = prices[0] + prices[1] + prices[2] + prices[3] + prices[4] + bound
    across = turn(jnp.where(low(), prices[1], prices[2]))
    before = pltpu.roll(prices[3], 1, 0)
    before = jnp.where(sub == 0, edges[0, 0, one], jnp.where(sub == 4, edges[0, 1, one], before))
    after = pltpu.roll(prices[4], 7, 0)
    after = jnp.where(sub == 3, edges[1, 0, one], jnp.where(sub == 7, edges[1, 1, one], after))
    lower = prices[0] + halo + across + before + after
    g = total - up(lower)
    pair = g + swap(g)
    return carry + jnp.where(later_half(shape), g, pair), carry + pair


def unpack_kernel(
    small, place, got, prices, halos, edges, bound, share, caps, limits, tail, masks, weight
):
    shape = (8, 128)
    weight[...] = jnp.full(shape, small[16])
    masks[ODD_X] = jnp.full(shape, place[0] // 2 % 2).astype(F32)
    masks[ODD_Y] = jnp.full(shape, place[1] % 2).astype(F32)
    lane = lanes(shape)
    deep = ((lane & 63) >= 1).astype(F32)
    half = later_half(shape)

    def pair(s, field):
        return mix(got[s, field], got[16 + s, field])

    for k in range(ARCS):
        masks[k] = jnp.broadcast_to(pair(0, k)[0][:, 0:1], shape) * deep
    masks[HALO] = jnp.broadcast_to(pair(0, RIM)[0][:, 0:1], shape) * deep
    for n in range(2):
        for x in range(2):
            at = 2 * n + x
            edge = got[16 * x, EXTRA, 2 * n : 2 * n + 1]
            masks[EDGES, at : at + 1] = jnp.broadcast_to(edge[:, 0:1], (1, 128)) * deep[0:1]
            masks[EDGES, 4 + at : 5 + at] = jnp.zeros((1, 128), F32)
    blocks = pair(0, BLOCK)[0]
    other = swap(blocks)
    masks[TONS] = jnp.where(half, other, blocks)
    masks[VALUE] = jnp.where(half, blocks, other)
    for s in range(ROWS // 2):
        two = slice(2 * s, 2 * s + 2)
        for n in range(2):
            for x in range(2):
                at = 2 * n + x
                edges[n, x, two] = got[16 * x + s, EXTRA, 2 * n : 2 * n + 2] * masks[EDGES, at : at + 1]
        caps[two] = got[s, EXTRA, 4:6]
        limits[two] = got[s, EXTRA, 6:8]
    carry = jnp.zeros(shape, F32)
    for s in reversed(range(ROWS // 2)):
        p = [pair(s, k) for k in range(ARCS)]
        b, u, h = pair(s, BOUND), pair(s, SHARE), pair(s, RIM)
        for a in (1, 0):
            r = 2 * s + a
            here = [p[k][a] * masks[k] for k in range(ARCS)]
            for k in range(ARCS):
                prices[k, r] = here[k]
            bound[r] = b[a]
            share[r] = u[a]
            halo = h[a] * masks[HALO]
            halos[r] = halo
            tail[r], carry = adjoint_row(here, b[a], halo, edges, r, carry)


def summed_row(got):
    total = got[0:8]
    for n in range(1, DEVICES // 8):
        total = total + got[8 * n : 8 * n + 8]
    return jnp.sum(total, axis=0, keepdims=True)


def lane_value(row, lane):
    return jnp.sum(jnp.where(lanes((1, 128)) == lane, row, 0.0), axis=1, keepdims=True)


def caps_after(row, caps, limits, weight):
    shape = (ROWS, 128)
    spread = jnp.where((lanes(shape) & 63) == subs(shape), jnp.broadcast_to(row, shape), 0.0)
    totals = half_sums(spread)
    tons_all = lane_value(row, LANE_TONS)
    return jnp.maximum(caps + weight * (totals - BLOCKS * limits) / tons_all, 0.0)


def weight_after(row, weight, mean, first):
    move_cap = jnp.sum(
        jnp.sum((mean - first) ** 2, axis=0, keepdims=True), axis=1, keepdims=True
    ) * (1.0 / 64.0)
    primal_move = lane_value(row, LANE_PRIMAL)
    dual_move = lane_value(row, LANE_DUAL) + move_cap
    return jnp.sqrt(weight * jnp.sqrt((dual_move + EPS) / (primal_move + EPS)))


def primal_step(
    caps, tail, share, planes, weight, new, head, x_one, x_two, y_one, y_two,
    first, last, row, cap_rows, rate_rows,
):
    shape = (8, 128)
    tons = planes[TONS]
    value = planes[VALUE]
    lean = tons / ROOT
    cap_rows[...] = caps
    periods = period_table()
    rate_rows[0] = jnp.exp(-RATE * periods)
    rate_rows[1] = SLOPE * (NP - periods)
    half = later_half(shape)
    odd_x = planes[ODD_X] > 0.5
    odd_y = planes[ODD_Y, 0:1] > 0.5
    carry = jnp.zeros(shape, F32)
    mined = []
    for r in range(ROWS):
        one = slice(r, r + 1)
        gradient = tail[r] + tons * cap_rows[one] / ROOT
        tau = 1.0 / (weight * (rate_rows[1, one] + lean))
        old = share[r]
        now = jnp.maximum(old - tau * (gradient - value * rate_rows[0, one]), 0.0)
        new[r] = now
        ahead = 2.0 * now - old
        pair = ahead + swap(ahead)
        cumulative = carry + jnp.where(half, pair, ahead)
        carry = carry + pair
        head[r] = cumulative
        for x in range(2):
            first[x, one] = cumulative[4 * x : 4 * x + 1]
            last[x, one] = cumulative[4 * x + 3 : 4 * x + 4]
        if r % 2 == 0:
            even = cumulative
        else:
            lows, highs = mix(even, cumulative)
            x_one[r // 2] = jnp.where(odd_x, lows, highs)
            x_two[r // 2] = jnp.where(odd_x, highs, lows)
        mined.append(tons * ahead)
    for x in range(2):
        y_one[x] = jnp.where(odd_y, first[x], last[x])
        y_two[x] = jnp.where(odd_y, last[x], first[x])
    mined.append(tons)
    sums = half_sums(jnp.concatenate(mined, axis=0))
    lane = lanes(shape)
    total = jnp.where(lane == LANE_TONS, sums[8 * ROWS :], 0.0)
    for r in range(ROWS):
        total = total + jnp.where((lane & 63) == r, sums[8 * r : 8 * r + 8], 0.0)
    row[...] = jnp.broadcast_to(jnp.sum(total, axis=0, keepdims=True), row.shape)


def primal_first_kernel(caps, tail, share, planes, weight, *rest):
    primal_step(caps[...], tail, share, planes, weight[0:1], *rest)


def primal_kernel(got, caps, limits, tail, share, planes, weight, caps_new, *rest):
    row = summed_row(got)
    caps_now = caps_after(row, caps[...], limits[...], weight[0:1])
    caps_new[...] = caps_now
    primal_step(caps_now, tail, share, planes, weight[0:1], *rest)


def restart(row, caps0, caps1, caps2, limits, weight):
    caps3 = caps_after(row, caps2[...], limits[...], weight[0:1])
    mean = (caps1[...] + caps2[...] + caps3) / INNER
    return mean, weight_after(row, weight[0:1], mean, caps0[...])


def primal_restart_kernel(
    got, caps0, caps1, caps2, limits, tail, share, planes, weight, caps_new, weight_new, *rest
):
    mean, new = restart(summed_row(got), caps0, caps1, caps2, limits, weight)
    caps_new[...] = mean
    weight_new[...] = jnp.broadcast_to(new, weight_new.shape)
    primal_step(mean, tail, share, planes, new, *rest)


def finish_kernel(got, caps0, caps1, caps2, limits, weight, caps_new, weight_new):
    row = jnp.sum(got[...], axis=0, keepdims=True)
    mean, new = restart(row, caps0, caps1, caps2, limits, weight)
    caps_new[...] = mean
    weight_new[...] = jnp.broadcast_to(new, weight_new.shape)


def dual_rows(weight, planes, y_one, y_two, first, last, edges, steps, ahead):
    odd_y = planes[ODD_Y, 0:1] > 0.5
    periods = period_table()
    steps[0] = weight[0:1] / (2.0 * (periods + 1.0))
    steps[1] = weight[0:1] / (periods + 1.0)
    new = []
    for n, inside in ((0, first), (1, last)):
        new.append([])
        for x in range(2):
            at = 2 * n + x
            before = jnp.where(odd_y, y_one[x], y_two[x])
            after = jnp.where(odd_y, y_two[x], y_one[x])
            there = after if n else before
            ahead[n, x] = down(there)
            price = edges[n, x] + steps[0] * (there - down(inside[x]))
            new[n].append(jnp.maximum(price, 0.0) * planes[EDGES, at : at + 1])
    return new


def dual_pair(s, planes, head, x_one, x_two, prices, halos, bound, steps, ahead_rows):
    odd = planes[ODD_X] > 0.5
    lower = jnp.where(odd, x_one[s], x_two[s])
    upper = jnp.where(odd, x_two[s], x_one[s])
    outside = mix(lower, upper)
    return [
        dual_row(2 * s + a, outside[a], planes, head, prices, halos, bound, steps, ahead_rows)
        for a in range(2)
    ]


def dual_row(r, outside, planes, head, prices, halos, bound, steps, ahead_rows):
    one = slice(r, r + 1)
    step = steps[0, one]
    here = head[r]
    under = down(here)
    away = down(outside)
    other = turn(under)
    sub = subs((8, 128))
    after = pltpu.roll(under, 7, 0)
    before = pltpu.roll(under, 1, 0)
    ahead = [
        under,
        jnp.where(low(), other, away),
        jnp.where(low(), away, other),
        jnp.where(
            sub == 3, ahead_rows[1, 0, one], jnp.where(sub == 7, ahead_rows[1, 1, one], after)
        ),
        jnp.where(
            sub == 0, ahead_rows[0, 0, one], jnp.where(sub == 4, ahead_rows[0, 1, one], before)
        ),
    ]
    p = [
        jnp.maximum(prices[k, r] + step * (here - ahead[k]), 0.0) * planes[k] for k in range(ARCS)
    ]
    b = jnp.maximum(bound[r] + steps[1, one] * (here - 1.0), 0.0)
    h = jnp.maximum(halos[r] + step * (outside - under), 0.0) * planes[HALO]
    return p, b, h


def dual_kernel(
    weight, planes, head, x_one, x_two, y_one, y_two, first, last, prices, halos, edges, bound,
    prices_new, halos_new, edges_new, bound_new, tail, steps, ahead,
):
    new = dual_rows(weight, planes, y_one, y_two, first, last, edges, steps, ahead)
    for n in range(2):
        for x in range(2):
            edges_new[n, x] = new[n][x]
    carry = jnp.zeros((8, 128), F32)
    for s in reversed(range(ROWS // 2)):
        both = dual_pair(s, planes, head, x_one, x_two, prices, halos, bound, steps, ahead)
        for a in (1, 0):
            r = 2 * s + a
            p, b, h = both[a]
            for k in range(ARCS):
                prices_new[k, r] = p[k]
            bound_new[r] = b
            halos_new[r] = h
            tail[r], carry = adjoint_row(p, b, h, edges_new, r, carry)


def mean_of(one, two, three):
    return (one + two + three) / INNER


def with_moves(row, primal_move, dual_move):
    lane = lanes((1, 128))

    def whole(v):
        return jnp.sum(jnp.sum(v, axis=0, keepdims=True), axis=1, keepdims=True)

    new = row[0:1] + jnp.where(lane == LANE_PRIMAL, whole(primal_move), 0.0)
    return new + jnp.where(lane == LANE_DUAL, whole(dual_move), 0.0)


def dual_restart_kernel(
    weight, planes, head, x_one, x_two, y_one, y_two, first, last, prices, halos, edges, bound,
    row, share3, *rest,
):
    olds, rest = rest[:9], rest[9:]
    prices_new, halos_new, edges_new, bound_new, tail, share_new, row_new, steps, ahead = rest[:9]
    sems, fetched = rest[9], rest[10:]
    copies = fetch(zip(olds, fetched), sems)
    prices0, prices1, bound0, bound1, share0, share1, share2, halos1, edges1 = fetched
    new = dual_rows(weight, planes, y_one, y_two, first, last, edges, steps, ahead)
    for copy in copies:
        copy.wait()
    for n in range(2):
        for x in range(2):
            edges_new[n, x] = mean_of(edges1[n, x], edges[n, x], new[n][x])
    shape = (8, 128)
    carry = jnp.zeros(shape, F32)
    primal_move = jnp.zeros(shape, F32)
    dual_move = jnp.zeros(shape, F32)
    for s in reversed(range(ROWS // 2)):
        both = dual_pair(s, planes, head, x_one, x_two, prices, halos, bound, steps, ahead)
        for a in (1, 0):
            r = 2 * s + a
            p, b, h = both[a]
            p = [mean_of(prices1[k, r], prices[k, r], p[k]) for k in range(ARCS)]
            b = mean_of(bound1[r], bound[r], b)
            h = mean_of(halos1[r], halos[r], h)
            u = mean_of(share1[r], share2[r], share3[r])
            primal_move = primal_move + (u - share0[r]) ** 2
            dual_move = dual_move + (b - bound0[r]) ** 2
            for k in range(ARCS):
                dual_move = dual_move + (p[k] - prices0[k, r]) ** 2
                prices_new[k, r] = p[k]
            bound_new[r] = b
            halos_new[r] = h
            share_new[r] = u
            tail[r], carry = adjoint_row(p, b, h, edges_new, r, carry)
    row_new[...] = jnp.broadcast_to(with_moves(row, primal_move, dual_move), row_new.shape)


def dual_final_kernel(
    weight, planes, head, x_one, x_two, y_one, y_two, first, last, prices, halos, edges, bound,
    row, share3, *rest,
):
    olds, rest = rest[:7], rest[7:]
    send, steps, ahead, sems = rest[:4]
    fetched = rest[4:]
    copies = fetch(zip(olds, fetched), sems)
    prices0, prices1, bound0, bound1, share0, share1, share2 = fetched
    dual_rows(weight, planes, y_one, y_two, first, last, edges, steps, ahead)
    for copy in copies:
        copy.wait()
    shape = (8, 128)
    primal_move = jnp.zeros(shape, F32)
    dual_move = jnp.zeros(shape, F32)
    for s in range(ROWS // 2):
        both = dual_pair(s, planes, head, x_one, x_two, prices, halos, bound, steps, ahead)
        means = []
        for a in range(2):
            r = 2 * s + a
            p, b, _ = both[a]
            p = [mean_of(prices1[k, r], prices[k, r], p[k]) for k in range(ARCS)]
            b = mean_of(bound1[r], bound[r], b)
            u = mean_of(share1[r], share2[r], share3[r])
            primal_move = primal_move + (u - share0[r]) ** 2
            dual_move = dual_move + (b - bound0[r]) ** 2
            for k in range(ARCS):
                dual_move = dual_move + (p[k] - prices0[k, r]) ** 2
            means.append(p + [b, u])
        for field in range(7):
            send[s, field], send[16 + s, field] = mix(means[0][field], means[1][field])
    tile = jnp.broadcast_to(with_moves(row, primal_move, dual_move), shape)
    for i in range(TILES):
        send[i, ROW] = tile


def plane_sum_kernel(got, out):
    total = got[0, ROW]
    for i in range(1, TILES):
        total = total + got[i, ROW]
    out[...] = total


def turn_back_kernel(got, share, prec, bound):
    def take(field, target):
        rows = [
            mix(got[member(2 * m), field], got[member(2 * m + 1), field]) for m in range(TILES // 2)
        ]
        for a in range(2):
            turned = jnp.concatenate([pair[a] for pair in rows], axis=0).T
            target(2 * a, turned[0:64])
            target(2 * a + 1, turned[64:128])

    for k in range(ARCS):

        def store(t, v, k=k):
            prec[k, t] = v

        take(k, store)

    def store_bound(t, v):
        bound[t] = v

    def store_share(t, v):
        share[t] = v

    take(BOUND, store_bound)
    take(SHARE, store_share)


def f32(*shape):
    return jax.ShapeDtypeStruct(shape, F32)


VMEM = pl.BlockSpec(memory_space=pltpu.VMEM)
SMEM = pl.BlockSpec(memory_space=pltpu.SMEM)
ANY = pl.BlockSpec(memory_space=pl.ANY)
FIELD = (ROWS, 8, 128)


def call(kernel, outs, scratch=(), scalars=0, far=0, out_space=VMEM, aliases=None):
    def run(*args):
        near = len(args) - scalars - far
        return pl.pallas_call(
            kernel,
            out_shape=[f32(*shape) for shape in outs],
            in_specs=[SMEM] * scalars + [VMEM] * near + [ANY] * far,
            out_specs=[out_space] * len(outs),
            scratch_shapes=[
                pltpu.VMEM(shape, F32) if isinstance(shape, tuple) else shape for shape in scratch
            ],
            input_output_aliases=aliases or {},
            compiler_params=pltpu.CompilerParams(vmem_limit_bytes=12 * 1024 * 1024),
            cost_estimate=pl.CostEstimate(
                flops=10**6, bytes_accessed=4 * 10**6, transcendentals=0
            ),
        )(*args)

    return run


def semaphores(n):
    return pltpu.SemaphoreType.DMA((n,))


STEP_OUTS = [
    FIELD, FIELD, (ROWS // 2, 8, 128), (ROWS // 2, 8, 128), (2, ROWS, 128), (2, ROWS, 128),
    (2, ROWS, 128), (2, ROWS, 128), (DEVICES, 128),
]
STEP_SCRATCH = [(ROWS, 128), (2, ROWS, 128)]
DUAL_OUTS = [(ARCS,) + FIELD, FIELD, (2, 2, ROWS, 128), FIELD, FIELD]
DUAL_SCRATCH = [(2, ROWS, 128), (2, 2, ROWS, 128)]
EVERY = ("strip", "period")


def share_row(row):
    return lax.all_to_all(row, EVERY, 0, 0, tiled=True)


def share_planes(row):
    planes = DEVICES // PLANE
    groups = [[PLANE * z + i for z in range(planes)] for i in range(PLANE)]
    return lax.all_to_all(row, EVERY, 0, 0, axis_index_groups=groups, tiled=True)


def exchange(slots):
    groups = [[PLANE * z + i for i in range(PLANE)] for z in range(DEVICES // PLANE)]
    return lax.all_to_all(slots, EVERY, 0, 0, axis_index_groups=groups)


def swap_x(value, odd):
    planes = DEVICES // PLANE
    pairs = []
    for z in range(planes):
        other = z + 1 if z % 2 == odd else z - 1
        if 0 <= other < planes:
            pairs += [(PLANE * z + i, PLANE * other + i) for i in range(PLANE)]
    return lax.ppermute(value, EVERY, pairs)


def swap_y(value, odd):
    pairs = []
    for j in range(TILES):
        other = j + 1 if j % 2 == odd else j - 1
        if 0 <= other < TILES:
            pairs += [
                (PLANE * z + member(j), PLANE * z + member(other)) for z in range(DEVICES // PLANE)
            ]
    return lax.ppermute(value, EVERY, pairs)


def halo(x_one, x_two, y_one, y_two):
    return swap_x(x_one, 0), swap_x(x_two, 1), swap_y(y_one, 0), swap_y(y_two, 1)


def per_device(
    u_start,
    dual_prec,
    dual_bound,
    dual_cap,
    capacity,
    block_value,
    ton_class,
    density,
    slope_code,
    omega_start,
):
    x, tile = lax.axis_index("strip"), lax.axis_index("period")
    arc = 2 - x % 2
    inside = jnp.where(x % 2 == 1, x + 1 < NX, x >= 1)
    toward = jnp.where(inside, slope_code >> (arc - 1) & 1, 0).astype(F32)[None]
    top = lax.broadcasted_iota(jnp.int32, (4, NZ, NY), 1) == 0
    rim = jnp.where(top, toward, lax.dynamic_index_in_dim(dual_prec[:, 0], arc, 0, False))
    swaps = [(i, i + 1 if i % 2 else i - 1) for i in range(1, NX - 1)]
    rim = lax.ppermute(rim, "strip", swaps)
    place = jnp.stack([x, tile]).astype(jnp.int32)
    small = jnp.concatenate([dual_cap, capacity, density, omega_start])
    plane = (NZ, NY)
    slots = (TILES, SLOTS, 8, 128)
    (send,) = call(
        pack_kernel,
        [slots],
        [
            pltpu.VMEM((1, NY), jnp.int32), pltpu.VMEM(plane, jnp.int32), plane, (4,) + plane,
            (ARCS, 4) + plane, (4,) + plane, semaphores(6),
        ],
        scalars=2,
        far=6,
    )(
        small, place, slope_code, ton_class[0], block_value[0], u_start[0], dual_prec[:, 0],
        dual_bound[0],
    )
    (send,) = call(
        rim_kernel,
        [slots],
        [(TILES, 8, 128), pltpu.SemaphoreType.DMA],
        far=1,
        out_space=ANY,
        aliases={1: 0},
    )(rim, send)
    got = exchange(send)
    prices, halos, edges, bound, share, caps, limits, tail, planes, weight = call(
        unpack_kernel,
        [
            (ARCS,) + FIELD, FIELD, (2, 2, ROWS, 128), FIELD, FIELD, (ROWS, 128), (ROWS, 128),
            FIELD, (PLANES, 8, 128), (8, 128),
        ],
        scalars=2,
    )(small, place, got)
    row_sums = None
    old_caps = None
    for outer in range(OUTER):
        shares, caps_list = [share], []
        price_list, halo_list, edge_list, bound_list = [prices], [halos], [edges], [bound]
        for inner in range(INNER):
            if inner == 0 and outer == 0:
                new, head, *sides, first, last, row = call(
                    primal_first_kernel, STEP_OUTS, STEP_SCRATCH
                )(caps, tail, share, planes, weight)
            elif inner == 0:
                caps, weight, new, head, *sides, first, last, row = call(
                    primal_restart_kernel, [(ROWS, 128), (8, 128)] + STEP_OUTS, STEP_SCRATCH
                )(row_sums, *old_caps, limits, tail, share, planes, weight)
            else:
                caps, new, head, *sides, first, last, row = call(
                    primal_kernel, [(ROWS, 128)] + STEP_OUTS, STEP_SCRATCH
                )(row_sums, caps, limits, tail, share, planes, weight)
            caps_list.append(caps)
            shares.append(new)
            share = new
            sides = halo(*sides)
            common = (
                weight, planes, head, *sides, first, last,
                prices, halos, edges, bound,
            )
            if inner < INNER - 1:
                row_sums = share_row(row)
                prices, halos, edges, bound, tail = call(
                    dual_kernel, DUAL_OUTS, DUAL_SCRATCH
                )(*common)
                price_list.append(prices)
                halo_list.append(halos)
                edge_list.append(edges)
                bound_list.append(bound)
            elif outer < OUTER - 1:
                olds = [
                    price_list[0], price_list[1], bound_list[0], bound_list[1], *shares[:3],
                    halo_list[1], edge_list[1],
                ]
                prices, halos, edges, bound, tail, share, row = call(
                    dual_restart_kernel,
                    DUAL_OUTS + [FIELD, (DEVICES, 128)],
                    DUAL_SCRATCH + [semaphores(9)] + [old.shape for old in olds],
                    far=9,
                )(*common, row, new, *olds)
                row_sums = share_row(row)
                old_caps = caps_list
            else:
                olds = [price_list[0], price_list[1], bound_list[0], bound_list[1], *shares[:3]]
                (send,) = call(
                    dual_final_kernel,
                    [(TILES, ROW + 1, 8, 128)],
                    DUAL_SCRATCH + [semaphores(7)] + [old.shape for old in olds],
                    far=7,
                )(*common, row, new, *olds)
                got = exchange(send)
                (row,) = call(plane_sum_kernel, [(8, 128)])(got)
                row_sums = share_planes(row)
                old_caps = caps_list
    mined, arcs, bounds = call(
        turn_back_kernel, [(4, NZ, NY), (ARCS, 4, NZ, NY), (4, NZ, NY)]
    )(got)
    caps, weight = call(finish_kernel, [(ROWS, 128), (8, 128)])(
        row_sums, *old_caps, limits, weight
    )
    own = lax.dynamic_slice(caps, (2 * tile, 0), (2, 128))[:, ::64]
    return (
        mined[None],
        arcs[:, None],
        bounds[None],
        jnp.reshape(own, (4,)),
        weight[0, 0:1],
    )


def solution(mesh):
    in_specs = (
        P("strip", "period", None, None),
        P(None, "strip", "period", None, None),
        P("strip", "period", None, None),
        P("period"),
        P("period"),
        P("strip", None, None),
        P("strip", None, None),
        P(),
        P("strip", None),
        P(),
    )
    out_specs = (
        P("strip", "period", None, None),
        P(None, "strip", "period", None, None),
        P("strip", "period", None, None),
        P("period"),
        P(),
    )
    return jax.shard_map(
        per_device, mesh=mesh, in_specs=in_specs, out_specs=out_specs, check_vma=False
    )
```

```python
import functools
import math

import jax
import jax.numpy as jnp
from jax import lax
from jax.experimental import pallas as pl
from jax.experimental.pallas import tpu as pltpu
from jax.sharding import PartitionSpec as P

OUTER = 2
INNER = 3
NX = 16
NY = 128
NZ = 64
NP = 64
RATE = math.log(1.1) / 12.0
EPS = 1e-06
SLOPE = 11.0
BLOCKS = float(NX * NY * NZ)
ROOT = math.sqrt(BLOCKS)
F32 = jnp.float32

PLANE = 32
TILES = 32
ROWS = NP // 2
DEVICES = 256
ARCS = 5
BOUND, SHARE, RIM, EXTRA = 5, 6, 7, 8
SLOTS = 9
LANE_PRIMAL, LANE_DUAL, LANE_TONS = 40, 41, 42
HALO, EDGES, TONS, VALUE, ODD_X, ODD_Y, LIMITS = 5, 6, 7, 8, 9, 10, 11
CONSTANTS = 15
TABLE = ROWS // 8
SHARES, SHARE_SUM, SHARE_FIRST, HEAD = 0, ROWS, 2 * ROWS, 3 * ROWS
CAPS = 4 * ROWS
CAP_SUM, CAP_FIRST, WEIGHT = CAPS + TABLE, CAPS + 2 * TABLE, CAPS + 3 * TABLE
FIRST = WEIGHT + 1
LAST = FIRST + 2 * TABLE
PRIMAL = LAST + 2 * TABLE
PRICES, BOUNDS, HALOS = 0, ARCS * ROWS, (ARCS + 1) * ROWS
EDGE_ROWS = (ARCS + 2) * ROWS
TAIL = EDGE_ROWS + 4 * TABLE
DUAL = TAIL + ROWS
ROW = 7


def member(tile):
    chip, core = divmod(tile, 2)
    row, at = divmod(chip, 4)
    at = at if row % 2 == 0 else 3 - at
    return row % 2 * 16 + at * 4 + row // 2 * 2 + core


def table(ref, at):
    return ref[at : at + TABLE].reshape(ROWS, 128)


def put_table(ref, at, value):
    ref[at : at + TABLE] = value.reshape(TABLE, 8, 128)


def line(ref, at, r):
    return ref[at + r // 8, r % 8 : r % 8 + 1]


def edge_at(n, x):
    return EDGE_ROWS + (2 * n + x) * TABLE


def lanes(shape):
    return lax.broadcasted_iota(jnp.int32, shape, len(shape) - 1)


def subs(shape):
    return lax.broadcasted_iota(jnp.int32, shape, len(shape) - 2)


def later_half(shape):
    return lanes(shape) >= 64


def half_matrix():
    a = subs((128, 128)) >= 64
    b = lanes((128, 128)) >= 64
    return (a == b).astype(F32)


def half_sums(rows):
    return jnp.dot(
        rows, half_matrix(), precision=lax.Precision.HIGHEST, preferred_element_type=F32
    )


def period_table():
    shape = (ROWS, 128)
    return (2 * subs(shape) + later_half(shape).astype(jnp.int32)).astype(F32)


def down(v):
    return pltpu.roll(v, 1, v.ndim - 1)


def up(v):
    return pltpu.roll(v, 127, v.ndim - 1)


def swap(v):
    return pltpu.roll(v, 64, v.ndim - 1)


def low(shape=(8, 128)):
    return subs(shape) < 4


def turn(v):
    return pltpu.roll(v, 4, v.ndim - 2)


def mix(one, two):
    return jnp.where(low(), one, turn(two)), jnp.where(low(), turn(one), two)


def fetch(pairs, sems):
    copies = [
        pltpu.make_async_copy(source, target, sems.at[n]) for n, (source, target) in enumerate(pairs)
    ]
    for copy in copies:
        copy.start()
    return copies


def put_tiles(source, target):
    one = jnp.concatenate([source(0), source(1)], axis=0).T
    two = jnp.concatenate([source(2), source(3)], axis=0).T
    for m in range(TILES // 2):
        here = slice(8 * m, 8 * m + 8)
        even, odd = mix(one[here], two[here])
        target(member(2 * m), even)
        target(member(2 * m + 1), odd)


def pack_kernel(
    small, place, slope_at, ton_class_at, value_at, share_at, prec_at, bound_at,
    out, slope, ton_class, value, share, prec, bound, sems,
):
    copies = fetch(
        [
            (slope_at, slope), (ton_class_at, ton_class), (value_at, value), (prec_at, prec),
            (bound_at, bound), (share_at, share),
        ],
        sems,
    )
    caps = [small[t] for t in range(4)]
    limits = [small[4 + t] for t in range(4)]
    density = [small[8 + c] for c in range(8)]
    for copy in copies:
        copy.wait()
    x = place[0]
    row = (1, 128)
    code = slope[...]
    column = lanes(row)
    mask = [
        None,
        ((code & 1 == 1) & (jnp.full(row, x) + 1 < NX)).astype(F32),
        ((code >> 1 & 1 == 1) & (jnp.full(row, x) >= 1)).astype(F32),
        ((code >> 2 & 1 == 1) & (column + 1 < NY)).astype(F32),
        ((code >> 3 & 1 == 1) & (column >= 1)).astype(F32),
    ]
    top = subs((NZ, NY)) == 0

    def put(field, source):
        def target(slot, tile):
            out[slot, field] = tile

        put_tiles(source, target)

    for k in range(ARCS):
        def source(t, k=k):
            spare = jnp.where(column % 2 == 0, caps[t], limits[t]) if k == 0 else mask[k]
            return jnp.where(top, spare, prec[k, t])

        put(k, source)
    put(BOUND, lambda t: bound[t])
    put(SHARE, lambda t: share[t])
    classes = ton_class[...]
    tons = jnp.zeros(classes.shape, F32)
    for c in range(8):
        tons = jnp.where(classes == c, (1.0 + c) * density[c], tons)
    blocks = jnp.concatenate([tons, value[...]], axis=0).T
    zero = jnp.zeros(row, F32)
    for j in range(TILES):
        i = member(j)
        out[i, EXTRA, 4:8] = blocks[4 * j : 4 * j + 4]
        for a in range(2):
            if j > 0:
                out[i, EXTRA, a : a + 1] = out[member(j - 1), 3, 4 * a + 3 : 4 * a + 4]
            else:
                out[i, EXTRA, a : a + 1] = zero
            if j < TILES - 1:
                out[i, EXTRA, 2 + a : 3 + a] = out[member(j + 1), 4, 4 * a : 4 * a + 1]
            else:
                out[i, EXTRA, 2 + a : 3 + a] = zero


def rim_kernel(rim, send, out, tiles, sem):
    def target(slot, tile):
        tiles[slot] = tile

    put_tiles(lambda t: rim[t], target)
    copy = pltpu.make_async_copy(tiles, out.at[:, RIM], sem)
    copy.start()
    copy.wait()


def adjoint_row(prices, bound, halo, dual, r, carry):
    shape = (8, 128)
    sub = subs(shape)
    edge = [[line(dual, edge_at(n, x), r) for x in range(2)] for n in range(2)]
    total = prices[0] + prices[1] + prices[2] + prices[3] + prices[4] + bound
    across = turn(jnp.where(low(), prices[1], prices[2]))
    before = pltpu.roll(prices[3], 1, 0)
    before = jnp.where(sub == 0, edge[0][0], jnp.where(sub == 4, edge[0][1], before))
    after = pltpu.roll(prices[4], 7, 0)
    after = jnp.where(sub == 3, edge[1][0], jnp.where(sub == 7, edge[1][1], after))
    lower = prices[0] + halo + across + before + after
    g = total - up(lower)
    pair = g + swap(g)
    return carry + jnp.where(later_half(shape), g, pair), carry + pair


def put_dual(dual, r, prices, bound, halo, carry):
    for k in range(ARCS):
        dual[PRICES + k * ROWS + r] = prices[k]
    dual[BOUNDS + r] = bound
    dual[HALOS + r] = halo
    dual[TAIL + r], carry = adjoint_row(prices, bound, halo, dual, r, carry)
    return carry


def unpack_kernel(small, place, got, primal, dual, const):
    shape = (8, 128)
    primal[WEIGHT] = jnp.full(shape, small[0])
    const[ODD_X] = jnp.full(shape, place[0] // 2 % 2).astype(F32)
    const[ODD_Y] = jnp.full(shape, place[1] % 2).astype(F32)
    lane = lanes(shape)
    deep = ((lane & 63) >= 1).astype(F32)
    half = later_half(shape)

    def pair(s, field):
        return mix(got[s, field], got[16 + s, field])

    const[0] = deep
    for k in range(1, ARCS):
        const[k] = jnp.broadcast_to(pair(0, k)[0][:, 0:1], shape) * deep
    const[HALO] = jnp.broadcast_to(pair(0, RIM)[0][:, 0:1], shape) * deep
    for n in range(2):
        for x in range(2):
            at = 2 * n + x
            edge = got[16 * x, EXTRA, 2 * n : 2 * n + 1]
            const[EDGES, at : at + 1] = jnp.broadcast_to(edge[:, 0:1], (1, 128)) * deep[0:1]
            const[EDGES, 4 + at : 5 + at] = jnp.zeros((1, 128), F32)
    blocks = jnp.where(low(), turn(got[0, EXTRA]), got[16, EXTRA])
    other = swap(blocks)
    const[TONS] = jnp.where(half, other, blocks)
    const[VALUE] = jnp.where(half, blocks, other)
    for s in range(ROWS // 2):
        tile, within = s // 4, slice(2 * s % 8, 2 * s % 8 + 2)
        for n in range(2):
            for x in range(2):
                at = 2 * n + x
                edge = got[16 * x + s, EXTRA, 2 * n : 2 * n + 2]
                dual[edge_at(n, x) + tile, within] = edge * const[EDGES, at : at + 1]
    carry = jnp.zeros(shape, F32)
    for s in reversed(range(ROWS // 2)):
        p = [pair(s, k) for k in range(ARCS)]
        b, u, h = pair(s, BOUND), pair(s, SHARE), pair(s, RIM)
        for a in (1, 0):
            r = 2 * s + a
            spare = jnp.where(
                half,
                jnp.broadcast_to(p[0][a][:, 64:65], shape),
                jnp.broadcast_to(p[0][a][:, 0:1], shape),
            )
            at = slice(r % 8, r % 8 + 1)
            primal[CAPS + r // 8, at] = spare[0:1]
            const[LIMITS + r // 8, at] = spare[1:2]
            primal[SHARES + r] = u[a]
            here = [p[k][a] * const[k] for k in range(ARCS)]
            carry = put_dual(dual, r, here, b[a], h[a] * const[HALO], carry)


def summed_row(got):
    total = got[0:8]
    for n in range(1, DEVICES // 8):
        total = total + got[8 * n : 8 * n + 8]
    return jnp.sum(total, axis=0, keepdims=True)


def lane_value(row, lane):
    return jnp.sum(jnp.where(lanes((1, 128)) == lane, row, 0.0), axis=1, keepdims=True)


def whole(v):
    return jnp.sum(jnp.sum(v, axis=0, keepdims=True), axis=1, keepdims=True)


def caps_after(row, primal, const):
    shape = (ROWS, 128)
    spread = jnp.where((lanes(shape) & 63) == subs(shape), jnp.broadcast_to(row, shape), 0.0)
    totals = half_sums(spread)
    tons_all = lane_value(row, LANE_TONS)
    over = (totals - BLOCKS * table(const, LIMITS)) / tons_all
    return jnp.maximum(table(primal, CAPS) + primal[WEIGHT, 0:1] * over, 0.0)


def restart(row, primal, const):
    mean = (table(primal, CAP_SUM) + caps_after(row, primal, const)) / INNER
    move_cap = whole((mean - table(primal, CAP_FIRST)) ** 2) * (1.0 / 64.0)
    primal_move = lane_value(row, LANE_PRIMAL)
    dual_move = lane_value(row, LANE_DUAL) + move_cap
    weight = primal[WEIGHT, 0:1]
    return mean, jnp.sqrt(weight * jnp.sqrt((dual_move + EPS) / (primal_move + EPS)))


def primal_step(inner, caps, weight, primal, dual, const, new, x_one, x_two, y_one, y_two, row, rates):
    shape = (8, 128)
    tons = const[TONS]
    value = const[VALUE]
    lean = tons / ROOT
    periods = period_table()
    rates[0] = jnp.exp(-RATE * periods)
    rates[1] = SLOPE * (NP - periods)
    put_table(new, CAPS, caps)
    put_table(new, CAP_FIRST, caps if inner == 0 else table(primal, CAP_FIRST))
    if inner == 0:
        put_table(new, CAP_SUM, jnp.zeros((ROWS, 128), F32))
    else:
        put_table(new, CAP_SUM, table(primal, CAP_SUM) + caps)
    new[WEIGHT] = jnp.broadcast_to(weight, shape)
    half = later_half(shape)
    odd_x = const[ODD_X] > 0.5
    odd_y = const[ODD_Y] > 0.5
    carry = jnp.zeros(shape, F32)
    moved = jnp.zeros(shape, F32)
    mined = []
    for r in range(ROWS):
        gradient = dual[TAIL + r] + tons * line(new, CAPS, r) / ROOT
        tau = 1.0 / (weight * (rates[1, r : r + 1] + lean))
        old = primal[SHARES + r]
        now = jnp.maximum(old - tau * (gradient - value * rates[0, r : r + 1]), 0.0)
        if inner == 0:
            new[SHARES + r] = now
            new[SHARE_SUM + r] = now
            new[SHARE_FIRST + r] = old
        elif inner < INNER - 1:
            new[SHARES + r] = now
            new[SHARE_SUM + r] = primal[SHARE_SUM + r] + now
            new[SHARE_FIRST + r] = primal[SHARE_FIRST + r]
        else:
            mean = (primal[SHARE_SUM + r] + now) / INNER
            new[SHARES + r] = mean
            moved = moved + (mean - primal[SHARE_FIRST + r]) ** 2
        ahead = 2.0 * now - old
        pair = ahead + swap(ahead)
        cumulative = carry + jnp.where(half, pair, ahead)
        carry = carry + pair
        new[HEAD + r] = cumulative
        at = slice(r % 8, r % 8 + 1)
        for x in range(2):
            tile = x * TABLE + r // 8
            new[FIRST + tile, at] = cumulative[4 * x : 4 * x + 1]
            new[LAST + tile, at] = cumulative[4 * x + 3 : 4 * x + 4]
        if r % 2 == 0:
            even = cumulative
        else:
            lows, highs = mix(even, cumulative)
            x_one[r // 2] = jnp.where(odd_x, lows, highs)
            x_two[r // 2] = jnp.where(odd_x, highs, lows)
        mined.append(tons * ahead)
    for n in range(2 * TABLE):
        y_one[n] = jnp.where(odd_y, new[FIRST + n], new[LAST + n])
        y_two[n] = jnp.where(odd_y, new[LAST + n], new[FIRST + n])
    mined.append(tons)
    sums = half_sums(jnp.concatenate(mined, axis=0))
    lane = lanes(shape)
    total = jnp.where(lane == LANE_TONS, sums[8 * ROWS :], 0.0)
    for r in range(ROWS):
        total = total + jnp.where((lane & 63) == r, sums[8 * r : 8 * r + 8], 0.0)
    total = jnp.sum(total, axis=0, keepdims=True)
    if inner == INNER - 1:
        total = total + jnp.where(lanes((1, 128)) == LANE_PRIMAL, whole(moved), 0.0)
    row[...] = jnp.broadcast_to(total, row.shape)


def primal_first_kernel(primal, dual, const, *rest):
    primal_step(0, table(primal, CAPS), primal[WEIGHT, 0:1], primal, dual, const, *rest)


def primal_kernel(inner, got, primal, dual, const, *rest):
    caps = caps_after(summed_row(got), primal, const)
    primal_step(inner, caps, primal[WEIGHT, 0:1], primal, dual, const, *rest)


def primal_restart_kernel(got, primal, dual, const, *rest):
    mean, weight = restart(summed_row(got), primal, const)
    primal_step(0, mean, weight, primal, dual, const, *rest)


def finish_kernel(got, primal, const, caps_new, weight_new):
    mean, weight = restart(jnp.sum(got[...], axis=0, keepdims=True), primal, const)
    caps_new[...] = mean
    weight_new[...] = jnp.broadcast_to(weight, weight_new.shape)


def dual_tables(primal, const, y_one, y_two, dual, steps, ahead):
    odd_y = const[ODD_Y, 0:1] > 0.5
    periods = period_table()
    weight = primal[WEIGHT, 0:1]
    steps[0] = weight / (2.0 * (periods + 1.0))
    steps[1] = weight / (periods + 1.0)
    new = []
    for n, inside in ((0, FIRST), (1, LAST)):
        new.append([])
        for x in range(2):
            at = 2 * n + x
            one, two = table(y_one, x * TABLE), table(y_two, x * TABLE)
            there = jnp.where(odd_y, two, one) if n else jnp.where(odd_y, one, two)
            ahead[n, x] = down(there)
            here = table(primal, inside + x * TABLE)
            price = table(dual, edge_at(n, x)) + steps[0] * (there - down(here))
            new[n].append(jnp.maximum(price, 0.0) * const[EDGES, at : at + 1])
    return new


def dual_pair(s, primal, const, x_one, x_two, dual, steps, ahead):
    odd = const[ODD_X] > 0.5
    lower = jnp.where(odd, x_one[s], x_two[s])
    upper = jnp.where(odd, x_two[s], x_one[s])
    outside = mix(lower, upper)
    return [dual_row(2 * s + a, outside[a], primal, const, dual, steps, ahead) for a in range(2)]


def dual_row(r, outside, primal, const, dual, steps, ahead_rows):
    one = slice(r, r + 1)
    step = steps[0, one]
    here = primal[HEAD + r]
    under = down(here)
    away = down(outside)
    other = turn(under)
    sub = subs((8, 128))
    after = pltpu.roll(under, 7, 0)
    before = pltpu.roll(under, 1, 0)
    ahead = [
        under,
        jnp.where(low(), other, away),
        jnp.where(low(), away, other),
        jnp.where(
            sub == 3, ahead_rows[1, 0, one], jnp.where(sub == 7, ahead_rows[1, 1, one], after)
        ),
        jnp.where(
            sub == 0, ahead_rows[0, 0, one], jnp.where(sub == 4, ahead_rows[0, 1, one], before)
        ),
    ]
    p = [
        jnp.maximum(dual[PRICES + k * ROWS + r] + step * (here - ahead[k]), 0.0) * const[k]
        for k in range(ARCS)
    ]
    b = jnp.maximum(dual[BOUNDS + r] + steps[1, one] * (here - 1.0), 0.0)
    h = jnp.maximum(dual[HALOS + r] + step * (outside - under), 0.0) * const[HALO]
    return p, b, h


def dual_kernel(primal, const, x_one, x_two, y_one, y_two, dual, new, steps, ahead):
    edges = dual_tables(primal, const, y_one, y_two, dual, steps, ahead)
    for n in range(2):
        for x in range(2):
            put_table(new, edge_at(n, x), edges[n][x])
    carry = jnp.zeros((8, 128), F32)
    for s in reversed(range(ROWS // 2)):
        both = dual_pair(s, primal, const, x_one, x_two, dual, steps, ahead)
        for a in (1, 0):
            carry = put_dual(new, 2 * s + a, *both[a], carry)


def mean_of(one, two, three):
    return (one + two + three) / INNER


def mean_row(r, dual0, dual1, dual, p, b, moved):
    mean = []
    for k in range(ARCS):
        at = PRICES + k * ROWS + r
        mean.append(mean_of(dual1[at], dual[at], p[k]))
        moved = moved + (mean[k] - dual0[at]) ** 2
    b = mean_of(dual1[BOUNDS + r], dual[BOUNDS + r], b)
    return mean, b, moved + (b - dual0[BOUNDS + r]) ** 2


def with_moves(row, moved):
    return row[0:1] + jnp.where(lanes((1, 128)) == LANE_DUAL, whole(moved), 0.0)


def dual_restart_kernel(
    primal, const, x_one, x_two, y_one, y_two, dual, row, dual0_at, dual1_at,
    new, row_new, steps, ahead, dual0, dual1, sems,
):
    copies = fetch([(dual0_at.at[0:HALOS], dual0), (dual1_at.at[0:TAIL], dual1)], sems)
    edges = dual_tables(primal, const, y_one, y_two, dual, steps, ahead)
    for copy in copies:
        copy.wait()
    for n in range(2):
        for x in range(2):
            at = edge_at(n, x)
            put_table(new, at, mean_of(table(dual1, at), table(dual, at), edges[n][x]))
    carry = jnp.zeros((8, 128), F32)
    moved = jnp.zeros((8, 128), F32)
    for s in reversed(range(ROWS // 2)):
        both = dual_pair(s, primal, const, x_one, x_two, dual, steps, ahead)
        for a in (1, 0):
            r = 2 * s + a
            p, b, h = both[a]
            p, b, moved = mean_row(r, dual0, dual1, dual, p, b, moved)
            h = mean_of(dual1[HALOS + r], dual[HALOS + r], h)
            carry = put_dual(new, r, p, b, h, carry)
    row_new[...] = jnp.broadcast_to(with_moves(row, moved), row_new.shape)


def dual_final_kernel(
    primal, const, x_one, x_two, y_one, y_two, dual, row, dual0_at, dual1_at,
    send, steps, ahead, dual0, dual1, sems,
):
    copies = fetch([(dual0_at.at[0:HALOS], dual0), (dual1_at.at[0:HALOS], dual1)], sems)
    dual_tables(primal, const, y_one, y_two, dual, steps, ahead)
    for copy in copies:
        copy.wait()
    moved = jnp.zeros((8, 128), F32)
    for s in range(ROWS // 2):
        both = dual_pair(s, primal, const, x_one, x_two, dual, steps, ahead)
        means = []
        for a in range(2):
            r = 2 * s + a
            p, b, _ = both[a]
            p, b, moved = mean_row(r, dual0, dual1, dual, p, b, moved)
            means.append(p + [b, primal[SHARES + r]])
        for field in range(ROW):
            send[s, field], send[16 + s, field] = mix(means[0][field], means[1][field])
    tile = jnp.broadcast_to(with_moves(row, moved), (8, 128))
    for i in range(TILES):
        send[i, ROW] = tile


def plane_sum_kernel(got, out):
    total = got[0, ROW]
    for i in range(1, TILES):
        total = total + got[i, ROW]
    out[...] = total


def turn_back_kernel(got, share, prec, bound):
    def take(field, target):
        rows = [
            mix(got[member(2 * m), field], got[member(2 * m + 1), field]) for m in range(TILES // 2)
        ]
        for a in range(2):
            turned = jnp.concatenate([pair[a] for pair in rows], axis=0).T
            target(2 * a, turned[0:64])
            target(2 * a + 1, turned[64:128])

    for k in range(ARCS):

        def store(t, v, k=k):
            prec[k, t] = v

        take(k, store)

    def store_bound(t, v):
        bound[t] = v

    def store_share(t, v):
        share[t] = v

    take(BOUND, store_bound)
    take(SHARE, store_share)


def f32(*shape):
    return jax.ShapeDtypeStruct(shape, F32)


VMEM = pl.BlockSpec(memory_space=pltpu.VMEM)
SMEM = pl.BlockSpec(memory_space=pltpu.SMEM)
ANY = pl.BlockSpec(memory_space=pl.ANY)


def call(kernel, outs, scratch=(), scalars=0, far=0, out_space=VMEM, aliases=None, vmem=12):
    def run(*args):
        near = len(args) - scalars - far
        return pl.pallas_call(
            kernel,
            out_shape=[f32(*shape) for shape in outs],
            in_specs=[SMEM] * scalars + [VMEM] * near + [ANY] * far,
            out_specs=[out_space] * len(outs),
            scratch_shapes=[
                pltpu.VMEM(shape, F32) if isinstance(shape, tuple) else shape for shape in scratch
            ],
            input_output_aliases=aliases or {},
            compiler_params=pltpu.CompilerParams(vmem_limit_bytes=vmem * 1024 * 1024),
            cost_estimate=pl.CostEstimate(
                flops=10**6, bytes_accessed=4 * 10**6, transcendentals=0
            ),
        )(*args)

    return run


def semaphores(n):
    return pltpu.SemaphoreType.DMA((n,))


STEP_OUTS = [
    (PRIMAL, 8, 128), (ROWS // 2, 8, 128), (ROWS // 2, 8, 128), (2 * TABLE, 8, 128),
    (2 * TABLE, 8, 128), (DEVICES, 128),
]
STEP_SCRATCH = [(2, ROWS, 128)]
DUAL_ARRAY = (DUAL, 8, 128)
DUAL_SCRATCH = [(2, ROWS, 128), (2, 2, ROWS, 128)]
PACK_VMEM = 62
EVERY = ("strip", "period")


def share_row(row):
    return lax.all_to_all(row, EVERY, 0, 0, tiled=True)


def share_planes(row):
    planes = DEVICES // PLANE
    groups = [[PLANE * z + i for z in range(planes)] for i in range(PLANE)]
    return lax.all_to_all(row, EVERY, 0, 0, axis_index_groups=groups, tiled=True)


def exchange(slots):
    groups = [[PLANE * z + i for i in range(PLANE)] for z in range(DEVICES // PLANE)]
    return lax.all_to_all(slots, EVERY, 0, 0, axis_index_groups=groups)


def swap_x(value, odd):
    planes = DEVICES // PLANE
    pairs = []
    for z in range(planes):
        other = z + 1 if z % 2 == odd else z - 1
        if 0 <= other < planes:
            pairs += [(PLANE * z + i, PLANE * other + i) for i in range(PLANE)]
    return lax.ppermute(value, EVERY, pairs)


def swap_y(value, odd):
    pairs = []
    for j in range(TILES):
        other = j + 1 if j % 2 == odd else j - 1
        if 0 <= other < TILES:
            pairs += [
                (PLANE * z + member(j), PLANE * z + member(other)) for z in range(DEVICES // PLANE)
            ]
    return lax.ppermute(value, EVERY, pairs)


def halo(x_one, x_two, y_one, y_two):
    return swap_x(x_one, 0), swap_x(x_two, 1), swap_y(y_one, 0), swap_y(y_two, 1)


def per_device(
    u_start,
    dual_prec,
    dual_bound,
    dual_cap,
    capacity,
    block_value,
    ton_class,
    density,
    slope_code,
    omega_start,
):
    x, tile = lax.axis_index("strip"), lax.axis_index("period")
    arc = 2 - x % 2
    inside = jnp.where(x % 2 == 1, x + 1 < NX, x >= 1)
    toward = jnp.where(inside, slope_code >> (arc - 1) & 1, 0).astype(F32)[None]
    top = lax.broadcasted_iota(jnp.int32, (4, NZ, NY), 1) == 0
    rim = jnp.where(top, toward, lax.dynamic_index_in_dim(dual_prec[:, 0], arc, 0, False))
    swaps = [(i, i + 1 if i % 2 else i - 1) for i in range(1, NX - 1)]
    rim = lax.ppermute(rim, "strip", swaps)
    place = jnp.stack([x, tile]).astype(jnp.int32)
    small = jnp.concatenate([dual_cap, capacity, density])
    plane = (NZ, NY)
    slots = (TILES, SLOTS, 8, 128)
    (send,) = call(
        pack_kernel,
        [slots],
        [
            pltpu.VMEM((1, NY), jnp.int32), pltpu.VMEM(plane, jnp.int32), plane, (4,) + plane,
            (ARCS, 4) + plane, (4,) + plane, semaphores(6),
        ],
        scalars=2,
        far=6,
        vmem=PACK_VMEM,
    )(
        small, place, slope_code, ton_class[0], block_value[0], u_start[0], dual_prec[:, 0],
        dual_bound[0],
    )
    (send,) = call(
        rim_kernel,
        [slots],
        [(TILES, 8, 128), pltpu.SemaphoreType.DMA],
        far=1,
        out_space=ANY,
        aliases={1: 0},
    )(rim, send)
    got = exchange(send)
    primal, dual, const = call(
        unpack_kernel, [(PRIMAL, 8, 128), DUAL_ARRAY, (CONSTANTS, 8, 128)], scalars=2
    )(omega_start, place, got)
    row_sums = None
    for outer in range(OUTER):
        duals = [dual]
        for inner in range(INNER):
            if inner > 0:
                step = functools.partial(primal_kernel, inner)
            else:
                step = primal_first_kernel if outer == 0 else primal_restart_kernel
            sums = [] if row_sums is None else [row_sums]
            primal, *sides, row = call(step, STEP_OUTS, STEP_SCRATCH)(*sums, primal, dual, const)
            sides = halo(*sides)
            if inner < INNER - 1:
                row_sums = share_row(row)
                (dual,) = call(dual_kernel, [DUAL_ARRAY], DUAL_SCRATCH)(
                    primal, const, *sides, dual
                )
                duals.append(dual)
            elif outer < OUTER - 1:
                dual, row = call(
                    dual_restart_kernel,
                    [DUAL_ARRAY, (DEVICES, 128)],
                    DUAL_SCRATCH + [(HALOS, 8, 128), (TAIL, 8, 128), semaphores(2)],
                    far=2,
                )(primal, const, *sides, dual, row, duals[0], duals[1])
                row_sums = share_row(row)
            else:
                (send,) = call(
                    dual_final_kernel,
                    [(TILES, ROW + 1, 8, 128)],
                    DUAL_SCRATCH + [(HALOS, 8, 128), (HALOS, 8, 128), semaphores(2)],
                    far=2,
                )(primal, const, *sides, dual, row, duals[0], duals[1])
                got = exchange(send)
                (row,) = call(plane_sum_kernel, [(8, 128)])(got)
                row_sums = share_planes(row)
    mined, arcs, bounds = call(
        turn_back_kernel, [(4, NZ, NY), (ARCS, 4, NZ, NY), (4, NZ, NY)]
    )(got)
    caps, weight = call(finish_kernel, [(ROWS, 128), (8, 128)])(row_sums, primal, const)
    own = lax.dynamic_slice(caps, (2 * tile, 0), (2, 128))[:, ::64]
    return (
        mined[None],
        arcs[:, None],
        bounds[None],
        jnp.reshape(own, (4,)),
        weight[0, 0:1],
    )


def solution(mesh):
    in_specs = (
        P("strip", "period", None, None),
        P(None, "strip", "period", None, None),
        P("strip", "period", None, None),
        P("period"),
        P("period"),
        P("strip", None, None),
        P("strip", None, None),
        P(),
        P("strip", None),
        P(),
    )
    out_specs = (
        P("strip", "period", None, None),
        P(None, "strip", "period", None, None),
        P("strip", "period", None, None),
        P("period"),
        P(),
    )
    return jax.shard_map(
        per_device, mesh=mesh, in_specs=in_specs, out_specs=out_specs, check_vma=False
    )
```

```python
import functools
import math

import jax
import jax.numpy as jnp
from jax import lax
from jax.experimental import pallas as pl
from jax.experimental.pallas import tpu as pltpu
from jax.sharding import PartitionSpec as P

OUTER = 2
INNER = 3
NX = 16
NY = 128
NZ = 64
NP = 64
RATE = math.log(1.1) / 12.0
EPS = 1e-06
SLOPE = 11.0
BLOCKS = float(NX * NY * NZ)
ROOT = math.sqrt(BLOCKS)
F32 = jnp.float32

PLANE = 32
TILES = 32
ROWS = NP // 2
DEVICES = 256
ARCS = 5
BOUND, SHARE, RIM, EXTRA = 5, 6, 7, 8
SLOTS = 9
LANE_PRIMAL, LANE_DUAL, LANE_TONS = 32, 33, 34
HALO, EDGES, TONS, VALUE, ODD_X, ODD_Y, LIMITS = 5, 6, 7, 8, 9, 10, 11
CONSTANTS = 15
TABLE = ROWS // 8
SHARES, SHARE_SUM, SHARE_FIRST, HEAD = 0, ROWS, 2 * ROWS, 3 * ROWS
CAPS = 4 * ROWS
CAP_SUM, CAP_FIRST, WEIGHT = CAPS + TABLE, CAPS + 2 * TABLE, CAPS + 3 * TABLE
FIRST = WEIGHT + 1
LAST = FIRST + 2 * TABLE
PRIMAL = LAST + 2 * TABLE
PRICES, BOUNDS = 0, ARCS * ROWS
DUAL = BOUNDS + ROWS
HALOS, EDGE_ROWS = 0, ROWS
INWARD = EDGE_ROWS + 4 * TABLE
BACK = 7


def member(tile):
    chip, core = divmod(tile, 2)
    row, at = divmod(chip, 4)
    at = at if row % 2 == 0 else 3 - at
    return row % 2 * 16 + at * 4 + row // 2 * 2 + core


def table(ref, at):
    return ref[at : at + TABLE].reshape(ROWS, 128)


def put_table(ref, at, value):
    ref[at : at + TABLE] = value.reshape(TABLE, 8, 128)


def line(ref, at, r):
    return ref[at + r // 8, r % 8 : r % 8 + 1]


def edge_at(n, x):
    return EDGE_ROWS + (2 * n + x) * TABLE


def lanes(shape):
    return lax.broadcasted_iota(jnp.int32, shape, len(shape) - 1)


def subs(shape):
    return lax.broadcasted_iota(jnp.int32, shape, len(shape) - 2)


def later_half(shape):
    return lanes(shape) >= 64


def half_matrix():
    a = subs((128, 128)) >= 64
    b = lanes((128, 128)) >= 64
    return (a == b).astype(F32)


def half_sums(rows):
    return jnp.dot(
        rows, half_matrix(), precision=lax.Precision.HIGHEST, preferred_element_type=F32
    )


def period_table():
    shape = (ROWS, 128)
    return (2 * subs(shape) + later_half(shape).astype(jnp.int32)).astype(F32)


def down(v):
    return pltpu.roll(v, 1, v.ndim - 1)


def up(v):
    return pltpu.roll(v, 127, v.ndim - 1)


def swap(v):
    return pltpu.roll(v, 64, v.ndim - 1)


def low(shape=(8, 128)):
    return subs(shape) < 4


def turn(v):
    return pltpu.roll(v, 4, v.ndim - 2)


def mix(one, two):
    return jnp.where(low(), one, turn(two)), jnp.where(low(), turn(one), two)


def fetch(pairs, sems):
    copies = [
        pltpu.make_async_copy(source, target, sems.at[n]) for n, (source, target) in enumerate(pairs)
    ]
    for copy in copies:
        copy.start()
    return copies


def put_tiles(source, target):
    one = jnp.concatenate([source(0), source(1)], axis=0).T
    two = jnp.concatenate([source(2), source(3)], axis=0).T
    for m in range(TILES // 2):
        here = slice(8 * m, 8 * m + 8)
        even, odd = mix(one[here], two[here])
        target(member(2 * m), even)
        target(member(2 * m + 1), odd)


def rim_kernel(slope_at, prec_at, rim, slope, sems):
    x = lax.axis_index("strip")
    odd = x % 2
    arc = 2 - odd
    copies = fetch([(slope_at, slope), (prec_at.at[arc], rim)], sems)
    inside = jnp.where(odd == 1, x + 1 < NX, x >= 1).astype(jnp.int32)
    for copy in copies:
        copy.wait()
    toward = ((slope[...] >> (arc - 1)) & inside).astype(F32)
    for t in range(rim.shape[0]):
        rim[t, 0:1] = toward


def pack_kernel(
    caps_at, limits_at, density_at, slope_at, ton_class_at, value_at, share_at, prec_at, bound_at,
    out, caps, limits, density, slope, ton_class, value, share, prec, bound, sems,
):
    copies = fetch(
        [
            (slope_at, slope), (ton_class_at, ton_class), (value_at, value), (prec_at, prec),
            (bound_at, bound), (share_at, share), (caps_at, caps), (limits_at, limits),
            (density_at, density),
        ],
        sems,
    )
    for copy in copies:
        copy.wait()
    x = lax.axis_index("strip")
    row = (1, 128)
    code = slope[...]
    column = lanes(row)
    mask = [
        None,
        ((code & 1 == 1) & (jnp.full(row, x) + 1 < NX)).astype(F32),
        ((code >> 1 & 1 == 1) & (jnp.full(row, x) >= 1)).astype(F32),
        ((code >> 2 & 1 == 1) & (column + 1 < NY)).astype(F32),
        ((code >> 3 & 1 == 1) & (column >= 1)).astype(F32),
    ]
    top = subs((NZ, NY)) == 0

    def put(field, source):
        def target(slot, tile):
            out[slot, field] = tile

        put_tiles(source, target)

    for k in range(ARCS):
        def source(t, k=k):
            spare = jnp.where(column % 2 == 0, caps[t], limits[t]) if k == 0 else mask[k]
            return jnp.where(top, spare, prec[k, t])

        put(k, source)
    put(BOUND, lambda t: bound[t])
    put(SHARE, lambda t: share[t])
    classes = ton_class[...]
    tons = jnp.zeros(classes.shape, F32)
    for c in range(8):
        tons = jnp.where(classes == c, (1.0 + c) * density[c], tons)
    blocks = jnp.concatenate([tons, value[...]], axis=0).T
    zero = jnp.zeros(row, F32)
    for j in range(TILES):
        i = member(j)
        out[i, EXTRA, 4:8] = blocks[4 * j : 4 * j + 4]
        for a in range(2):
            if j > 0:
                out[i, EXTRA, a : a + 1] = out[member(j - 1), 3, 4 * a + 3 : 4 * a + 4]
            else:
                out[i, EXTRA, a : a + 1] = zero
            if j < TILES - 1:
                out[i, EXTRA, 2 + a : 3 + a] = out[member(j + 1), 4, 4 * a : 4 * a + 1]
            else:
                out[i, EXTRA, 2 + a : 3 + a] = zero


def put_rim_kernel(rim_at, send, out, rim, tiles, sems):
    (copy,) = fetch([(rim_at, rim)], sems)
    copy.wait()

    def target(slot, tile):
        tiles[slot] = tile

    put_tiles(lambda t: rim[t], target)
    (copy,) = fetch([(tiles, out.at[:, RIM])], sems)
    copy.wait()


def adjoint_row(prices, bound, halo, inward, r, carry):
    shape = (8, 128)
    sub = subs(shape)
    edge = [[line(inward, edge_at(n, x), r) for x in range(2)] for n in range(2)]
    total = prices[0] + prices[1] + prices[2] + prices[3] + prices[4] + bound
    across = turn(jnp.where(low(), prices[1], prices[2]))
    before = pltpu.roll(prices[3], 1, 0)
    before = jnp.where(sub == 0, edge[0][0], jnp.where(sub == 4, edge[0][1], before))
    after = pltpu.roll(prices[4], 7, 0)
    after = jnp.where(sub == 3, edge[1][0], jnp.where(sub == 7, edge[1][1], after))
    lower = prices[0] + halo + across + before + after
    g = total - up(lower)
    pair = g + swap(g)
    return carry + jnp.where(later_half(shape), g, pair), carry + pair


def put_dual(dual, inward, tail, r, prices, bound, halo, carry):
    for k in range(ARCS):
        dual[PRICES + k * ROWS + r] = prices[k]
    dual[BOUNDS + r] = bound
    inward[HALOS + r] = halo
    tail[r], carry = adjoint_row(prices, bound, halo, inward, r, carry)
    return carry


def unpack_kernel(got, weight, primal, dual, inward, tail, const):
    shape = (8, 128)
    primal[WEIGHT] = jnp.broadcast_to(weight[...], shape)
    const[ODD_X] = jnp.full(shape, lax.axis_index("strip") // 2 % 2).astype(F32)
    const[ODD_Y] = jnp.full(shape, lax.axis_index("period") % 2).astype(F32)
    lane = lanes(shape)
    deep = ((lane & 63) >= 1).astype(F32)
    half = later_half(shape)

    def pair(s, field):
        return mix(got[s, field], got[16 + s, field])

    const[0] = deep
    for k in range(1, ARCS):
        const[k] = jnp.broadcast_to(pair(0, k)[0][:, 0:1], shape) * deep
    const[HALO] = jnp.broadcast_to(pair(0, RIM)[0][:, 0:1], shape) * deep
    for n in range(2):
        for x in range(2):
            at = 2 * n + x
            edge = got[16 * x, EXTRA, 2 * n : 2 * n + 1]
            const[EDGES, at : at + 1] = jnp.broadcast_to(edge[:, 0:1], (1, 128)) * deep[0:1]
            const[EDGES, 4 + at : 5 + at] = jnp.zeros((1, 128), F32)
    blocks = jnp.where(low(), turn(got[0, EXTRA]), got[16, EXTRA])
    other = swap(blocks)
    const[TONS] = jnp.where(half, other, blocks)
    const[VALUE] = jnp.where(half, blocks, other)
    for s in range(ROWS // 2):
        tile, within = s // 4, slice(2 * s % 8, 2 * s % 8 + 2)
        for n in range(2):
            for x in range(2):
                at = 2 * n + x
                edge = got[16 * x + s, EXTRA, 2 * n : 2 * n + 2]
                inward[edge_at(n, x) + tile, within] = edge * const[EDGES, at : at + 1]
    carry = jnp.zeros(shape, F32)
    for s in reversed(range(ROWS // 2)):
        p = [pair(s, k) for k in range(ARCS)]
        b, u, h = pair(s, BOUND), pair(s, SHARE), pair(s, RIM)
        for a in (1, 0):
            r = 2 * s + a
            spare = jnp.where(
                half,
                jnp.broadcast_to(p[0][a][:, 64:65], shape),
                jnp.broadcast_to(p[0][a][:, 0:1], shape),
            )
            at = slice(r % 8, r % 8 + 1)
            primal[CAPS + r // 8, at] = spare[0:1]
            const[LIMITS + r // 8, at] = spare[1:2]
            primal[SHARES + r] = u[a]
            here = [p[k][a] * const[k] for k in range(ARCS)]
            carry = put_dual(dual, inward, tail, r, here, b[a], h[a] * const[HALO], carry)


def summed_row(got):
    total = got[0:8]
    for n in range(1, DEVICES // 8):
        total = total + got[8 * n : 8 * n + 8]
    return jnp.sum(total, axis=0, keepdims=True)


def lane_value(row, lane):
    return jnp.sum(jnp.where(lanes((1, 128)) == lane, row, 0.0), axis=1, keepdims=True)


def whole(v):
    return jnp.sum(jnp.sum(v, axis=0, keepdims=True), axis=1, keepdims=True)


def caps_after(row, primal, const):
    shape = (ROWS, 128)
    spread = jnp.where((lanes(shape) & 63) == subs(shape), jnp.broadcast_to(row, shape), 0.0)
    totals = half_sums(spread)
    tons_all = lane_value(row, LANE_TONS)
    over = (totals - BLOCKS * table(const, LIMITS)) / tons_all
    return jnp.maximum(table(primal, CAPS) + primal[WEIGHT, 0:1] * over, 0.0)


def restart(row, primal, const):
    mean = (table(primal, CAP_SUM) + caps_after(row, primal, const)) / INNER
    move_cap = whole((mean - table(primal, CAP_FIRST)) ** 2) * (1.0 / 64.0)
    primal_move = lane_value(row, LANE_PRIMAL)
    dual_move = lane_value(row, LANE_DUAL) + move_cap
    weight = primal[WEIGHT, 0:1]
    return mean, jnp.sqrt(weight * jnp.sqrt((dual_move + EPS) / (primal_move + EPS)))


def primal_step(inner, caps, weight, primal, tail, const, new, x_one, x_two, y_one, y_two, row, rates):
    shape = (8, 128)
    tons = const[TONS]
    value = const[VALUE]
    lean = tons / ROOT
    periods = period_table()
    rates[0] = jnp.exp(-RATE * periods)
    rates[1] = SLOPE * (NP - periods)
    put_table(new, CAPS, caps)
    put_table(new, CAP_FIRST, caps if inner == 0 else table(primal, CAP_FIRST))
    if inner == 0:
        put_table(new, CAP_SUM, jnp.zeros((ROWS, 128), F32))
    else:
        put_table(new, CAP_SUM, table(primal, CAP_SUM) + caps)
    new[WEIGHT] = jnp.broadcast_to(weight, shape)
    half = later_half(shape)
    odd_x = const[ODD_X] > 0.5
    odd_y = const[ODD_Y] > 0.5
    carry = jnp.zeros(shape, F32)
    moved = jnp.zeros(shape, F32)
    mined = []
    for r in range(ROWS):
        gradient = tail[r] + tons * line(new, CAPS, r) / ROOT
        tau = 1.0 / (weight * (rates[1, r : r + 1] + lean))
        old = primal[SHARES + r]
        now = jnp.maximum(old - tau * (gradient - value * rates[0, r : r + 1]), 0.0)
        if inner == 0:
            new[SHARES + r] = now
            new[SHARE_SUM + r] = now
            new[SHARE_FIRST + r] = old
        elif inner < INNER - 1:
            new[SHARES + r] = now
            new[SHARE_SUM + r] = primal[SHARE_SUM + r] + now
            new[SHARE_FIRST + r] = primal[SHARE_FIRST + r]
        else:
            mean = (primal[SHARE_SUM + r] + now) / INNER
            new[SHARES + r] = mean
            moved = moved + (mean - primal[SHARE_FIRST + r]) ** 2
        ahead = 2.0 * now - old
        pair = ahead + swap(ahead)
        cumulative = carry + jnp.where(half, pair, ahead)
        carry = carry + pair
        new[HEAD + r] = cumulative
        at = slice(r % 8, r % 8 + 1)
        for x in range(2):
            tile = x * TABLE + r // 8
            new[FIRST + tile, at] = cumulative[4 * x : 4 * x + 1]
            new[LAST + tile, at] = cumulative[4 * x + 3 : 4 * x + 4]
        if r % 2 == 0:
            even = cumulative
        else:
            lows, highs = mix(even, cumulative)
            x_one[r // 2] = jnp.where(odd_x, lows, highs)
            x_two[r // 2] = jnp.where(odd_x, highs, lows)
        mined.append(tons * ahead)
    for n in range(2 * TABLE):
        y_one[n] = jnp.where(odd_y, new[FIRST + n], new[LAST + n])
        y_two[n] = jnp.where(odd_y, new[LAST + n], new[FIRST + n])
    mined.append(tons)
    sums = half_sums(jnp.concatenate(mined, axis=0))
    lane = lanes(shape)
    total = jnp.where(lane == LANE_TONS, sums[8 * ROWS :], 0.0)
    for r in range(ROWS):
        total = total + jnp.where((lane & 63) == r, sums[8 * r : 8 * r + 8], 0.0)
    total = jnp.sum(total, axis=0, keepdims=True)
    if inner == INNER - 1:
        total = total + jnp.where(lanes((1, 128)) == LANE_PRIMAL, whole(moved), 0.0)
    row[...] = jnp.broadcast_to(total, row.shape)


def primal_first_kernel(primal, tail, const, *rest):
    primal_step(0, table(primal, CAPS), primal[WEIGHT, 0:1], primal, tail, const, *rest)


def primal_kernel(inner, got, primal, tail, const, *rest):
    caps = caps_after(summed_row(got), primal, const)
    primal_step(inner, caps, primal[WEIGHT, 0:1], primal, tail, const, *rest)


def primal_restart_kernel(got, primal, tail, const, *rest):
    mean, weight = restart(summed_row(got), primal, const)
    primal_step(0, mean, weight, primal, tail, const, *rest)


def finish_kernel(got, primal, const, caps_new, weight_new):
    mean, weight = restart(jnp.sum(got[...], axis=0, keepdims=True), primal, const)
    own = lax.axis_index("period")
    shape = mean.shape
    for t in range(4):
        here = (subs(shape) == 2 * own + t // 2) & (lanes(shape) == 64 * (t % 2))
        caps_new[t] = jnp.sum(jnp.where(here, mean, 0.0))
    weight_new[0] = jnp.max(weight)


def dual_tables(primal, const, y_one, y_two, inward, steps, ahead):
    odd_y = const[ODD_Y, 0:1] > 0.5
    periods = period_table()
    weight = primal[WEIGHT, 0:1]
    steps[0] = weight / (2.0 * (periods + 1.0))
    steps[1] = weight / (periods + 1.0)
    new = []
    for n, inside in ((0, FIRST), (1, LAST)):
        new.append([])
        for x in range(2):
            at = 2 * n + x
            one, two = table(y_one, x * TABLE), table(y_two, x * TABLE)
            there = jnp.where(odd_y, two, one) if n else jnp.where(odd_y, one, two)
            ahead[n, x] = down(there)
            here = table(primal, inside + x * TABLE)
            price = table(inward, edge_at(n, x)) + steps[0] * (there - down(here))
            new[n].append(jnp.maximum(price, 0.0) * const[EDGES, at : at + 1])
    return new


def dual_pair(s, primal, const, x_one, x_two, dual, inward, steps, ahead):
    odd = const[ODD_X] > 0.5
    lower = jnp.where(odd, x_one[s], x_two[s])
    upper = jnp.where(odd, x_two[s], x_one[s])
    outside = mix(lower, upper)
    return [
        dual_row(2 * s + a, outside[a], primal, const, dual, inward, steps, ahead)
        for a in range(2)
    ]


def dual_row(r, outside, primal, const, dual, inward, steps, ahead_rows):
    one = slice(r, r + 1)
    step = steps[0, one]
    here = primal[HEAD + r]
    under = down(here)
    away = down(outside)
    other = turn(under)
    sub = subs((8, 128))
    after = pltpu.roll(under, 7, 0)
    before = pltpu.roll(under, 1, 0)
    ahead = [
        under,
        jnp.where(low(), other, away),
        jnp.where(low(), away, other),
        jnp.where(
            sub == 3, ahead_rows[1, 0, one], jnp.where(sub == 7, ahead_rows[1, 1, one], after)
        ),
        jnp.where(
            sub == 0, ahead_rows[0, 0, one], jnp.where(sub == 4, ahead_rows[0, 1, one], before)
        ),
    ]
    p = [
        jnp.maximum(dual[PRICES + k * ROWS + r] + step * (here - ahead[k]), 0.0) * const[k]
        for k in range(ARCS)
    ]
    b = jnp.maximum(dual[BOUNDS + r] + steps[1, one] * (here - 1.0), 0.0)
    h = jnp.maximum(inward[HALOS + r] + step * (outside - under), 0.0) * const[HALO]
    return p, b, h


def dual_kernel(
    primal, const, x_one, x_two, y_one, y_two, dual, inward, new, inward_new, tail, steps, ahead
):
    edges = dual_tables(primal, const, y_one, y_two, inward, steps, ahead)
    for n in range(2):
        for x in range(2):
            put_table(inward_new, edge_at(n, x), edges[n][x])
    carry = jnp.zeros((8, 128), F32)
    for s in reversed(range(ROWS // 2)):
        both = dual_pair(s, primal, const, x_one, x_two, dual, inward, steps, ahead)
        for a in (1, 0):
            carry = put_dual(new, inward_new, tail, 2 * s + a, *both[a], carry)


def start_kernel(
    got, weight, dual, inward, const, new, x_one, x_two, y_one, y_two, row, primal, tail, rates
):
    unpack_kernel(got, weight, primal, dual, inward, tail, const)
    primal_first_kernel(primal, tail, const, new, x_one, x_two, y_one, y_two, row, rates)


def step_kernel(
    inner, got, primal, const, x_one, x_two, y_one, y_two, dual, inward, dual_new, inward_new, *rest
):
    *outs, rates, steps, ahead, tail = rest
    dual_kernel(
        primal, const, x_one, x_two, y_one, y_two, dual, inward, dual_new, inward_new, tail, steps,
        ahead,
    )
    primal_kernel(inner, got, primal, tail, const, *outs, rates)


def mean_of(one, two, three):
    return (one + two + three) / INNER


def mean_row(r, dual0, dual1, dual, p, b, moved):
    mean = []
    for k in range(ARCS):
        at = PRICES + k * ROWS + r
        mean.append(mean_of(dual1[at], dual[at], p[k]))
        moved = moved + (mean[k] - dual0[at]) ** 2
    b = mean_of(dual1[BOUNDS + r], dual[BOUNDS + r], b)
    return mean, b, moved + (b - dual0[BOUNDS + r]) ** 2


def with_moves(row, moved):
    return row[0:1] + jnp.where(lanes((1, 128)) == LANE_DUAL, whole(moved), 0.0)


def dual_restart_kernel(
    primal, const, x_one, x_two, y_one, y_two, dual, inward, row, inward1, dual0, dual1,
    new, inward_new, tail, row_new, steps, ahead,
):
    edges = dual_tables(primal, const, y_one, y_two, inward, steps, ahead)
    for n in range(2):
        for x in range(2):
            at = edge_at(n, x)
            mean = mean_of(table(inward1, at), table(inward, at), edges[n][x])
            put_table(inward_new, at, mean)
    carry = jnp.zeros((8, 128), F32)
    moved = jnp.zeros((8, 128), F32)
    for s in reversed(range(ROWS // 2)):
        both = dual_pair(s, primal, const, x_one, x_two, dual, inward, steps, ahead)
        for a in (1, 0):
            r = 2 * s + a
            p, b, h = both[a]
            p, b, moved = mean_row(r, dual0, dual1, dual, p, b, moved)
            h = mean_of(inward1[HALOS + r], inward[HALOS + r], h)
            carry = put_dual(new, inward_new, tail, r, p, b, h, carry)
    row_new[...] = jnp.broadcast_to(with_moves(row, moved), row_new.shape)


def spread_row(row):
    shape = (ROWS + 8, 128)
    spread = jnp.where((lanes(shape) & 63) == subs(shape), jnp.broadcast_to(row, shape), 0.0)
    return half_sums(spread)


def dual_final_kernel(
    primal, const, x_one, x_two, y_one, y_two, dual, inward, row, dual0, dual1,
    send, steps, ahead,
):
    dual_tables(primal, const, y_one, y_two, inward, steps, ahead)
    moved = jnp.zeros((8, 128), F32)
    for s in range(ROWS // 2):
        both = dual_pair(s, primal, const, x_one, x_two, dual, inward, steps, ahead)
        means = []
        for a in range(2):
            r = 2 * s + a
            p, b, _ = both[a]
            p, b, moved = mean_row(r, dual0, dual1, dual, p, b, moved)
            means.append(p + [b, primal[SHARES + r]])
        for field in range(ARCS, BACK):
            send[s, field], send[16 + s, field] = mix(means[0][field], means[1][field])
        for k in range(ARCS):
            send[s, k], send[16 + s, k] = mix(means[0][k], means[1][k])
    sums = spread_row(with_moves(row, moved))
    top = (lanes((8, 128)) & 63) == 0
    for k in range(ARCS):
        tile = sums[8 * k : 8 * k + 8]
        for i in range(TILES):
            send[i, k] = jnp.where(top, tile, send[i, k])


def plane_sum_kernel(got, out):
    top = (lanes((8, 128)) & 63) == 0
    tiles = []
    for k in range(ARCS):
        total = got[0, k]
        for i in range(1, TILES):
            total = total + got[i, k]
        tiles.append(jnp.where(top, total, 0.0))
    sums = half_sums(jnp.concatenate(tiles, axis=0))
    shape = sums.shape
    row = jnp.sum(jnp.where((lanes(shape) & 63) == subs(shape), sums, 0.0), axis=0, keepdims=True)
    out[...] = jnp.broadcast_to(row, out.shape)


def turn_back_kernel(got, share, prec, bound):
    def take(field, target):
        rows = [
            mix(got[member(2 * m), field], got[member(2 * m + 1), field]) for m in range(TILES // 2)
        ]
        for a in range(2):
            turned = jnp.concatenate([pair[a] for pair in rows], axis=0).T
            target(2 * a, turned[0:64])
            target(2 * a + 1, turned[64:128])

    for k in range(ARCS):

        def store(t, v, k=k):
            prec[k, t] = jnp.where(subs(v.shape) == 0, 0.0, v)

        take(k, store)

    def store_bound(t, v):
        bound[t] = v

    def store_share(t, v):
        share[t] = v

    take(BOUND, store_bound)
    take(SHARE, store_share)


def f32(*shape):
    return jax.ShapeDtypeStruct(shape, F32)


VMEM = pl.BlockSpec(memory_space=pltpu.VMEM)
SMEM = pl.BlockSpec(memory_space=pltpu.SMEM)
ANY = pl.BlockSpec(memory_space=pl.ANY)


def call(kernel, outs, scratch=(), far=0, out_spaces=None, aliases=None, vmem=12):
    def run(*args):
        return pl.pallas_call(
            kernel,
            out_shape=[f32(*shape) for shape in outs],
            in_specs=[VMEM] * (len(args) - far) + [ANY] * far,
            out_specs=out_spaces or [VMEM] * len(outs),
            scratch_shapes=[
                pltpu.VMEM(shape, F32) if isinstance(shape, tuple) else shape for shape in scratch
            ],
            input_output_aliases=aliases or {},
            compiler_params=pltpu.CompilerParams(vmem_limit_bytes=vmem * 1024 * 1024),
            cost_estimate=pl.CostEstimate(
                flops=10**6, bytes_accessed=4 * 10**6, transcendentals=0
            ),
        )(*args)

    return run


def semaphores(n):
    return pltpu.SemaphoreType.DMA((n,))


STEP_OUTS = [
    (PRIMAL, 8, 128), (ROWS // 2, 8, 128), (ROWS // 2, 8, 128), (2 * TABLE, 8, 128),
    (2 * TABLE, 8, 128), (DEVICES, 128),
]
STEP_SCRATCH = [(2, ROWS, 128)]
DUAL_ARRAY = (DUAL, 8, 128)
INWARD_ARRAY = (INWARD, 8, 128)
TAIL_ARRAY = (ROWS, 8, 128)
DUAL_OUTS = [DUAL_ARRAY, INWARD_ARRAY, TAIL_ARRAY]
DUAL_SCRATCH = [(2, ROWS, 128), (2, 2, ROWS, 128)]
ALL_VMEM = 62
EVERY = ("strip", "period")


def share_row(row):
    return lax.all_to_all(row, EVERY, 0, 0, tiled=True)


def share_planes(row):
    planes = DEVICES // PLANE
    groups = [[PLANE * z + i for z in range(planes)] for i in range(PLANE)]
    return lax.all_to_all(row, EVERY, 0, 0, axis_index_groups=groups, tiled=True)


def exchange(slots):
    groups = [[PLANE * z + i for i in range(PLANE)] for z in range(DEVICES // PLANE)]
    return lax.all_to_all(slots, EVERY, 0, 0, axis_index_groups=groups)


def swap_x(value, odd):
    planes = DEVICES // PLANE
    pairs = []
    for z in range(planes):
        other = z + 1 if z % 2 == odd else z - 1
        if 0 <= other < planes:
            pairs += [(PLANE * z + i, PLANE * other + i) for i in range(PLANE)]
    return lax.ppermute(value, EVERY, pairs)


def swap_y(value, odd):
    pairs = []
    for j in range(TILES):
        other = j + 1 if j % 2 == odd else j - 1
        if 0 <= other < TILES:
            pairs += [
                (PLANE * z + member(j), PLANE * z + member(other)) for z in range(DEVICES // PLANE)
            ]
    return lax.ppermute(value, EVERY, pairs)


def halo(x_one, x_two, y_one, y_two):
    y_one, y_two = swap_y(y_one, 0), swap_y(y_two, 1)
    return swap_x(x_one, 0), swap_x(x_two, 1), y_one, y_two


def per_device(
    u_start,
    dual_prec,
    dual_bound,
    dual_cap,
    capacity,
    block_value,
    ton_class,
    density,
    slope_code,
    omega_start,
):
    plane = (NZ, NY)
    slots = (TILES, SLOTS, 8, 128)
    prec = dual_prec[:, 0]
    ints = pltpu.VMEM((1, NY), jnp.int32)
    (rim,) = call(rim_kernel, [(4,) + plane], [ints, semaphores(2)], far=2, vmem=ALL_VMEM)(
        slope_code, prec
    )
    swaps = [(i, i + 1 if i % 2 else i - 1) for i in range(1, NX - 1)]
    rim = lax.ppermute(rim, "strip", swaps)
    (send,) = call(
        pack_kernel,
        [slots],
        [
            pltpu.SMEM((4,), F32), pltpu.SMEM((4,), F32), pltpu.SMEM((8,), F32), ints,
            pltpu.VMEM(plane, jnp.int32), plane, (4,) + plane, (ARCS, 4) + plane, (4,) + plane,
            semaphores(9),
        ],
        far=9,
        vmem=ALL_VMEM,
    )(
        dual_cap, capacity, density, slope_code, ton_class[0], block_value[0], u_start[0], prec,
        dual_bound[0],
    )
    (send,) = call(
        put_rim_kernel,
        [slots],
        [(4,) + plane, (TILES, 8, 128), semaphores(1)],
        far=2,
        out_spaces=[ANY],
        aliases={1: 0},
        vmem=ALL_VMEM,
    )(rim, send)
    got = exchange(send)
    dual, inward, const, primal, *sides, row = call(
        start_kernel,
        [DUAL_ARRAY, INWARD_ARRAY, (CONSTANTS, 8, 128)] + STEP_OUTS,
        [(PRIMAL, 8, 128), TAIL_ARRAY] + STEP_SCRATCH,
    )(got, jnp.reshape(omega_start, (1, 1)))
    for outer in range(OUTER):
        if outer > 0:
            primal, *sides, row = call(primal_restart_kernel, STEP_OUTS, STEP_SCRATCH)(
                row_sums, primal, tail, const
            )
        duals, inwards = [dual], [inward]
        for inner in range(1, INNER):
            row_sums = share_row(row)
            dual, inward, primal, *sides, row = call(
                functools.partial(step_kernel, inner),
                [DUAL_ARRAY, INWARD_ARRAY] + STEP_OUTS,
                STEP_SCRATCH + DUAL_SCRATCH + [TAIL_ARRAY],
            )(row_sums, primal, const, *halo(*sides), dual, inward)
            duals.append(dual)
            inwards.append(inward)
        sides = halo(*sides)
        if outer < OUTER - 1:
            dual, inward, tail, row = call(
                dual_restart_kernel, DUAL_OUTS + [(DEVICES, 128)], DUAL_SCRATCH
            )(primal, const, *sides, dual, inward, row, inwards[1], duals[0], duals[1])
            row_sums = share_row(row)
        else:
            (send,) = call(dual_final_kernel, [(TILES, BACK, 8, 128)], DUAL_SCRATCH)(
                primal, const, *sides, dual, inward, row, duals[0], duals[1]
            )
            got = exchange(send)
            (row,) = call(plane_sum_kernel, [(8, 128)])(got)
            row_sums = share_planes(row)
    mined, arcs, bounds = call(
        turn_back_kernel, [(4, NZ, NY), (ARCS, 4, NZ, NY), (4, NZ, NY)]
    )(got)
    caps, weight = call(finish_kernel, [(4,), (1,)], out_spaces=[SMEM, SMEM])(
        row_sums, primal, const
    )
    return (
        mined[None],
        arcs[:, None],
        bounds[None],
        caps,
        weight,
    )


def solution(mesh):
    in_specs = (
        P("strip", "period", None, None),
        P(None, "strip", "period", None, None),
        P("strip", "period", None, None),
        P("period"),
        P("period"),
        P("strip", None, None),
        P("strip", None, None),
        P(),
        P("strip", None),
        P(),
    )
    out_specs = (
        P("strip", "period", None, None),
        P(None, "strip", "period", None, None),
        P("strip", "period", None, None),
        P("period"),
        P(),
    )
    return jax.shard_map(
        per_device, mesh=mesh, in_specs=in_specs, out_specs=out_specs, check_vma=False
    )
```

```python
import functools
import math

import jax
import jax.numpy as jnp
from jax import lax
from jax.experimental import pallas as pl
from jax.experimental.pallas import tpu as pltpu
from jax.sharding import PartitionSpec as P

OUTER = 2
INNER = 3
NX = 16
NY = 128
NZ = 64
NP = 64
RATE = math.log(1.1) / 12.0
EPS = 1e-06
SLOPE = 11.0
BLOCKS = float(NX * NY * NZ)
ROOT = math.sqrt(BLOCKS)
F32 = jnp.float32

PLANE = 32
TILES = 32
ROWS = NP // 2
DEVICES = 256
ARCS = 5
BOUND, SHARE, RIM, EXTRA = 5, 6, 7, 8
SLOTS = 9
LANE_PRIMAL, LANE_DUAL, LANE_TONS = 32, 33, 34
HALO, EDGES, TONS, VALUE, ODD_X, ODD_Y, LIMITS = 5, 6, 7, 8, 9, 10, 11
CONSTANTS = 15
TABLE = ROWS // 8
SHARES, SHARE_SUM, SHARE_FIRST, HEAD = 0, ROWS, 2 * ROWS, 3 * ROWS
CAPS = 4 * ROWS
CAP_SUM, CAP_FIRST, WEIGHT = CAPS + TABLE, CAPS + 2 * TABLE, CAPS + 3 * TABLE
FIRST = WEIGHT + 1
LAST = FIRST + 2 * TABLE
PRIMAL = LAST + 2 * TABLE
PRICES, BOUNDS = 0, ARCS * ROWS
DUAL = BOUNDS + ROWS
HALOS, EDGE_ROWS = 0, ROWS
INWARD = EDGE_ROWS + 4 * TABLE
BACK = 7


def member(tile):
    chip, core = divmod(tile, 2)
    row, at = divmod(chip, 4)
    at = at if row % 2 == 0 else 3 - at
    return row % 2 * 16 + at * 4 + row // 2 * 2 + core


def table(ref, at):
    return ref[at : at + TABLE].reshape(ROWS, 128)


def put_table(ref, at, value):
    ref[at : at + TABLE] = value.reshape(TABLE, 8, 128)


def line(ref, at, r):
    return ref[at + r // 8, r % 8 : r % 8 + 1]


def edge_at(n, x):
    return EDGE_ROWS + (2 * n + x) * TABLE


def lanes(shape):
    return lax.broadcasted_iota(jnp.int32, shape, len(shape) - 1)


def subs(shape):
    return lax.broadcasted_iota(jnp.int32, shape, len(shape) - 2)


def later_half(shape):
    return lanes(shape) >= 64


def half_matrix():
    a = subs((128, 128)) >= 64
    b = lanes((128, 128)) >= 64
    return (a == b).astype(F32)


def half_sums(rows):
    return jnp.dot(
        rows, half_matrix(), precision=lax.Precision.HIGHEST, preferred_element_type=F32
    )


def period_table():
    shape = (ROWS, 128)
    return (2 * subs(shape) + later_half(shape).astype(jnp.int32)).astype(F32)


def down(v):
    return pltpu.roll(v, 1, v.ndim - 1)


def up(v):
    return pltpu.roll(v, 127, v.ndim - 1)


def swap(v):
    return pltpu.roll(v, 64, v.ndim - 1)


def low(shape=(8, 128)):
    return subs(shape) < 4


def turn(v):
    return pltpu.roll(v, 4, v.ndim - 2)


def mix(one, two):
    return jnp.where(low(), one, turn(two)), jnp.where(low(), turn(one), two)


def fetch(pairs, sems):
    copies = [
        pltpu.make_async_copy(source, target, sems.at[n]) for n, (source, target) in enumerate(pairs)
    ]
    for copy in copies:
        copy.start()
    return copies


def put_tiles(source, target):
    one = jnp.concatenate([source(0), source(1)], axis=0).T
    two = jnp.concatenate([source(2), source(3)], axis=0).T
    for m in range(TILES // 2):
        here = slice(8 * m, 8 * m + 8)
        even, odd = mix(one[here], two[here])
        target(member(2 * m), even)
        target(member(2 * m + 1), odd)


def rim_kernel(slope_at, prec_at, rim, slope, sems):
    x = lax.axis_index("strip")
    odd = x % 2
    arc = 2 - odd
    copies = fetch([(slope_at, slope), (prec_at.at[arc], rim)], sems)
    inside = jnp.where(odd == 1, x + 1 < NX, x >= 1).astype(jnp.int32)
    for copy in copies:
        copy.wait()
    toward = ((slope[...] >> (arc - 1)) & inside).astype(F32)
    for t in range(rim.shape[0]):
        rim[t, 0:1] = toward


def pack_kernel(
    caps_at, limits_at, density_at, slope_at, ton_class_at, value_at, share_at, prec_at, bound_at,
    out, caps, limits, density, slope, ton_class, value, share, prec, bound, sems,
):
    copies = fetch(
        [
            (slope_at, slope), (ton_class_at, ton_class), (value_at, value), (prec_at, prec),
            (bound_at, bound), (share_at, share), (caps_at, caps), (limits_at, limits),
            (density_at, density),
        ],
        sems,
    )
    for copy in copies:
        copy.wait()
    x = lax.axis_index("strip")
    row = (1, 128)
    code = slope[...]
    column = lanes(row)
    mask = [
        None,
        ((code & 1 == 1) & (jnp.full(row, x) + 1 < NX)).astype(F32),
        ((code >> 1 & 1 == 1) & (jnp.full(row, x) >= 1)).astype(F32),
        ((code >> 2 & 1 == 1) & (column + 1 < NY)).astype(F32),
        ((code >> 3 & 1 == 1) & (column >= 1)).astype(F32),
    ]
    top = subs((NZ, NY)) == 0

    def put(field, source):
        def target(slot, tile):
            out[slot, field] = tile

        put_tiles(source, target)

    for k in range(ARCS):
        def source(t, k=k):
            spare = jnp.where(column % 2 == 0, caps[t], limits[t]) if k == 0 else mask[k]
            return jnp.where(top, spare, prec[k, t])

        put(k, source)
    put(BOUND, lambda t: bound[t])
    put(SHARE, lambda t: share[t])
    classes = ton_class[...]
    tons = jnp.zeros(classes.shape, F32)
    for c in range(8):
        tons = jnp.where(classes == c, (1.0 + c) * density[c], tons)
    blocks = jnp.concatenate([tons, value[...]], axis=0).T
    zero = jnp.zeros(row, F32)
    for j in range(TILES):
        i = member(j)
        out[i, EXTRA, 4:8] = blocks[4 * j : 4 * j + 4]
        for a in range(2):
            if j > 0:
                out[i, EXTRA, a : a + 1] = out[member(j - 1), 3, 4 * a + 3 : 4 * a + 4]
            else:
                out[i, EXTRA, a : a + 1] = zero
            if j < TILES - 1:
                out[i, EXTRA, 2 + a : 3 + a] = out[member(j + 1), 4, 4 * a : 4 * a + 1]
            else:
                out[i, EXTRA, 2 + a : 3 + a] = zero


def put_rim_kernel(rim_at, send, out, rim, tiles, sems):
    (copy,) = fetch([(rim_at, rim)], sems)
    copy.wait()

    def target(slot, tile):
        tiles[slot] = tile

    put_tiles(lambda t: rim[t], target)
    (copy,) = fetch([(tiles, out.at[:, RIM])], sems)
    copy.wait()


def adjoint_row(prices, bound, halo, inward, r, carry):
    shape = (8, 128)
    sub = subs(shape)
    edge = [[line(inward, edge_at(n, x), r) for x in range(2)] for n in range(2)]
    total = prices[0] + prices[1] + prices[2] + prices[3] + prices[4] + bound
    across = turn(jnp.where(low(), prices[1], prices[2]))
    before = pltpu.roll(prices[3], 1, 0)
    before = jnp.where(sub == 0, edge[0][0], jnp.where(sub == 4, edge[0][1], before))
    after = pltpu.roll(prices[4], 7, 0)
    after = jnp.where(sub == 3, edge[1][0], jnp.where(sub == 7, edge[1][1], after))
    lower = prices[0] + halo + across + before + after
    g = total - up(lower)
    pair = g + swap(g)
    return carry + jnp.where(later_half(shape), g, pair), carry + pair


def put_dual(dual, inward, tail, r, prices, bound, halo, carry):
    for k in range(ARCS):
        dual[PRICES + k * ROWS + r] = prices[k]
    dual[BOUNDS + r] = bound
    inward[HALOS + r] = halo
    tail[r], carry = adjoint_row(prices, bound, halo, inward, r, carry)
    return carry


def unpack_kernel(got, weight, primal, dual, inward, tail, const):
    shape = (8, 128)
    primal[WEIGHT] = jnp.broadcast_to(weight[...], shape)
    const[ODD_X] = jnp.full(shape, lax.axis_index("strip") // 2 % 2).astype(F32)
    const[ODD_Y] = jnp.full(shape, lax.axis_index("period") % 2).astype(F32)
    lane = lanes(shape)
    deep = ((lane & 63) >= 1).astype(F32)
    half = later_half(shape)

    def pair(s, field):
        return mix(got[s, field], got[16 + s, field])

    const[0] = deep
    for k in range(1, ARCS):
        const[k] = jnp.broadcast_to(pair(0, k)[0][:, 0:1], shape) * deep
    const[HALO] = jnp.broadcast_to(pair(0, RIM)[0][:, 0:1], shape) * deep
    for n in range(2):
        for x in range(2):
            at = 2 * n + x
            edge = got[16 * x, EXTRA, 2 * n : 2 * n + 1]
            const[EDGES, at : at + 1] = jnp.broadcast_to(edge[:, 0:1], (1, 128)) * deep[0:1]
            const[EDGES, 4 + at : 5 + at] = jnp.zeros((1, 128), F32)
    blocks = jnp.where(low(), turn(got[0, EXTRA]), got[16, EXTRA])
    other = swap(blocks)
    const[TONS] = jnp.where(half, other, blocks)
    const[VALUE] = jnp.where(half, blocks, other)
    for s in range(ROWS // 2):
        tile, within = s // 4, slice(2 * s % 8, 2 * s % 8 + 2)
        for n in range(2):
            for x in range(2):
                at = 2 * n + x
                edge = got[16 * x + s, EXTRA, 2 * n : 2 * n + 2]
                inward[edge_at(n, x) + tile, within] = edge * const[EDGES, at : at + 1]
    carry = jnp.zeros(shape, F32)
    for s in reversed(range(ROWS // 2)):
        p = [pair(s, k) for k in range(ARCS)]
        b, u, h = pair(s, BOUND), pair(s, SHARE), pair(s, RIM)
        for a in (1, 0):
            r = 2 * s + a
            spare = jnp.where(
                half,
                jnp.broadcast_to(p[0][a][:, 64:65], shape),
                jnp.broadcast_to(p[0][a][:, 0:1], shape),
            )
            at = slice(r % 8, r % 8 + 1)
            primal[CAPS + r // 8, at] = spare[0:1]
            const[LIMITS + r // 8, at] = spare[1:2]
            primal[SHARES + r] = u[a]
            here = [p[k][a] * const[k] for k in range(ARCS)]
            carry = put_dual(dual, inward, tail, r, here, b[a], h[a] * const[HALO], carry)


def summed_row(got):
    total = got[0:8]
    for n in range(1, DEVICES // 8):
        total = total + got[8 * n : 8 * n + 8]
    return jnp.sum(total, axis=0, keepdims=True)


def lane_value(row, lane):
    return jnp.sum(jnp.where(lanes((1, 128)) == lane, row, 0.0), axis=1, keepdims=True)


def whole(v):
    return jnp.sum(jnp.sum(v, axis=0, keepdims=True), axis=1, keepdims=True)


def caps_after(row, primal, const):
    shape = (ROWS, 128)
    spread = jnp.where((lanes(shape) & 63) == subs(shape), jnp.broadcast_to(row, shape), 0.0)
    totals = half_sums(spread)
    tons_all = lane_value(row, LANE_TONS)
    over = (totals - BLOCKS * table(const, LIMITS)) / tons_all
    return jnp.maximum(table(primal, CAPS) + primal[WEIGHT, 0:1] * over, 0.0)


def restart(row, primal, const):
    mean = (table(primal, CAP_SUM) + caps_after(row, primal, const)) / INNER
    move_cap = whole((mean - table(primal, CAP_FIRST)) ** 2) * (1.0 / 64.0)
    primal_move = lane_value(row, LANE_PRIMAL)
    dual_move = lane_value(row, LANE_DUAL) + move_cap
    weight = primal[WEIGHT, 0:1]
    return mean, jnp.sqrt(weight * jnp.sqrt((dual_move + EPS) / (primal_move + EPS)))


def primal_step(inner, caps, weight, primal, tail, const, new, x_one, x_two, y_one, y_two, row, rates):
    shape = (8, 128)
    tons = const[TONS]
    value = const[VALUE]
    lean = tons / ROOT
    periods = period_table()
    rates[0] = jnp.exp(-RATE * periods)
    rates[1] = SLOPE * (NP - periods)
    put_table(new, CAPS, caps)
    put_table(new, CAP_FIRST, caps if inner == 0 else table(primal, CAP_FIRST))
    if inner == 0:
        put_table(new, CAP_SUM, jnp.zeros((ROWS, 128), F32))
    else:
        put_table(new, CAP_SUM, table(primal, CAP_SUM) + caps)
    new[WEIGHT] = jnp.broadcast_to(weight, shape)
    half = later_half(shape)
    odd_x = const[ODD_X] > 0.5
    odd_y = const[ODD_Y] > 0.5
    carry = jnp.zeros(shape, F32)
    moved = jnp.zeros(shape, F32)
    mined = []
    for r in range(ROWS):
        gradient = tail[r] + tons * line(new, CAPS, r) / ROOT
        tau = 1.0 / (weight * (rates[1, r : r + 1] + lean))
        old = primal[SHARES + r]
        now = jnp.maximum(old - tau * (gradient - value * rates[0, r : r + 1]), 0.0)
        if inner == 0:
            new[SHARES + r] = now
            new[SHARE_SUM + r] = now
            new[SHARE_FIRST + r] = old
        elif inner < INNER - 1:
            new[SHARES + r] = now
            new[SHARE_SUM + r] = primal[SHARE_SUM + r] + now
            new[SHARE_FIRST + r] = primal[SHARE_FIRST + r]
        else:
            mean = (primal[SHARE_SUM + r] + now) / INNER
            new[SHARES + r] = mean
            moved = moved + (mean - primal[SHARE_FIRST + r]) ** 2
        ahead = 2.0 * now - old
        pair = ahead + swap(ahead)
        cumulative = carry + jnp.where(half, pair, ahead)
        carry = carry + pair
        new[HEAD + r] = cumulative
        at = slice(r % 8, r % 8 + 1)
        for x in range(2):
            tile = x * TABLE + r // 8
            new[FIRST + tile, at] = cumulative[4 * x : 4 * x + 1]
            new[LAST + tile, at] = cumulative[4 * x + 3 : 4 * x + 4]
        if r % 2 == 0:
            even = cumulative
        else:
            lows, highs = mix(even, cumulative)
            x_one[r // 2] = jnp.where(odd_x, lows, highs)
            x_two[r // 2] = jnp.where(odd_x, highs, lows)
        mined.append(tons * ahead)
    for n in range(2 * TABLE):
        y_one[n] = jnp.where(odd_y, new[FIRST + n], new[LAST + n])
        y_two[n] = jnp.where(odd_y, new[LAST + n], new[FIRST + n])
    mined.append(tons)
    sums = half_sums(jnp.concatenate(mined, axis=0))
    lane = lanes(shape)
    total = jnp.where(lane == LANE_TONS, sums[8 * ROWS :], 0.0)
    for r in range(ROWS):
        total = total + jnp.where((lane & 63) == r, sums[8 * r : 8 * r + 8], 0.0)
    total = jnp.sum(total, axis=0, keepdims=True)
    if inner == INNER - 1:
        total = total + jnp.where(lanes((1, 128)) == LANE_PRIMAL, whole(moved), 0.0)
    row[...] = jnp.broadcast_to(total, row.shape)


def primal_first_kernel(primal, tail, const, *rest):
    primal_step(0, table(primal, CAPS), primal[WEIGHT, 0:1], primal, tail, const, *rest)


def primal_kernel(inner, got, primal, tail, const, *rest):
    caps = caps_after(summed_row(got), primal, const)
    primal_step(inner, caps, primal[WEIGHT, 0:1], primal, tail, const, *rest)


def primal_restart_kernel(got, primal, tail, const, *rest):
    mean, weight = restart(summed_row(got), primal, const)
    primal_step(0, mean, weight, primal, tail, const, *rest)


def finish_kernel(got, primal, const, caps_new, weight_new):
    mean, weight = restart(jnp.sum(got[...], axis=0, keepdims=True), primal, const)
    own = lax.axis_index("period")
    shape = mean.shape
    for t in range(4):
        here = (subs(shape) == 2 * own + t // 2) & (lanes(shape) == 64 * (t % 2))
        caps_new[t] = jnp.sum(jnp.where(here, mean, 0.0))
    weight_new[0] = jnp.max(weight)


def dual_tables(primal, const, y_one, y_two, inward, steps, ahead):
    odd_y = const[ODD_Y, 0:1] > 0.5
    periods = period_table()
    weight = primal[WEIGHT, 0:1]
    steps[0] = weight / (2.0 * (periods + 1.0))
    steps[1] = weight / (periods + 1.0)
    new = []
    for n, inside in ((0, FIRST), (1, LAST)):
        new.append([])
        for x in range(2):
            at = 2 * n + x
            one, two = table(y_one, x * TABLE), table(y_two, x * TABLE)
            there = jnp.where(odd_y, two, one) if n else jnp.where(odd_y, one, two)
            ahead[n, x] = down(there)
            here = table(primal, inside + x * TABLE)
            price = table(inward, edge_at(n, x)) + steps[0] * (there - down(here))
            new[n].append(jnp.maximum(price, 0.0) * const[EDGES, at : at + 1])
    return new


def dual_pair(s, primal, const, x_one, x_two, dual, inward, steps, ahead):
    odd = const[ODD_X] > 0.5
    lower = jnp.where(odd, x_one[s], x_two[s])
    upper = jnp.where(odd, x_two[s], x_one[s])
    outside = mix(lower, upper)
    return [
        dual_row(2 * s + a, outside[a], primal, const, dual, inward, steps, ahead)
        for a in range(2)
    ]


def dual_row(r, outside, primal, const, dual, inward, steps, ahead_rows):
    one = slice(r, r + 1)
    step = steps[0, one]
    here = primal[HEAD + r]
    under = down(here)
    away = down(outside)
    other = turn(under)
    sub = subs((8, 128))
    after = pltpu.roll(under, 7, 0)
    before = pltpu.roll(under, 1, 0)
    ahead = [
        under,
        jnp.where(low(), other, away),
        jnp.where(low(), away, other),
        jnp.where(
            sub == 3, ahead_rows[1, 0, one], jnp.where(sub == 7, ahead_rows[1, 1, one], after)
        ),
        jnp.where(
            sub == 0, ahead_rows[0, 0, one], jnp.where(sub == 4, ahead_rows[0, 1, one], before)
        ),
    ]
    p = [
        jnp.maximum(dual[PRICES + k * ROWS + r] + step * (here - ahead[k]), 0.0) * const[k]
        for k in range(ARCS)
    ]
    b = jnp.maximum(dual[BOUNDS + r] + steps[1, one] * (here - 1.0), 0.0)
    h = jnp.maximum(inward[HALOS + r] + step * (outside - under), 0.0) * const[HALO]
    return p, b, h


def dual_kernel(
    primal, const, x_one, x_two, y_one, y_two, dual, inward, new, inward_new, tail, steps, ahead
):
    edges = dual_tables(primal, const, y_one, y_two, inward, steps, ahead)
    for n in range(2):
        for x in range(2):
            put_table(inward_new, edge_at(n, x), edges[n][x])
    carry = jnp.zeros((8, 128), F32)
    for s in reversed(range(ROWS // 2)):
        both = dual_pair(s, primal, const, x_one, x_two, dual, inward, steps, ahead)
        for a in (1, 0):
            carry = put_dual(new, inward_new, tail, 2 * s + a, *both[a], carry)


def start_kernel(
    got, weight, dual, inward, const, new, x_one, x_two, y_one, y_two, row, primal, tail, rates
):
    unpack_kernel(got, weight, primal, dual, inward, tail, const)
    primal_first_kernel(primal, tail, const, new, x_one, x_two, y_one, y_two, row, rates)


def step_kernel(
    inner, got, primal, const, x_one, x_two, y_one, y_two, dual, inward, dual_new, inward_new, *rest
):
    *outs, rates, steps, ahead, tail = rest
    dual_kernel(
        primal, const, x_one, x_two, y_one, y_two, dual, inward, dual_new, inward_new, tail, steps,
        ahead,
    )
    primal_kernel(inner, got, primal, tail, const, *outs, rates)


def mean_of(one, two, three):
    return (one + two + three) / INNER


def mean_row(r, dual0, dual1, dual, p, b, moved):
    mean = []
    for k in range(ARCS):
        at = PRICES + k * ROWS + r
        mean.append(mean_of(dual1[at], dual[at], p[k]))
        moved = moved + (mean[k] - dual0[at]) ** 2
    b = mean_of(dual1[BOUNDS + r], dual[BOUNDS + r], b)
    return mean, b, moved + (b - dual0[BOUNDS + r]) ** 2


def with_moves(row, moved):
    return row[0:1] + jnp.where(lanes((1, 128)) == LANE_DUAL, whole(moved), 0.0)


def dual_restart_kernel(
    primal, const, x_one, x_two, y_one, y_two, dual, inward, row, inward1, dual0, dual1,
    new, inward_new, tail, row_new, steps, ahead,
):
    edges = dual_tables(primal, const, y_one, y_two, inward, steps, ahead)
    for n in range(2):
        for x in range(2):
            at = edge_at(n, x)
            mean = mean_of(table(inward1, at), table(inward, at), edges[n][x])
            put_table(inward_new, at, mean)
    carry = jnp.zeros((8, 128), F32)
    moved = jnp.zeros((8, 128), F32)
    for s in reversed(range(ROWS // 2)):
        both = dual_pair(s, primal, const, x_one, x_two, dual, inward, steps, ahead)
        for a in (1, 0):
            r = 2 * s + a
            p, b, h = both[a]
            p, b, moved = mean_row(r, dual0, dual1, dual, p, b, moved)
            h = mean_of(inward1[HALOS + r], inward[HALOS + r], h)
            carry = put_dual(new, inward_new, tail, r, p, b, h, carry)
    row_new[...] = jnp.broadcast_to(with_moves(row, moved), row_new.shape)


def spread_row(row):
    shape = (ROWS + 8, 128)
    spread = jnp.where((lanes(shape) & 63) == subs(shape), jnp.broadcast_to(row, shape), 0.0)
    return half_sums(spread)


def dual_final_kernel(
    primal, const, x_one, x_two, y_one, y_two, dual, inward, row, dual0, dual1,
    send, steps, ahead,
):
    dual_tables(primal, const, y_one, y_two, inward, steps, ahead)
    moved = jnp.zeros((8, 128), F32)
    for s in range(ROWS // 2):
        both = dual_pair(s, primal, const, x_one, x_two, dual, inward, steps, ahead)
        means = []
        for a in range(2):
            r = 2 * s + a
            p, b, _ = both[a]
            p, b, moved = mean_row(r, dual0, dual1, dual, p, b, moved)
            means.append(p + [b, primal[SHARES + r]])
        for field in range(ARCS, BACK):
            send[s, field], send[16 + s, field] = mix(means[0][field], means[1][field])
        for k in range(ARCS):
            send[s, k], send[16 + s, k] = mix(means[0][k], means[1][k])
    sums = spread_row(with_moves(row, moved))
    top = (lanes((8, 128)) & 63) == 0
    for k in range(ARCS):
        tile = sums[8 * k : 8 * k + 8]
        for i in range(TILES):
            send[i, k] = jnp.where(top, tile, send[i, k])


def plane_sum_kernel(got, out):
    top = (lanes((8, 128)) & 63) == 0
    tiles = []
    for k in range(ARCS):
        total = got[0, k]
        for i in range(1, TILES):
            total = total + got[i, k]
        tiles.append(jnp.where(top, total, 0.0))
    sums = half_sums(jnp.concatenate(tiles, axis=0))
    shape = sums.shape
    row = jnp.sum(jnp.where((lanes(shape) & 63) == subs(shape), sums, 0.0), axis=0, keepdims=True)
    out[...] = jnp.broadcast_to(row, out.shape)


def turn_back_kernel(got, share, prec, bound):
    def take(field, target):
        rows = [
            mix(got[member(2 * m), field], got[member(2 * m + 1), field]) for m in range(TILES // 2)
        ]
        for a in range(2):
            turned = jnp.concatenate([pair[a] for pair in rows], axis=0).T
            target(2 * a, turned[0:64])
            target(2 * a + 1, turned[64:128])

    for k in range(ARCS):

        def store(t, v, k=k):
            prec[k, t] = jnp.where(subs(v.shape) == 0, 0.0, v)

        take(k, store)

    def store_bound(t, v):
        bound[t] = v

    def store_share(t, v):
        share[t] = v

    take(BOUND, store_bound)
    take(SHARE, store_share)


def f32(*shape):
    return jax.ShapeDtypeStruct(shape, F32)


VMEM = pl.BlockSpec(memory_space=pltpu.VMEM)
SMEM = pl.BlockSpec(memory_space=pltpu.SMEM)
ANY = pl.BlockSpec(memory_space=pl.ANY)


def call(kernel, outs, scratch=(), far=0, out_spaces=None, aliases=None, vmem=12):
    def run(*args):
        return pl.pallas_call(
            kernel,
            out_shape=[f32(*shape) for shape in outs],
            in_specs=[VMEM] * (len(args) - far) + [ANY] * far,
            out_specs=out_spaces or [VMEM] * len(outs),
            scratch_shapes=[
                pltpu.VMEM(shape, F32) if isinstance(shape, tuple) else shape for shape in scratch
            ],
            input_output_aliases=aliases or {},
            compiler_params=pltpu.CompilerParams(vmem_limit_bytes=vmem * 1024 * 1024),
            cost_estimate=pl.CostEstimate(
                flops=10**6, bytes_accessed=4 * 10**6, transcendentals=0
            ),
        )(*args)

    return run


def semaphores(n):
    return pltpu.SemaphoreType.DMA((n,))


STEP_OUTS = [
    (PRIMAL, 8, 128), (ROWS // 2, 8, 128), (ROWS // 2, 8, 128), (2 * TABLE, 8, 128),
    (2 * TABLE, 8, 128), (DEVICES, 128),
]
STEP_SCRATCH = [(2, ROWS, 128)]
DUAL_ARRAY = (DUAL, 8, 128)
INWARD_ARRAY = (INWARD, 8, 128)
TAIL_ARRAY = (ROWS, 8, 128)
DUAL_OUTS = [DUAL_ARRAY, INWARD_ARRAY, TAIL_ARRAY]
DUAL_SCRATCH = [(2, ROWS, 128), (2, 2, ROWS, 128)]
ALL_VMEM = 62
EVERY = ("strip", "period")


def share_row(row):
    return lax.all_to_all(row, EVERY, 0, 0, tiled=True)


def share_planes(row):
    planes = DEVICES // PLANE
    groups = [[PLANE * z + i for z in range(planes)] for i in range(PLANE)]
    return lax.all_to_all(row, EVERY, 0, 0, axis_index_groups=groups, tiled=True)


def exchange(slots):
    groups = [[PLANE * z + i for i in range(PLANE)] for z in range(DEVICES // PLANE)]
    return lax.all_to_all(slots, EVERY, 0, 0, axis_index_groups=groups)


def swap_x(value, odd):
    planes = DEVICES // PLANE
    pairs = []
    for z in range(planes):
        other = z + 1 if z % 2 == odd else z - 1
        if 0 <= other < planes:
            pairs += [(PLANE * z + i, PLANE * other + i) for i in range(PLANE)]
    return lax.ppermute(value, EVERY, pairs)


def swap_y(value, odd):
    pairs = []
    for j in range(TILES):
        other = j + 1 if j % 2 == odd else j - 1
        if 0 <= other < TILES:
            pairs += [
                (PLANE * z + member(j), PLANE * z + member(other)) for z in range(DEVICES // PLANE)
            ]
    return lax.ppermute(value, EVERY, pairs)


def halo(x_one, x_two, y_one, y_two):
    y_one, y_two = swap_y(y_one, 0), swap_y(y_two, 1)
    return swap_x(x_one, 0), swap_x(x_two, 1), y_one, y_two


def per_device(
    u_start,
    dual_prec,
    dual_bound,
    dual_cap,
    capacity,
    block_value,
    ton_class,
    density,
    slope_code,
    omega_start,
):
    plane = (NZ, NY)
    slots = (TILES, SLOTS, 8, 128)
    prec = dual_prec[:, 0]
    ints = pltpu.VMEM((1, NY), jnp.int32)
    (rim,) = call(rim_kernel, [(4,) + plane], [ints, semaphores(2)], far=2, vmem=ALL_VMEM)(
        slope_code, prec
    )
    swaps = [(i, i + 1 if i % 2 else i - 1) for i in range(1, NX - 1)]
    rim = lax.ppermute(rim, "strip", swaps)
    (send,) = call(
        pack_kernel,
        [slots],
        [
            pltpu.SMEM((4,), F32), pltpu.SMEM((4,), F32), pltpu.SMEM((8,), F32), ints,
            pltpu.VMEM(plane, jnp.int32), plane, (4,) + plane, (ARCS, 4) + plane, (4,) + plane,
            semaphores(9),
        ],
        far=9,
        vmem=ALL_VMEM,
    )(
        dual_cap, capacity, density, slope_code, ton_class[0], block_value[0], u_start[0], prec,
        dual_bound[0],
    )
    (send,) = call(
        put_rim_kernel,
        [slots],
        [(4,) + plane, (TILES, 8, 128), semaphores(1)],
        far=2,
        out_spaces=[ANY],
        aliases={1: 0},
        vmem=ALL_VMEM,
    )(rim, send)
    got = exchange(send)
    dual, inward, const, primal, *sides, row = call(
        start_kernel,
        [DUAL_ARRAY, INWARD_ARRAY, (CONSTANTS, 8, 128)] + STEP_OUTS,
        [(PRIMAL, 8, 128), TAIL_ARRAY] + STEP_SCRATCH,
    )(got, jnp.reshape(omega_start, (1, 1)))
    for outer in range(OUTER):
        if outer > 0:
            primal, *sides, row = call(
                primal_restart_kernel, STEP_OUTS, STEP_SCRATCH, aliases={0: 5, 1: 0}
            )(row_sums, primal, tail, const)
        duals, inwards = [dual], [inward]
        for inner in range(1, INNER):
            row_sums = share_row(row)
            dual, inward, primal, *sides, row = call(
                functools.partial(step_kernel, inner),
                [DUAL_ARRAY, INWARD_ARRAY] + STEP_OUTS,
                STEP_SCRATCH + DUAL_SCRATCH + [TAIL_ARRAY],
                aliases={0: 7, 1: 2, 3: 3, 4: 4, 5: 5, 6: 6} | ({8: 1} if inner == 1 else {}),
            )(row_sums, primal, const, *halo(*sides), dual, inward)
            duals.append(dual)
            inwards.append(inward)
        sides = halo(*sides)
        if outer < OUTER - 1:
            dual, inward, tail, row = call(
                dual_restart_kernel,
                DUAL_OUTS + [(DEVICES, 128)],
                DUAL_SCRATCH,
                aliases={8: 3, 9: 1, 11: 0},
            )(primal, const, *sides, dual, inward, row, inwards[1], duals[0], duals[1])
            row_sums = share_row(row)
        else:
            (send,) = call(dual_final_kernel, [(TILES, BACK, 8, 128)], DUAL_SCRATCH)(
                primal, const, *sides, dual, inward, row, duals[0], duals[1]
            )
            got = exchange(send)
            (row,) = call(plane_sum_kernel, [(8, 128)])(got)
            row_sums = share_planes(row)
    mined, arcs, bounds = call(
        turn_back_kernel, [(4, NZ, NY), (ARCS, 4, NZ, NY), (4, NZ, NY)]
    )(got)
    caps, weight = call(finish_kernel, [(4,), (1,)], out_spaces=[SMEM, SMEM])(
        row_sums, primal, const
    )
    return (
        mined[None],
        arcs[:, None],
        bounds[None],
        caps,
        weight,
    )


def solution(mesh):
    in_specs = (
        P("strip", "period", None, None),
        P(None, "strip", "period", None, None),
        P("strip", "period", None, None),
        P("period"),
        P("period"),
        P("strip", None, None),
        P("strip", None, None),
        P(),
        P("strip", None),
        P(),
    )
    out_specs = (
        P("strip", "period", None, None),
        P(None, "strip", "period", None, None),
        P("strip", "period", None, None),
        P("period"),
        P(),
    )
    return jax.shard_map(
        per_device, mesh=mesh, in_specs=in_specs, out_specs=out_specs, check_vma=False
    )
```

```python
import functools
import math

import jax
import jax.numpy as jnp
from jax import lax
from jax.experimental import pallas as pl
from jax.experimental.pallas import tpu as pltpu
from jax.sharding import PartitionSpec as P

OUTER = 2
INNER = 3
NX = 16
NY = 128
NZ = 64
NP = 64
RATE = math.log(1.1) / 12.0
EPS = 1e-06
SLOPE = 11.0
BLOCKS = float(NX * NY * NZ)
ROOT = math.sqrt(BLOCKS)
F32 = jnp.float32

PLANE = 32
TILES = 32
ROWS = NP // 2
DEVICES = 256
ARCS = 5
BOUND, SHARE, RIM, EXTRA = 5, 6, 7, 8
SLOTS = 9
LANE_PRIMAL, LANE_DUAL, LANE_TONS = 32, 33, 34
HALO, EDGES, TONS, VALUE, ODD_X, ODD_Y, LIMITS = 5, 6, 7, 8, 9, 10, 11
CONSTANTS = 15
TABLE = ROWS // 8
SHARES, SHARE_SUM, SHARE_FIRST, HEAD = 0, ROWS, 2 * ROWS, 3 * ROWS
CAPS = 4 * ROWS
CAP_SUM, CAP_FIRST, WEIGHT = CAPS + TABLE, CAPS + 2 * TABLE, CAPS + 3 * TABLE
FIRST = WEIGHT + 1
LAST = FIRST + 2 * TABLE
PRIMAL = LAST + 2 * TABLE
PRICES, BOUNDS = 0, ARCS * ROWS
DUAL = BOUNDS + ROWS
HALOS, EDGE_ROWS = 0, ROWS
INWARD = EDGE_ROWS + 4 * TABLE
BACK = 7


def member(tile):
    chip, core = divmod(tile, 2)
    row, at = divmod(chip, 4)
    at = at if row % 2 == 0 else 3 - at
    return row % 2 * 16 + at * 4 + row // 2 * 2 + core


def table(ref, at):
    return ref[at : at + TABLE].reshape(ROWS, 128)


def put_table(ref, at, value):
    ref[at : at + TABLE] = value.reshape(TABLE, 8, 128)


def line(ref, at, r):
    return ref[at + r // 8, r % 8 : r % 8 + 1]


def edge_at(n, x):
    return EDGE_ROWS + (2 * n + x) * TABLE


def lanes(shape):
    return lax.broadcasted_iota(jnp.int32, shape, len(shape) - 1)


def subs(shape):
    return lax.broadcasted_iota(jnp.int32, shape, len(shape) - 2)


def later_half(shape):
    return lanes(shape) >= 64


def half_matrix():
    a = subs((128, 128)) >= 64
    b = lanes((128, 128)) >= 64
    return (a == b).astype(F32)


def half_sums(rows):
    return jnp.dot(
        rows, half_matrix(), precision=lax.Precision.HIGHEST, preferred_element_type=F32
    )


def period_table():
    shape = (ROWS, 128)
    return (2 * subs(shape) + later_half(shape).astype(jnp.int32)).astype(F32)


def down(v):
    return pltpu.roll(v, 1, v.ndim - 1)


def up(v):
    return pltpu.roll(v, 127, v.ndim - 1)


def swap(v):
    return pltpu.roll(v, 64, v.ndim - 1)


def low(shape=(8, 128)):
    return subs(shape) < 4


def turn(v):
    return pltpu.roll(v, 4, v.ndim - 2)


def mix(one, two):
    return jnp.where(low(), one, turn(two)), jnp.where(low(), turn(one), two)


def fetch(pairs, sems):
    copies = [
        pltpu.make_async_copy(source, target, sems.at[n]) for n, (source, target) in enumerate(pairs)
    ]
    for copy in copies:
        copy.start()
    return copies


def put_tiles(source, target):
    one = jnp.concatenate([source(0), source(1)], axis=0).T
    two = jnp.concatenate([source(2), source(3)], axis=0).T
    for m in range(TILES // 2):
        here = slice(8 * m, 8 * m + 8)
        even, odd = mix(one[here], two[here])
        target(member(2 * m), even)
        target(member(2 * m + 1), odd)


def rim_kernel(slope_at, prec_at, rim, slope, sems):
    x = lax.axis_index("strip")
    odd = x % 2
    arc = 2 - odd
    copies = fetch([(slope_at, slope), (prec_at.at[arc], rim)], sems)
    inside = jnp.where(odd == 1, x + 1 < NX, x >= 1).astype(jnp.int32)
    for copy in copies:
        copy.wait()
    toward = ((slope[...] >> (arc - 1)) & inside).astype(F32)
    for t in range(rim.shape[0]):
        rim[t, 0:1] = toward


def pack_kernel(
    caps_at, limits_at, density_at, slope_at, ton_class_at, value_at, share_at, prec_at, bound_at,
    out, caps, limits, density, slope, ton_class, value, share, prec, bound, sems,
):
    copies = fetch(
        [
            (slope_at, slope), (ton_class_at, ton_class), (value_at, value), (prec_at, prec),
            (bound_at, bound), (share_at, share), (caps_at, caps), (limits_at, limits),
            (density_at, density),
        ],
        sems,
    )
    for copy in copies:
        copy.wait()
    x = lax.axis_index("strip")
    row = (1, 128)
    code = slope[...]
    column = lanes(row)
    mask = [
        None,
        ((code & 1 == 1) & (jnp.full(row, x) + 1 < NX)).astype(F32),
        ((code >> 1 & 1 == 1) & (jnp.full(row, x) >= 1)).astype(F32),
        ((code >> 2 & 1 == 1) & (column + 1 < NY)).astype(F32),
        ((code >> 3 & 1 == 1) & (column >= 1)).astype(F32),
    ]
    top = subs((NZ, NY)) == 0

    def put(field, source):
        def target(slot, tile):
            out[slot, field] = tile

        put_tiles(source, target)

    for k in range(ARCS):
        def source(t, k=k):
            spare = jnp.where(column % 2 == 0, caps[t], limits[t]) if k == 0 else mask[k]
            return jnp.where(top, spare, prec[k, t])

        put(k, source)
    put(BOUND, lambda t: bound[t])
    put(SHARE, lambda t: share[t])
    classes = ton_class[...]
    tons = jnp.zeros(classes.shape, F32)
    for c in range(8):
        tons = jnp.where(classes == c, (1.0 + c) * density[c], tons)
    blocks = jnp.concatenate([tons, value[...]], axis=0).T
    zero = jnp.zeros(row, F32)
    for j in range(TILES):
        i = member(j)
        out[i, EXTRA, 4:8] = blocks[4 * j : 4 * j + 4]
        for a in range(2):
            if j > 0:
                out[i, EXTRA, a : a + 1] = out[member(j - 1), 3, 4 * a + 3 : 4 * a + 4]
            else:
                out[i, EXTRA, a : a + 1] = zero
            if j < TILES - 1:
                out[i, EXTRA, 2 + a : 3 + a] = out[member(j + 1), 4, 4 * a : 4 * a + 1]
            else:
                out[i, EXTRA, 2 + a : 3 + a] = zero


def put_rim_kernel(rim_at, send, out, rim, tiles, sems):
    (copy,) = fetch([(rim_at, rim)], sems)
    copy.wait()

    def target(slot, tile):
        tiles[slot] = tile

    put_tiles(lambda t: rim[t], target)
    (copy,) = fetch([(tiles, out.at[:, RIM])], sems)
    copy.wait()


def adjoint_row(prices, bound, halo, inward, r, carry):
    shape = (8, 128)
    sub = subs(shape)
    edge = [[line(inward, edge_at(n, x), r) for x in range(2)] for n in range(2)]
    total = prices[0] + prices[1] + prices[2] + prices[3] + prices[4] + bound
    across = turn(jnp.where(low(), prices[1], prices[2]))
    before = pltpu.roll(prices[3], 1, 0)
    before = jnp.where(sub == 0, edge[0][0], jnp.where(sub == 4, edge[0][1], before))
    after = pltpu.roll(prices[4], 7, 0)
    after = jnp.where(sub == 3, edge[1][0], jnp.where(sub == 7, edge[1][1], after))
    lower = prices[0] + halo + across + before + after
    g = total - up(lower)
    pair = g + swap(g)
    return carry + jnp.where(later_half(shape), g, pair), carry + pair


def put_dual(dual, inward, tail, r, prices, bound, halo, carry):
    for k in range(ARCS):
        dual[PRICES + k * ROWS + r] = prices[k]
    dual[BOUNDS + r] = bound
    inward[HALOS + r] = halo
    tail[r], carry = adjoint_row(prices, bound, halo, inward, r, carry)
    return carry


def unpack_kernel(got, weight, primal, dual, inward, tail, const):
    shape = (8, 128)
    primal[WEIGHT] = jnp.broadcast_to(weight[...], shape)
    const[ODD_X] = jnp.full(shape, lax.axis_index("strip") // 2 % 2).astype(F32)
    const[ODD_Y] = jnp.full(shape, lax.axis_index("period") % 2).astype(F32)
    lane = lanes(shape)
    deep = ((lane & 63) >= 1).astype(F32)
    half = later_half(shape)

    def pair(s, field):
        return mix(got[s, field], got[16 + s, field])

    const[0] = deep
    for k in range(1, ARCS):
        const[k] = jnp.broadcast_to(pair(0, k)[0][:, 0:1], shape) * deep
    const[HALO] = jnp.broadcast_to(pair(0, RIM)[0][:, 0:1], shape) * deep
    for n in range(2):
        for x in range(2):
            at = 2 * n + x
            edge = got[16 * x, EXTRA, 2 * n : 2 * n + 1]
            const[EDGES, at : at + 1] = jnp.broadcast_to(edge[:, 0:1], (1, 128)) * deep[0:1]
            const[EDGES, 4 + at : 5 + at] = jnp.zeros((1, 128), F32)
    blocks = jnp.where(low(), turn(got[0, EXTRA]), got[16, EXTRA])
    other = swap(blocks)
    const[TONS] = jnp.where(half, other, blocks)
    const[VALUE] = jnp.where(half, blocks, other)
    for s in range(ROWS // 2):
        tile, within = s // 4, slice(2 * s % 8, 2 * s % 8 + 2)
        for n in range(2):
            for x in range(2):
                at = 2 * n + x
                edge = got[16 * x + s, EXTRA, 2 * n : 2 * n + 2]
                inward[edge_at(n, x) + tile, within] = edge * const[EDGES, at : at + 1]
    carry = jnp.zeros(shape, F32)
    for s in reversed(range(ROWS // 2)):
        p = [pair(s, k) for k in range(ARCS)]
        b, u, h = pair(s, BOUND), pair(s, SHARE), pair(s, RIM)
        for a in (1, 0):
            r = 2 * s + a
            spare = jnp.where(
                half,
                jnp.broadcast_to(p[0][a][:, 64:65], shape),
                jnp.broadcast_to(p[0][a][:, 0:1], shape),
            )
            at = slice(r % 8, r % 8 + 1)
            primal[CAPS + r // 8, at] = spare[0:1]
            const[LIMITS + r // 8, at] = spare[1:2]
            primal[SHARES + r] = u[a]
            here = [p[k][a] * const[k] for k in range(ARCS)]
            carry = put_dual(dual, inward, tail, r, here, b[a], h[a] * const[HALO], carry)


def summed_row(got):
    total = got[0:8]
    for n in range(1, DEVICES // 8):
        total = total + got[8 * n : 8 * n + 8]
    return jnp.sum(total, axis=0, keepdims=True)


def lane_value(row, lane):
    return jnp.sum(jnp.where(lanes((1, 128)) == lane, row, 0.0), axis=1, keepdims=True)


def whole(v):
    return jnp.sum(jnp.sum(v, axis=0, keepdims=True), axis=1, keepdims=True)


def caps_after(row, primal, const):
    shape = (ROWS, 128)
    spread = jnp.where((lanes(shape) & 63) == subs(shape), jnp.broadcast_to(row, shape), 0.0)
    totals = half_sums(spread)
    tons_all = lane_value(row, LANE_TONS)
    over = (totals - BLOCKS * table(const, LIMITS)) / tons_all
    return jnp.maximum(table(primal, CAPS) + primal[WEIGHT, 0:1] * over, 0.0)


def restart(row, primal, const):
    mean = (table(primal, CAP_SUM) + caps_after(row, primal, const)) / INNER
    move_cap = whole((mean - table(primal, CAP_FIRST)) ** 2) * (1.0 / 64.0)
    primal_move = lane_value(row, LANE_PRIMAL)
    dual_move = lane_value(row, LANE_DUAL) + move_cap
    weight = primal[WEIGHT, 0:1]
    return mean, jnp.sqrt(weight * jnp.sqrt((dual_move + EPS) / (primal_move + EPS)))


def primal_step(inner, caps, weight, primal, tail, const, new, x_one, x_two, y_one, y_two, row, rates):
    shape = (8, 128)
    tons = const[TONS]
    value = const[VALUE]
    lean = tons / ROOT
    periods = period_table()
    rates[0] = jnp.exp(-RATE * periods)
    rates[1] = SLOPE * (NP - periods)
    put_table(new, CAPS, caps)
    put_table(new, CAP_FIRST, caps if inner == 0 else table(primal, CAP_FIRST))
    if inner == 0:
        put_table(new, CAP_SUM, jnp.zeros((ROWS, 128), F32))
    else:
        put_table(new, CAP_SUM, table(primal, CAP_SUM) + caps)
    new[WEIGHT] = jnp.broadcast_to(weight, shape)
    half = later_half(shape)
    odd_x = const[ODD_X] > 0.5
    odd_y = const[ODD_Y] > 0.5
    carry = jnp.zeros(shape, F32)
    moved = jnp.zeros(shape, F32)
    mined = []
    for r in range(ROWS):
        gradient = tail[r] + tons * line(new, CAPS, r) / ROOT
        tau = 1.0 / (weight * (rates[1, r : r + 1] + lean))
        old = primal[SHARES + r]
        now = jnp.maximum(old - tau * (gradient - value * rates[0, r : r + 1]), 0.0)
        if inner == 0:
            new[SHARES + r] = now
            new[SHARE_SUM + r] = now
            new[SHARE_FIRST + r] = old
        elif inner < INNER - 1:
            new[SHARES + r] = now
            new[SHARE_SUM + r] = primal[SHARE_SUM + r] + now
            new[SHARE_FIRST + r] = primal[SHARE_FIRST + r]
        else:
            mean = (primal[SHARE_SUM + r] + now) / INNER
            new[SHARES + r] = mean
            moved = moved + (mean - primal[SHARE_FIRST + r]) ** 2
        ahead = 2.0 * now - old
        pair = ahead + swap(ahead)
        cumulative = carry + jnp.where(half, pair, ahead)
        carry = carry + pair
        new[HEAD + r] = cumulative
        at = slice(r % 8, r % 8 + 1)
        for x in range(2):
            tile = x * TABLE + r // 8
            new[FIRST + tile, at] = cumulative[4 * x : 4 * x + 1]
            new[LAST + tile, at] = cumulative[4 * x + 3 : 4 * x + 4]
        if r % 2 == 0:
            even = cumulative
        else:
            lows, highs = mix(even, cumulative)
            x_one[r // 2] = jnp.where(odd_x, lows, highs)
            x_two[r // 2] = jnp.where(odd_x, highs, lows)
        mined.append(tons * ahead)
    for n in range(2 * TABLE):
        y_one[n] = jnp.where(odd_y, new[FIRST + n], new[LAST + n])
        y_two[n] = jnp.where(odd_y, new[LAST + n], new[FIRST + n])
    mined.append(tons)
    sums = half_sums(jnp.concatenate(mined, axis=0))
    lane = lanes(shape)
    total = jnp.where(lane == LANE_TONS, sums[8 * ROWS :], 0.0)
    for r in range(ROWS):
        total = total + jnp.where((lane & 63) == r, sums[8 * r : 8 * r + 8], 0.0)
    total = jnp.sum(total, axis=0, keepdims=True)
    if inner == INNER - 1:
        total = total + jnp.where(lanes((1, 128)) == LANE_PRIMAL, whole(moved), 0.0)
    row[...] = jnp.broadcast_to(total, row.shape)


def primal_first_kernel(primal, tail, const, *rest):
    primal_step(0, table(primal, CAPS), primal[WEIGHT, 0:1], primal, tail, const, *rest)


def primal_kernel(inner, got, primal, tail, const, *rest):
    caps = caps_after(summed_row(got), primal, const)
    primal_step(inner, caps, primal[WEIGHT, 0:1], primal, tail, const, *rest)


def primal_restart_kernel(got, primal, tail, const, *rest):
    mean, weight = restart(summed_row(got), primal, const)
    primal_step(0, mean, weight, primal, tail, const, *rest)


def finish_kernel(got, primal, const, caps_new, weight_new):
    mean, weight = restart(jnp.sum(got[...], axis=0, keepdims=True), primal, const)
    own = lax.axis_index("period")
    shape = mean.shape
    for t in range(4):
        here = (subs(shape) == 2 * own + t // 2) & (lanes(shape) == 64 * (t % 2))
        caps_new[t] = jnp.sum(jnp.where(here, mean, 0.0))
    weight_new[0] = jnp.max(weight)


def dual_tables(primal, const, y_one, y_two, inward, steps, ahead):
    odd_y = const[ODD_Y, 0:1] > 0.5
    periods = period_table()
    weight = primal[WEIGHT, 0:1]
    steps[0] = weight / (2.0 * (periods + 1.0))
    steps[1] = weight / (periods + 1.0)
    new = []
    for n, inside in ((0, FIRST), (1, LAST)):
        new.append([])
        for x in range(2):
            at = 2 * n + x
            one, two = table(y_one, x * TABLE), table(y_two, x * TABLE)
            there = jnp.where(odd_y, two, one) if n else jnp.where(odd_y, one, two)
            ahead[n, x] = down(there)
            here = table(primal, inside + x * TABLE)
            price = table(inward, edge_at(n, x)) + steps[0] * (there - down(here))
            new[n].append(jnp.maximum(price, 0.0) * const[EDGES, at : at + 1])
    return new


def dual_pair(s, primal, const, x_one, x_two, dual, inward, steps, ahead):
    odd = const[ODD_X] > 0.5
    lower = jnp.where(odd, x_one[s], x_two[s])
    upper = jnp.where(odd, x_two[s], x_one[s])
    outside = mix(lower, upper)
    return [
        dual_row(2 * s + a, outside[a], primal, const, dual, inward, steps, ahead)
        for a in range(2)
    ]


def dual_row(r, outside, primal, const, dual, inward, steps, ahead_rows):
    one = slice(r, r + 1)
    step = steps[0, one]
    here = primal[HEAD + r]
    under = down(here)
    away = down(outside)
    other = turn(under)
    sub = subs((8, 128))
    after = pltpu.roll(under, 7, 0)
    before = pltpu.roll(under, 1, 0)
    ahead = [
        under,
        jnp.where(low(), other, away),
        jnp.where(low(), away, other),
        jnp.where(
            sub == 3, ahead_rows[1, 0, one], jnp.where(sub == 7, ahead_rows[1, 1, one], after)
        ),
        jnp.where(
            sub == 0, ahead_rows[0, 0, one], jnp.where(sub == 4, ahead_rows[0, 1, one], before)
        ),
    ]
    p = [
        jnp.maximum(dual[PRICES + k * ROWS + r] + step * (here - ahead[k]), 0.0) * const[k]
        for k in range(ARCS)
    ]
    b = jnp.maximum(dual[BOUNDS + r] + steps[1, one] * (here - 1.0), 0.0)
    h = jnp.maximum(inward[HALOS + r] + step * (outside - under), 0.0) * const[HALO]
    return p, b, h


def dual_kernel(
    primal, const, x_one, x_two, y_one, y_two, dual, inward, new, inward_new, tail, steps, ahead
):
    edges = dual_tables(primal, const, y_one, y_two, inward, steps, ahead)
    for n in range(2):
        for x in range(2):
            put_table(inward_new, edge_at(n, x), edges[n][x])
    carry = jnp.zeros((8, 128), F32)
    for s in reversed(range(ROWS // 2)):
        both = dual_pair(s, primal, const, x_one, x_two, dual, inward, steps, ahead)
        for a in (1, 0):
            carry = put_dual(new, inward_new, tail, 2 * s + a, *both[a], carry)


def start_kernel(
    got, weight, dual, inward, const, new, x_one, x_two, y_one, y_two, row, primal, tail, rates
):
    unpack_kernel(got, weight, primal, dual, inward, tail, const)
    primal_first_kernel(primal, tail, const, new, x_one, x_two, y_one, y_two, row, rates)


def step_kernel(
    inner, got, primal, const, x_one, x_two, y_one, y_two, dual, inward, dual_new, inward_new, *rest
):
    *outs, rates, steps, ahead, tail = rest
    dual_kernel(
        primal, const, x_one, x_two, y_one, y_two, dual, inward, dual_new, inward_new, tail, steps,
        ahead,
    )
    primal_kernel(inner, got, primal, tail, const, *outs, rates)


def mean_of(one, two, three):
    return (one + two + three) / INNER


def mean_row(r, dual0, dual1, dual, p, b, moved):
    mean = []
    for k in range(ARCS):
        at = PRICES + k * ROWS + r
        mean.append(mean_of(dual1[at], dual[at], p[k]))
        moved = moved + (mean[k] - dual0[at]) ** 2
    b = mean_of(dual1[BOUNDS + r], dual[BOUNDS + r], b)
    return mean, b, moved + (b - dual0[BOUNDS + r]) ** 2


def with_moves(row, moved):
    return row[0:1] + jnp.where(lanes((1, 128)) == LANE_DUAL, whole(moved), 0.0)


def dual_restart_kernel(
    primal, const, x_one, x_two, y_one, y_two, dual, inward, row, inward1, dual0, dual1,
    new, inward_new, tail, row_new, steps, ahead,
):
    edges = dual_tables(primal, const, y_one, y_two, inward, steps, ahead)
    for n in range(2):
        for x in range(2):
            at = edge_at(n, x)
            mean = mean_of(table(inward1, at), table(inward, at), edges[n][x])
            put_table(inward_new, at, mean)
    carry = jnp.zeros((8, 128), F32)
    moved = jnp.zeros((8, 128), F32)
    for s in reversed(range(ROWS // 2)):
        both = dual_pair(s, primal, const, x_one, x_two, dual, inward, steps, ahead)
        for a in (1, 0):
            r = 2 * s + a
            p, b, h = both[a]
            p, b, moved = mean_row(r, dual0, dual1, dual, p, b, moved)
            h = mean_of(inward1[HALOS + r], inward[HALOS + r], h)
            carry = put_dual(new, inward_new, tail, r, p, b, h, carry)
    row_new[...] = jnp.broadcast_to(with_moves(row, moved), row_new.shape)


def spread_row(row):
    shape = (ROWS + 8, 128)
    spread = jnp.where((lanes(shape) & 63) == subs(shape), jnp.broadcast_to(row, shape), 0.0)
    return half_sums(spread)


def dual_final_kernel(
    primal, const, x_one, x_two, y_one, y_two, dual, inward, row, dual0, dual1,
    send, steps, ahead,
):
    dual_tables(primal, const, y_one, y_two, inward, steps, ahead)
    moved = jnp.zeros((8, 128), F32)
    for s in range(ROWS // 2):
        both = dual_pair(s, primal, const, x_one, x_two, dual, inward, steps, ahead)
        means = []
        for a in range(2):
            r = 2 * s + a
            p, b, _ = both[a]
            p, b, moved = mean_row(r, dual0, dual1, dual, p, b, moved)
            means.append(p + [b, primal[SHARES + r]])
        for field in range(ARCS, BACK):
            send[s, field], send[16 + s, field] = mix(means[0][field], means[1][field])
        for k in range(ARCS):
            send[s, k], send[16 + s, k] = mix(means[0][k], means[1][k])
    sums = spread_row(with_moves(row, moved))
    top = (lanes((8, 128)) & 63) == 0
    for k in range(ARCS):
        tile = sums[8 * k : 8 * k + 8]
        for i in range(TILES):
            send[i, k] = jnp.where(top, tile, send[i, k])


def plane_sum_kernel(got, out):
    top = (lanes((8, 128)) & 63) == 0
    tiles = []
    for k in range(ARCS):
        total = got[0, k]
        for i in range(1, TILES):
            total = total + got[i, k]
        tiles.append(jnp.where(top, total, 0.0))
    sums = half_sums(jnp.concatenate(tiles, axis=0))
    shape = sums.shape
    row = jnp.sum(jnp.where((lanes(shape) & 63) == subs(shape), sums, 0.0), axis=0, keepdims=True)
    out[...] = jnp.broadcast_to(row, out.shape)


def turn_back_kernel(got, share, prec, bound):
    def take(field, target):
        rows = [
            mix(got[member(2 * m), field], got[member(2 * m + 1), field]) for m in range(TILES // 2)
        ]
        for a in range(2):
            turned = jnp.concatenate([pair[a] for pair in rows], axis=0).T
            target(2 * a, turned[0:64])
            target(2 * a + 1, turned[64:128])

    for k in range(ARCS):

        def store(t, v, k=k):
            prec[k, t] = jnp.where(subs(v.shape) == 0, 0.0, v)

        take(k, store)

    def store_bound(t, v):
        bound[t] = v

    def store_share(t, v):
        share[t] = v

    take(BOUND, store_bound)
    take(SHARE, store_share)


def f32(*shape):
    return jax.ShapeDtypeStruct(shape, F32)


VMEM = pl.BlockSpec(memory_space=pltpu.VMEM)
SMEM = pl.BlockSpec(memory_space=pltpu.SMEM)
ANY = pl.BlockSpec(memory_space=pl.ANY)


def call(kernel, outs, scratch=(), far=0, out_spaces=None, aliases=None, vmem=12):
    def run(*args):
        return pl.pallas_call(
            kernel,
            out_shape=[f32(*shape) for shape in outs],
            in_specs=[VMEM] * (len(args) - far) + [ANY] * far,
            out_specs=out_spaces or [VMEM] * len(outs),
            scratch_shapes=[
                pltpu.VMEM(shape, F32) if isinstance(shape, tuple) else shape for shape in scratch
            ],
            input_output_aliases=aliases or {},
            compiler_params=pltpu.CompilerParams(vmem_limit_bytes=vmem * 1024 * 1024),
            cost_estimate=pl.CostEstimate(
                flops=10**6, bytes_accessed=4 * 10**6, transcendentals=0
            ),
        )(*args)

    return run


def semaphores(n):
    return pltpu.SemaphoreType.DMA((n,))


STEP_OUTS = [
    (PRIMAL, 8, 128), (ROWS // 2, 8, 128), (ROWS // 2, 8, 128), (2 * TABLE, 8, 128),
    (2 * TABLE, 8, 128), (DEVICES, 128),
]
STEP_SCRATCH = [(2, ROWS, 128)]
DUAL_ARRAY = (DUAL, 8, 128)
INWARD_ARRAY = (INWARD, 8, 128)
TAIL_ARRAY = (ROWS, 8, 128)
DUAL_OUTS = [DUAL_ARRAY, INWARD_ARRAY, TAIL_ARRAY]
DUAL_SCRATCH = [(2, ROWS, 128), (2, 2, ROWS, 128)]
ALL_VMEM = 62
EVERY = ("strip", "period")


def share_row(row):
    return lax.all_to_all(row, EVERY, 0, 0, tiled=True)


def share_planes(row):
    planes = DEVICES // PLANE
    groups = [[PLANE * z + i for z in range(planes)] for i in range(PLANE)]
    return lax.all_to_all(row, EVERY, 0, 0, axis_index_groups=groups, tiled=True)


def exchange(slots):
    groups = [[PLANE * z + i for i in range(PLANE)] for z in range(DEVICES // PLANE)]
    return lax.all_to_all(slots, EVERY, 0, 0, axis_index_groups=groups)


def swap_x(value, odd):
    planes = DEVICES // PLANE
    pairs = []
    for z in range(planes):
        other = z + 1 if z % 2 == odd else z - 1
        if 0 <= other < planes:
            pairs += [(PLANE * z + i, PLANE * other + i) for i in range(PLANE)]
    return lax.ppermute(value, EVERY, pairs)


def swap_y(value, odd):
    pairs = []
    for j in range(TILES):
        other = j + 1 if j % 2 == odd else j - 1
        if 0 <= other < TILES:
            pairs += [
                (PLANE * z + member(j), PLANE * z + member(other)) for z in range(DEVICES // PLANE)
            ]
    return lax.ppermute(value, EVERY, pairs)


def halo(x_one, x_two, y_one, y_two):
    y_one, y_two = swap_y(y_one, 0), swap_y(y_two, 1)
    return swap_x(x_one, 0), swap_x(x_two, 1), y_one, y_two


def per_device(
    u_start,
    dual_prec,
    dual_bound,
    dual_cap,
    capacity,
    block_value,
    ton_class,
    density,
    slope_code,
    omega_start,
):
    plane = (NZ, NY)
    slots = (TILES, SLOTS, 8, 128)
    prec = dual_prec[:, 0]
    ints = pltpu.VMEM((1, NY), jnp.int32)
    (rim,) = call(rim_kernel, [(4,) + plane], [ints, semaphores(2)], far=2, vmem=ALL_VMEM)(
        slope_code, prec
    )
    swaps = [(i, i + 1 if i % 2 else i - 1) for i in range(1, NX - 1)]
    rim = lax.ppermute(rim, "strip", swaps)
    (send,) = call(
        pack_kernel,
        [slots],
        [
            pltpu.SMEM((4,), F32), pltpu.SMEM((4,), F32), pltpu.SMEM((8,), F32), ints,
            pltpu.VMEM(plane, jnp.int32), plane, (4,) + plane, (ARCS, 4) + plane, (4,) + plane,
            semaphores(9),
        ],
        far=9,
        vmem=ALL_VMEM,
    )(
        dual_cap, capacity, density, slope_code, ton_class[0], block_value[0], u_start[0], prec,
        dual_bound[0],
    )
    (send,) = call(
        put_rim_kernel,
        [slots],
        [(4,) + plane, (TILES, 8, 128), semaphores(1)],
        far=2,
        out_spaces=[ANY],
        aliases={1: 0},
        vmem=ALL_VMEM,
    )(rim, send)
    got = exchange(send)
    dual, inward, const, primal, *sides, row = call(
        start_kernel,
        [DUAL_ARRAY, INWARD_ARRAY, (CONSTANTS, 8, 128)] + STEP_OUTS,
        [(PRIMAL, 8, 128), TAIL_ARRAY] + STEP_SCRATCH,
    )(got, jnp.reshape(omega_start, (1, 1)))
    for outer in range(OUTER):
        if outer > 0:
            primal, *sides, row = call(
                primal_restart_kernel, STEP_OUTS, STEP_SCRATCH, aliases={1: 0}
            )(row_sums, primal, tail, const)
        duals, inwards = [dual], [inward]
        for inner in range(1, INNER):
            row_sums = share_row(row)
            dual, inward, primal, *sides, row = call(
                functools.partial(step_kernel, inner),
                [DUAL_ARRAY, INWARD_ARRAY] + STEP_OUTS,
                STEP_SCRATCH + DUAL_SCRATCH + [TAIL_ARRAY],
                aliases={1: 2, 3: 3, 4: 4, 5: 5, 6: 6} | ({8: 1} if inner == 1 else {}),
            )(row_sums, primal, const, *halo(*sides), dual, inward)
            duals.append(dual)
            inwards.append(inward)
        sides = halo(*sides)
        if outer < OUTER - 1:
            dual, inward, tail, row = call(
                dual_restart_kernel,
                DUAL_OUTS + [(DEVICES, 128)],
                DUAL_SCRATCH,
                aliases={9: 1},
            )(primal, const, *sides, dual, inward, row, inwards[1], duals[0], duals[1])
            row_sums = share_row(row)
        else:
            (send,) = call(dual_final_kernel, [(TILES, BACK, 8, 128)], DUAL_SCRATCH)(
                primal, const, *sides, dual, inward, row, duals[0], duals[1]
            )
            got = exchange(send)
            (row,) = call(plane_sum_kernel, [(8, 128)])(got)
            row_sums = share_planes(row)
    mined, arcs, bounds = call(
        turn_back_kernel, [(4, NZ, NY), (ARCS, 4, NZ, NY), (4, NZ, NY)]
    )(got)
    caps, weight = call(finish_kernel, [(4,), (1,)], out_spaces=[SMEM, SMEM])(
        row_sums, primal, const
    )
    return (
        mined[None],
        arcs[:, None],
        bounds[None],
        caps,
        weight,
    )


def solution(mesh):
    in_specs = (
        P("strip", "period", None, None),
        P(None, "strip", "period", None, None),
        P("strip", "period", None, None),
        P("period"),
        P("period"),
        P("strip", None, None),
        P("strip", None, None),
        P(),
        P("strip", None),
        P(),
    )
    out_specs = (
        P("strip", "period", None, None),
        P(None, "strip", "period", None, None),
        P("strip", "period", None, None),
        P("period"),
        P(),
    )
    return jax.shard_map(
        per_device, mesh=mesh, in_specs=in_specs, out_specs=out_specs, check_vma=False
    )
```

```python
import functools
import math

import jax
import jax.numpy as jnp
from jax import lax
from jax.experimental import pallas as pl
from jax.experimental.pallas import tpu as pltpu
from jax.sharding import PartitionSpec as P

OUTER = 2
INNER = 3
NX = 16
NY = 128
NZ = 64
NP = 64
RATE = math.log(1.1) / 12.0
EPS = 1e-06
SLOPE = 11.0
BLOCKS = float(NX * NY * NZ)
ROOT = math.sqrt(BLOCKS)
F32 = jnp.float32

PLANE = 32
TILES = 32
ROWS = NP // 2
DEVICES = 256
ARCS = 5
BOUND, SHARE, RIM, EXTRA = 5, 6, 7, 8
SLOTS = 9
LANE_PRIMAL, LANE_DUAL, LANE_TONS = 32, 33, 34
HALO, EDGES, TONS, VALUE, ODD_X, EVEN_Y, LIMITS = 5, 6, 7, 8, 9, 10, 11
CONSTANTS = 15
TABLE = ROWS // 8
SHARES, SHARE_SUM, SHARE_FIRST, HEAD = 0, ROWS, 2 * ROWS, 3 * ROWS
CAPS = 4 * ROWS
CAP_SUM, CAP_FIRST, WEIGHT = CAPS + TABLE, CAPS + 2 * TABLE, CAPS + 3 * TABLE
FIRST = WEIGHT + 1
LAST = FIRST + 2 * TABLE
PRIMAL = LAST + 2 * TABLE
PRICES, BOUNDS = 0, ARCS * ROWS
DUAL = BOUNDS + ROWS
HALOS, EDGE_ROWS = 0, ROWS
INWARD = EDGE_ROWS + 4 * TABLE
BACK = 7


def member(tile):
    chip, core = divmod(tile, 2)
    row, at = divmod(chip, 4)
    at = at if row % 2 == 0 else 3 - at
    return row % 2 * 16 + at * 4 + row // 2 * 2 + core


def table(ref, at):
    return ref[at : at + TABLE].reshape(ROWS, 128)


def put_table(ref, at, value):
    ref[at : at + TABLE] = value.reshape(TABLE, 8, 128)


def line(ref, at, r):
    return ref[at + r // 8, r % 8 : r % 8 + 1]


def edge_at(n, x):
    return EDGE_ROWS + (2 * n + x) * TABLE


def lanes(shape):
    return lax.broadcasted_iota(jnp.int32, shape, len(shape) - 1)


def subs(shape):
    return lax.broadcasted_iota(jnp.int32, shape, len(shape) - 2)


def later_half(shape):
    return lanes(shape) >= 64


def half_matrix():
    a = subs((128, 128)) >= 64
    b = lanes((128, 128)) >= 64
    return (a == b).astype(F32)


def half_sums(rows):
    return jnp.dot(
        rows, half_matrix(), precision=lax.Precision.HIGHEST, preferred_element_type=F32
    )


def period_table():
    shape = (ROWS, 128)
    return (2 * subs(shape) + later_half(shape).astype(jnp.int32)).astype(F32)


def down(v):
    return pltpu.roll(v, 1, v.ndim - 1)


def up(v):
    return pltpu.roll(v, 127, v.ndim - 1)


def swap(v):
    return pltpu.roll(v, 64, v.ndim - 1)


def low(shape=(8, 128)):
    return subs(shape) < 4


def turn(v):
    return pltpu.roll(v, 4, v.ndim - 2)


def mix(one, two):
    return jnp.where(low(), one, turn(two)), jnp.where(low(), turn(one), two)


def fetch(pairs, sems):
    copies = [
        pltpu.make_async_copy(source, target, sems.at[n]) for n, (source, target) in enumerate(pairs)
    ]
    for copy in copies:
        copy.start()
    return copies


def put_tiles(source, target):
    one = jnp.concatenate([source(0), source(1)], axis=0).T
    two = jnp.concatenate([source(2), source(3)], axis=0).T
    for m in range(TILES // 2):
        here = slice(8 * m, 8 * m + 8)
        even, odd = mix(one[here], two[here])
        target(member(2 * m), even)
        target(member(2 * m + 1), odd)


def rim_kernel(slope_at, prec_at, rim, slope, sems):
    x = lax.axis_index("strip")
    odd = x % 2
    arc = 2 - odd
    copies = fetch([(slope_at, slope), (prec_at.at[arc], rim)], sems)
    inside = jnp.where(odd == 1, x + 1 < NX, x >= 1).astype(jnp.int32)
    for copy in copies:
        copy.wait()
    toward = ((slope[...] >> (arc - 1)) & inside).astype(F32)
    for t in range(rim.shape[0]):
        rim[t, 0:1] = toward


def pack_kernel(
    caps_at, limits_at, density_at, slope_at, ton_class_at, value_at, share_at, prec_at, bound_at,
    out, caps, limits, density, slope, ton_class, value, share, prec, bound, sems,
):
    copies = fetch(
        [
            (slope_at, slope), (ton_class_at, ton_class), (value_at, value), (prec_at, prec),
            (bound_at, bound), (share_at, share), (caps_at, caps), (limits_at, limits),
            (density_at, density),
        ],
        sems,
    )
    for copy in copies:
        copy.wait()
    x = lax.axis_index("strip")
    row = (1, 128)
    code = slope[...]
    column = lanes(row)
    mask = [
        None,
        ((code & 1 == 1) & (jnp.full(row, x) + 1 < NX)).astype(F32),
        ((code >> 1 & 1 == 1) & (jnp.full(row, x) >= 1)).astype(F32),
        ((code >> 2 & 1 == 1) & (column + 1 < NY)).astype(F32),
        ((code >> 3 & 1 == 1) & (column >= 1)).astype(F32),
    ]
    top = subs((NZ, NY)) == 0

    def put(field, source):
        def target(slot, tile):
            out[slot, field] = tile

        put_tiles(source, target)

    for k in range(ARCS):
        def source(t, k=k):
            spare = jnp.where(column % 2 == 0, caps[t], limits[t]) if k == 0 else mask[k]
            return jnp.where(top, spare, prec[k, t])

        put(k, source)
    put(BOUND, lambda t: bound[t])
    put(SHARE, lambda t: share[t])
    classes = ton_class[...]
    tons = jnp.zeros(classes.shape, F32)
    for c in range(8):
        tons = jnp.where(classes == c, (1.0 + c) * density[c], tons)
    blocks = jnp.concatenate([tons, value[...]], axis=0).T
    zero = jnp.zeros(row, F32)
    for j in range(TILES):
        i = member(j)
        out[i, EXTRA, 4:8] = blocks[4 * j : 4 * j + 4]
        for a in range(2):
            if j > 0:
                out[i, EXTRA, a : a + 1] = out[member(j - 1), 3, 4 * a + 3 : 4 * a + 4]
            else:
                out[i, EXTRA, a : a + 1] = zero
            if j < TILES - 1:
                out[i, EXTRA, 2 + a : 3 + a] = out[member(j + 1), 4, 4 * a : 4 * a + 1]
            else:
                out[i, EXTRA, 2 + a : 3 + a] = zero


def put_rim_kernel(rim_at, send, out, rim, tiles, sems):
    (copy,) = fetch([(rim_at, rim)], sems)
    copy.wait()

    def target(slot, tile):
        tiles[slot] = tile

    put_tiles(lambda t: rim[t], target)
    (copy,) = fetch([(tiles, out.at[:, RIM])], sems)
    copy.wait()


def adjoint_row(prices, bound, halo, inward, r, carry):
    shape = (8, 128)
    sub = subs(shape)
    edge = [[line(inward, edge_at(n, x), r) for x in range(2)] for n in range(2)]
    total = prices[0] + prices[1] + prices[2] + prices[3] + prices[4] + bound
    across = turn(jnp.where(low(), prices[1], prices[2]))
    before = pltpu.roll(prices[3], 1, 0)
    before = jnp.where(sub == 0, edge[0][0], jnp.where(sub == 4, edge[0][1], before))
    after = pltpu.roll(prices[4], 7, 0)
    after = jnp.where(sub == 3, edge[1][0], jnp.where(sub == 7, edge[1][1], after))
    lower = prices[0] + halo + across + before + after
    g = total - up(lower)
    pair = g + swap(g)
    return carry + jnp.where(later_half(shape), g, pair), carry + pair


def put_dual(dual, inward, tail, r, prices, bound, halo, carry):
    for k in range(ARCS):
        dual[PRICES + k * ROWS + r] = prices[k]
    dual[BOUNDS + r] = bound
    inward[HALOS + r] = halo
    tail[r], carry = adjoint_row(prices, bound, halo, inward, r, carry)
    return carry


def unpack_kernel(got, weight, primal, dual, inward, tail, const):
    shape = (8, 128)
    primal[WEIGHT] = jnp.broadcast_to(weight[...], shape)
    const[ODD_X] = jnp.full(shape, lax.axis_index("strip") // 2 % 2).astype(F32)
    const[EVEN_Y] = jnp.full(shape, 1 - lax.axis_index("period") % 2).astype(F32)
    lane = lanes(shape)
    deep = ((lane & 63) >= 1).astype(F32)
    half = later_half(shape)

    def pair(s, field):
        return mix(got[s, field], got[16 + s, field])

    const[0] = deep
    for k in range(1, ARCS):
        const[k] = jnp.broadcast_to(pair(0, k)[0][:, 0:1], shape) * deep
    const[HALO] = jnp.broadcast_to(pair(0, RIM)[0][:, 0:1], shape) * deep
    for n in range(2):
        for x in range(2):
            at = 2 * n + x
            edge = got[16 * x, EXTRA, 2 * n : 2 * n + 1]
            const[EDGES, at : at + 1] = jnp.broadcast_to(edge[:, 0:1], (1, 128)) * deep[0:1]
            const[EDGES, 4 + at : 5 + at] = jnp.zeros((1, 128), F32)
    blocks = jnp.where(low(), turn(got[0, EXTRA]), got[16, EXTRA])
    other = swap(blocks)
    const[TONS] = jnp.where(half, other, blocks)
    const[VALUE] = jnp.where(half, blocks, other)
    for s in range(ROWS // 2):
        tile, within = s // 4, slice(2 * s % 8, 2 * s % 8 + 2)
        for n in range(2):
            for x in range(2):
                at = 2 * n + x
                edge = got[16 * x + s, EXTRA, 2 * n : 2 * n + 2]
                inward[edge_at(n, x) + tile, within] = edge * const[EDGES, at : at + 1]
    carry = jnp.zeros(shape, F32)
    for s in reversed(range(ROWS // 2)):
        p = [pair(s, k) for k in range(ARCS)]
        b, u, h = pair(s, BOUND), pair(s, SHARE), pair(s, RIM)
        for a in (1, 0):
            r = 2 * s + a
            spare = jnp.where(
                half,
                jnp.broadcast_to(p[0][a][:, 64:65], shape),
                jnp.broadcast_to(p[0][a][:, 0:1], shape),
            )
            at = slice(r % 8, r % 8 + 1)
            primal[CAPS + r // 8, at] = spare[0:1]
            const[LIMITS + r // 8, at] = spare[1:2]
            primal[SHARES + r] = u[a]
            here = [p[k][a] * const[k] for k in range(ARCS)]
            carry = put_dual(dual, inward, tail, r, here, b[a], h[a] * const[HALO], carry)


def summed_row(got):
    total = got[0:8]
    for n in range(1, DEVICES // 8):
        total = total + got[8 * n : 8 * n + 8]
    return jnp.sum(total, axis=0, keepdims=True)


def lane_value(row, lane):
    return jnp.sum(jnp.where(lanes((1, 128)) == lane, row, 0.0), axis=1, keepdims=True)


def whole(v):
    return jnp.sum(jnp.sum(v, axis=0, keepdims=True), axis=1, keepdims=True)


def caps_after(row, primal, const):
    shape = (ROWS, 128)
    spread = jnp.where((lanes(shape) & 63) == subs(shape), jnp.broadcast_to(row, shape), 0.0)
    totals = half_sums(spread)
    tons_all = lane_value(row, LANE_TONS)
    over = (totals - BLOCKS * table(const, LIMITS)) / tons_all
    return jnp.maximum(table(primal, CAPS) + primal[WEIGHT, 0:1] * over, 0.0)


def restart(row, primal, const):
    mean = (table(primal, CAP_SUM) + caps_after(row, primal, const)) / INNER
    move_cap = whole((mean - table(primal, CAP_FIRST)) ** 2) * (1.0 / 64.0)
    primal_move = lane_value(row, LANE_PRIMAL)
    dual_move = lane_value(row, LANE_DUAL) + move_cap
    weight = primal[WEIGHT, 0:1]
    return mean, jnp.sqrt(weight * jnp.sqrt((dual_move + EPS) / (primal_move + EPS)))


def primal_step(inner, caps, weight, primal, tail, const, new, x_one, x_two, y_one, y_two, row, rates):
    shape = (8, 128)
    tons = const[TONS]
    value = const[VALUE]
    lean = tons / ROOT
    periods = period_table()
    rates[0] = jnp.exp(-RATE * periods)
    rates[1] = SLOPE * (NP - periods)
    put_table(new, CAPS, caps)
    put_table(new, CAP_FIRST, caps if inner == 0 else table(primal, CAP_FIRST))
    if inner == 0:
        put_table(new, CAP_SUM, jnp.zeros((ROWS, 128), F32))
    else:
        put_table(new, CAP_SUM, table(primal, CAP_SUM) + caps)
    new[WEIGHT] = jnp.broadcast_to(weight, shape)
    half = later_half(shape)
    odd_x = const[ODD_X] > 0.5
    even_y = const[EVEN_Y] > 0.5
    carry = jnp.zeros(shape, F32)
    moved = jnp.zeros(shape, F32)
    mined = []
    for r in range(ROWS):
        gradient = tail[r] + tons * line(new, CAPS, r) / ROOT
        tau = 1.0 / (weight * (rates[1, r : r + 1] + lean))
        old = primal[SHARES + r]
        now = jnp.maximum(old - tau * (gradient - value * rates[0, r : r + 1]), 0.0)
        if inner == 0:
            new[SHARES + r] = now
            new[SHARE_SUM + r] = now
            new[SHARE_FIRST + r] = old
        elif inner < INNER - 1:
            new[SHARES + r] = now
            new[SHARE_SUM + r] = primal[SHARE_SUM + r] + now
            new[SHARE_FIRST + r] = primal[SHARE_FIRST + r]
        else:
            mean = (primal[SHARE_SUM + r] + now) / INNER
            new[SHARES + r] = mean
            moved = moved + (mean - primal[SHARE_FIRST + r]) ** 2
        ahead = 2.0 * now - old
        pair = ahead + swap(ahead)
        cumulative = carry + jnp.where(half, pair, ahead)
        carry = carry + pair
        new[HEAD + r] = cumulative
        at = slice(r % 8, r % 8 + 1)
        for x in range(2):
            tile = x * TABLE + r // 8
            new[FIRST + tile, at] = cumulative[4 * x : 4 * x + 1]
            new[LAST + tile, at] = cumulative[4 * x + 3 : 4 * x + 4]
        if r % 2 == 0:
            even = cumulative
        else:
            lows, highs = mix(even, cumulative)
            x_one[r // 2] = jnp.where(odd_x, lows, highs)
            x_two[r // 2] = jnp.where(odd_x, highs, lows)
        mined.append(tons * ahead)
    for n in range(2 * TABLE):
        y_one[n] = jnp.where(even_y, new[FIRST + n], new[LAST + n])
        y_two[n] = jnp.where(even_y, new[LAST + n], new[FIRST + n])
    mined.append(tons)
    sums = half_sums(jnp.concatenate(mined, axis=0))
    lane = lanes(shape)
    total = jnp.where(lane == LANE_TONS, sums[8 * ROWS :], 0.0)
    for r in range(ROWS):
        total = total + jnp.where((lane & 63) == r, sums[8 * r : 8 * r + 8], 0.0)
    total = jnp.sum(total, axis=0, keepdims=True)
    if inner == INNER - 1:
        total = total + jnp.where(lanes((1, 128)) == LANE_PRIMAL, whole(moved), 0.0)
    row[...] = jnp.broadcast_to(total, row.shape)


def primal_first_kernel(primal, tail, const, *rest):
    primal_step(0, table(primal, CAPS), primal[WEIGHT, 0:1], primal, tail, const, *rest)


def primal_kernel(inner, got, primal, tail, const, *rest):
    caps = caps_after(summed_row(got), primal, const)
    primal_step(inner, caps, primal[WEIGHT, 0:1], primal, tail, const, *rest)


def primal_restart_kernel(got, primal, tail, const, *rest):
    mean, weight = restart(summed_row(got), primal, const)
    primal_step(0, mean, weight, primal, tail, const, *rest)


def finish_kernel(got, primal, const, caps_new, weight_new):
    mean, weight = restart(jnp.sum(got[...], axis=0, keepdims=True), primal, const)
    own = lax.axis_index("period")
    shape = mean.shape
    for t in range(4):
        here = (subs(shape) == 2 * own + t // 2) & (lanes(shape) == 64 * (t % 2))
        caps_new[t] = jnp.sum(jnp.where(here, mean, 0.0))
    weight_new[0] = jnp.max(weight)


def dual_tables(primal, const, y_one, y_two, inward, steps, ahead):
    even_y = const[EVEN_Y, 0:1] > 0.5
    periods = period_table()
    weight = primal[WEIGHT, 0:1]
    steps[0] = weight / (2.0 * (periods + 1.0))
    steps[1] = weight / (periods + 1.0)
    new = []
    for n, inside in ((0, FIRST), (1, LAST)):
        new.append([])
        for x in range(2):
            at = 2 * n + x
            one, two = table(y_one, x * TABLE), table(y_two, x * TABLE)
            there = jnp.where(even_y, two, one) if n else jnp.where(even_y, one, two)
            ahead[n, x] = down(there)
            here = table(primal, inside + x * TABLE)
            price = table(inward, edge_at(n, x)) + steps[0] * (there - down(here))
            new[n].append(jnp.maximum(price, 0.0) * const[EDGES, at : at + 1])
    return new


def dual_pair(s, primal, const, x_one, x_two, dual, inward, steps, ahead):
    odd = const[ODD_X] > 0.5
    lower = jnp.where(odd, x_one[s], x_two[s])
    upper = jnp.where(odd, x_two[s], x_one[s])
    outside = mix(lower, upper)
    return [
        dual_row(2 * s + a, outside[a], primal, const, dual, inward, steps, ahead)
        for a in range(2)
    ]


def dual_row(r, outside, primal, const, dual, inward, steps, ahead_rows):
    one = slice(r, r + 1)
    step = steps[0, one]
    here = primal[HEAD + r]
    under = down(here)
    away = down(outside)
    other = turn(under)
    sub = subs((8, 128))
    after = pltpu.roll(under, 7, 0)
    before = pltpu.roll(under, 1, 0)
    ahead = [
        under,
        jnp.where(low(), other, away),
        jnp.where(low(), away, other),
        jnp.where(
            sub == 3, ahead_rows[1, 0, one], jnp.where(sub == 7, ahead_rows[1, 1, one], after)
        ),
        jnp.where(
            sub == 0, ahead_rows[0, 0, one], jnp.where(sub == 4, ahead_rows[0, 1, one], before)
        ),
    ]
    p = [
        jnp.maximum(dual[PRICES + k * ROWS + r] + step * (here - ahead[k]), 0.0) * const[k]
        for k in range(ARCS)
    ]
    b = jnp.maximum(dual[BOUNDS + r] + steps[1, one] * (here - 1.0), 0.0)
    h = jnp.maximum(inward[HALOS + r] + step * (outside - under), 0.0) * const[HALO]
    return p, b, h


def dual_kernel(
    primal, const, x_one, x_two, y_one, y_two, dual, inward, new, inward_new, tail, steps, ahead
):
    edges = dual_tables(primal, const, y_one, y_two, inward, steps, ahead)
    for n in range(2):
        for x in range(2):
            put_table(inward_new, edge_at(n, x), edges[n][x])
    carry = jnp.zeros((8, 128), F32)
    for s in reversed(range(ROWS // 2)):
        both = dual_pair(s, primal, const, x_one, x_two, dual, inward, steps, ahead)
        for a in (1, 0):
            carry = put_dual(new, inward_new, tail, 2 * s + a, *both[a], carry)


def start_kernel(
    got, weight, dual, inward, const, new, x_one, x_two, y_one, y_two, row, primal, tail, rates
):
    unpack_kernel(got, weight, primal, dual, inward, tail, const)
    primal_first_kernel(primal, tail, const, new, x_one, x_two, y_one, y_two, row, rates)


def step_kernel(
    inner, got, primal, const, x_one, x_two, y_one, y_two, dual, inward, dual_new, inward_new, *rest
):
    *outs, rates, steps, ahead, tail = rest
    dual_kernel(
        primal, const, x_one, x_two, y_one, y_two, dual, inward, dual_new, inward_new, tail, steps,
        ahead,
    )
    primal_kernel(inner, got, primal, tail, const, *outs, rates)


def mean_of(one, two, three):
    return (one + two + three) / INNER


def mean_row(r, dual0, dual1, dual, p, b, moved):
    mean = []
    for k in range(ARCS):
        at = PRICES + k * ROWS + r
        mean.append(mean_of(dual1[at], dual[at], p[k]))
        moved = moved + (mean[k] - dual0[at]) ** 2
    b = mean_of(dual1[BOUNDS + r], dual[BOUNDS + r], b)
    return mean, b, moved + (b - dual0[BOUNDS + r]) ** 2


def with_moves(row, moved):
    return row[0:1] + jnp.where(lanes((1, 128)) == LANE_DUAL, whole(moved), 0.0)


def dual_restart_kernel(
    primal, const, x_one, x_two, y_one, y_two, dual, inward, row, inward1, dual0, dual1,
    new, inward_new, tail, row_new, steps, ahead,
):
    edges = dual_tables(primal, const, y_one, y_two, inward, steps, ahead)
    for n in range(2):
        for x in range(2):
            at = edge_at(n, x)
            mean = mean_of(table(inward1, at), table(inward, at), edges[n][x])
            put_table(inward_new, at, mean)
    carry = jnp.zeros((8, 128), F32)
    moved = jnp.zeros((8, 128), F32)
    for s in reversed(range(ROWS // 2)):
        both = dual_pair(s, primal, const, x_one, x_two, dual, inward, steps, ahead)
        for a in (1, 0):
            r = 2 * s + a
            p, b, h = both[a]
            p, b, moved = mean_row(r, dual0, dual1, dual, p, b, moved)
            h = mean_of(inward1[HALOS + r], inward[HALOS + r], h)
            carry = put_dual(new, inward_new, tail, r, p, b, h, carry)
    row_new[...] = jnp.broadcast_to(with_moves(row, moved), row_new.shape)


def spread_row(row):
    shape = (ROWS + 8, 128)
    spread = jnp.where((lanes(shape) & 63) == subs(shape), jnp.broadcast_to(row, shape), 0.0)
    return half_sums(spread)


def dual_final_kernel(
    primal, const, x_one, x_two, y_one, y_two, dual, inward, row, dual0, dual1,
    send, steps, ahead,
):
    dual_tables(primal, const, y_one, y_two, inward, steps, ahead)
    moved = jnp.zeros((8, 128), F32)
    for s in range(ROWS // 2):
        both = dual_pair(s, primal, const, x_one, x_two, dual, inward, steps, ahead)
        means = []
        for a in range(2):
            r = 2 * s + a
            p, b, _ = both[a]
            p, b, moved = mean_row(r, dual0, dual1, dual, p, b, moved)
            means.append(p + [b, primal[SHARES + r]])
        for field in range(ARCS, BACK):
            send[s, field], send[16 + s, field] = mix(means[0][field], means[1][field])
        for k in range(ARCS):
            send[s, k], send[16 + s, k] = mix(means[0][k], means[1][k])
    sums = spread_row(with_moves(row, moved))
    top = (lanes((8, 128)) & 63) == 0
    for k in range(ARCS):
        tile = sums[8 * k : 8 * k + 8]
        for i in range(TILES):
            send[i, k] = jnp.where(top, tile, send[i, k])


def plane_sum_kernel(got, out):
    top = (lanes((8, 128)) & 63) == 0
    tiles = []
    for k in range(ARCS):
        total = got[0, k]
        for i in range(1, TILES):
            total = total + got[i, k]
        tiles.append(jnp.where(top, total, 0.0))
    sums = half_sums(jnp.concatenate(tiles, axis=0))
    shape = sums.shape
    row = jnp.sum(jnp.where((lanes(shape) & 63) == subs(shape), sums, 0.0), axis=0, keepdims=True)
    out[...] = jnp.broadcast_to(row, out.shape)


def turn_back_kernel(got, share, prec, bound):
    def take(field, target):
        rows = [
            mix(got[member(2 * m), field], got[member(2 * m + 1), field]) for m in range(TILES // 2)
        ]
        for a in range(2):
            turned = jnp.concatenate([pair[a] for pair in rows], axis=0).T
            target(2 * a, turned[0:64])
            target(2 * a + 1, turned[64:128])

    for k in range(ARCS):

        def store(t, v, k=k):
            prec[k, t] = jnp.where(subs(v.shape) == 0, 0.0, v)

        take(k, store)

    def store_bound(t, v):
        bound[t] = v

    def store_share(t, v):
        share[t] = v

    take(BOUND, store_bound)
    take(SHARE, store_share)


def f32(*shape):
    return jax.ShapeDtypeStruct(shape, F32)


VMEM = pl.BlockSpec(memory_space=pltpu.VMEM)
SMEM = pl.BlockSpec(memory_space=pltpu.SMEM)
ANY = pl.BlockSpec(memory_space=pl.ANY)


def call(kernel, outs, scratch=(), far=0, out_spaces=None, aliases=None, vmem=12):
    def run(*args):
        return pl.pallas_call(
            kernel,
            out_shape=[f32(*shape) for shape in outs],
            in_specs=[VMEM] * (len(args) - far) + [ANY] * far,
            out_specs=out_spaces or [VMEM] * len(outs),
            scratch_shapes=[
                pltpu.VMEM(shape, F32) if isinstance(shape, tuple) else shape for shape in scratch
            ],
            input_output_aliases=aliases or {},
            compiler_params=pltpu.CompilerParams(vmem_limit_bytes=vmem * 1024 * 1024),
            cost_estimate=pl.CostEstimate(
                flops=10**6, bytes_accessed=4 * 10**6, transcendentals=0
            ),
        )(*args)

    return run


def semaphores(n):
    return pltpu.SemaphoreType.DMA((n,))


STEP_OUTS = [
    (PRIMAL, 8, 128), (ROWS // 2, 8, 128), (ROWS // 2, 8, 128), (2 * TABLE, 8, 128),
    (2 * TABLE, 8, 128), (DEVICES, 128),
]
STEP_SCRATCH = [(2, ROWS, 128)]
DUAL_ARRAY = (DUAL, 8, 128)
INWARD_ARRAY = (INWARD, 8, 128)
TAIL_ARRAY = (ROWS, 8, 128)
DUAL_OUTS = [DUAL_ARRAY, INWARD_ARRAY, TAIL_ARRAY]
DUAL_SCRATCH = [(2, ROWS, 128), (2, 2, ROWS, 128)]
ALL_VMEM = 62
EVERY = ("strip", "period")


def share_row(row):
    return lax.all_to_all(row, EVERY, 0, 0, tiled=True)


def share_planes(row):
    planes = DEVICES // PLANE
    groups = [[PLANE * z + i for z in range(planes)] for i in range(PLANE)]
    return lax.all_to_all(row, EVERY, 0, 0, axis_index_groups=groups, tiled=True)


def exchange(slots):
    groups = [[PLANE * z + i for i in range(PLANE)] for z in range(DEVICES // PLANE)]
    return lax.all_to_all(slots, EVERY, 0, 0, axis_index_groups=groups)


def swap_x(value, odd):
    planes = DEVICES // PLANE
    pairs = []
    for z in range(planes):
        other = z + 1 if z % 2 == odd else z - 1
        if 0 <= other < planes:
            pairs += [(PLANE * z + i, PLANE * other + i) for i in range(PLANE)]
    return lax.ppermute(value, EVERY, pairs)


def swap_y(value, odd):
    pairs = []
    for j in range(TILES):
        other = j + 1 if j % 2 == odd else j - 1
        if 0 <= other < TILES:
            pairs += [
                (PLANE * z + member(j), PLANE * z + member(other)) for z in range(DEVICES // PLANE)
            ]
    return lax.ppermute(value, EVERY, pairs)


def halo(x_one, x_two, y_one, y_two):
    return swap_x(x_one, 0), swap_x(x_two, 1), swap_y(y_one, 1), swap_y(y_two, 0)


def per_device(
    u_start,
    dual_prec,
    dual_bound,
    dual_cap,
    capacity,
    block_value,
    ton_class,
    density,
    slope_code,
    omega_start,
):
    plane = (NZ, NY)
    slots = (TILES, SLOTS, 8, 128)
    prec = dual_prec[:, 0]
    ints = pltpu.VMEM((1, NY), jnp.int32)
    (rim,) = call(rim_kernel, [(4,) + plane], [ints, semaphores(2)], far=2, vmem=ALL_VMEM)(
        slope_code, prec
    )
    swaps = [(i, i + 1 if i % 2 else i - 1) for i in range(1, NX - 1)]
    rim = lax.ppermute(rim, "strip", swaps)
    (send,) = call(
        pack_kernel,
        [slots],
        [
            pltpu.SMEM((4,), F32), pltpu.SMEM((4,), F32), pltpu.SMEM((8,), F32), ints,
            pltpu.VMEM(plane, jnp.int32), plane, (4,) + plane, (ARCS, 4) + plane, (4,) + plane,
            semaphores(9),
        ],
        far=9,
        vmem=ALL_VMEM,
    )(
        dual_cap, capacity, density, slope_code, ton_class[0], block_value[0], u_start[0], prec,
        dual_bound[0],
    )
    (send,) = call(
        put_rim_kernel,
        [slots],
        [(4,) + plane, (TILES, 8, 128), semaphores(1)],
        far=2,
        out_spaces=[ANY],
        aliases={1: 0},
        vmem=ALL_VMEM,
    )(rim, send)
    got = exchange(send)
    dual, inward, const, primal, *sides, row = call(
        start_kernel,
        [DUAL_ARRAY, INWARD_ARRAY, (CONSTANTS, 8, 128)] + STEP_OUTS,
        [(PRIMAL, 8, 128), TAIL_ARRAY] + STEP_SCRATCH,
    )(got, jnp.reshape(omega_start, (1, 1)))
    for outer in range(OUTER):
        if outer > 0:
            primal, *sides, row = call(
                primal_restart_kernel, STEP_OUTS, STEP_SCRATCH, aliases={1: 0}
            )(row_sums, primal, tail, const)
        duals, inwards = [dual], [inward]
        for inner in range(1, INNER):
            row_sums = share_row(row)
            dual, inward, primal, *sides, row = call(
                functools.partial(step_kernel, inner),
                [DUAL_ARRAY, INWARD_ARRAY] + STEP_OUTS,
                STEP_SCRATCH + DUAL_SCRATCH + [TAIL_ARRAY],
                aliases={1: 2, 3: 3, 4: 4, 5: 5, 6: 6} | ({8: 1} if inner == 1 else {}),
            )(row_sums, primal, const, *halo(*sides), dual, inward)
            duals.append(dual)
            inwards.append(inward)
        sides = halo(*sides)
        if outer < OUTER - 1:
            dual, inward, tail, row = call(
                dual_restart_kernel,
                DUAL_OUTS + [(DEVICES, 128)],
                DUAL_SCRATCH,
                aliases={9: 1},
            )(primal, const, *sides, dual, inward, row, inwards[1], duals[0], duals[1])
            row_sums = share_row(row)
        else:
            (send,) = call(dual_final_kernel, [(TILES, BACK, 8, 128)], DUAL_SCRATCH)(
                primal, const, *sides, dual, inward, row, duals[0], duals[1]
            )
            got = exchange(send)
            (row,) = call(plane_sum_kernel, [(8, 128)])(got)
            row_sums = share_planes(row)
    mined, arcs, bounds = call(
        turn_back_kernel, [(4, NZ, NY), (ARCS, 4, NZ, NY), (4, NZ, NY)]
    )(got)
    caps, weight = call(finish_kernel, [(4,), (1,)], out_spaces=[SMEM, SMEM])(
        row_sums, primal, const
    )
    return (
        mined[None],
        arcs[:, None],
        bounds[None],
        caps,
        weight,
    )


def solution(mesh):
    in_specs = (
        P("strip", "period", None, None),
        P(None, "strip", "period", None, None),
        P("strip", "period", None, None),
        P("period"),
        P("period"),
        P("strip", None, None),
        P("strip", None, None),
        P(),
        P("strip", None),
        P(),
    )
    out_specs = (
        P("strip", "period", None, None),
        P(None, "strip", "period", None, None),
        P("strip", "period", None, None),
        P("period"),
        P(),
    )
    return jax.shard_map(
        per_device, mesh=mesh, in_specs=in_specs, out_specs=out_specs, check_vma=False
    )
```
